128 devices in a mesh: section: 16 (over y, x_hi, core), seq: 8 (over z, x_lo).
Axes of the slice: x: 4 (x_hi: 2, x_lo: 2; x = x_hi * 2 + x_lo), y: 4, z: 4, core: 2. Of those that a mesh axis runs over, the one named last changes fastest.
Arguments:
- section_input: bfloat16 [16, 1024, 2560], P('section', 'seq'), may hold values from -6 to 6
- state_in: float32 [16, 20, 128, 128], P('section'), may hold values from -24 to 24
- decay_table: float32 [16], replicated, may hold values from 0.96 to 1
- head_rate: int32 [16, 20], P('section'), may hold values from 0 to 15
- gates: float32 [16, 1024, 20], P('section', 'seq'), may hold values from 0.5 to 1
- query_gain: float32 [16, 2560], P('section'), may hold values from 0.25 to 1.75
- key_gain: float32 [16, 2560], P('section'), may hold values from 0.25 to 1.75
- out_gain: float32 [16, 2560], P('section'), may hold values from 0.25 to 1.75
- global_gain: float32 [2, 2560], replicated, may hold values from 0.25 to 1.75
- cache_kv: bfloat16 [8192, 5120], P(('section', 'seq')), may hold values from -480 to 480
- cache_pos: int32 [8192], P(('section', 'seq')), may hold values from 0 to 8191, each once
- span_start: int32 [16], P('section'), may hold values from 0 to 7168
Outputs:
- section_output: bfloat16 [16, 1024, 2560], P('section', 'seq')
- state_out: float32 [16, 20, 128, 128], P('section', None, 'seq')
- global_new: bfloat16 [8, 16, 8, 5120], P('seq', 'section')
The draws below stay inside these ranges and needn't reach their ends.
All inputs are finite; a program needn't handle non-finite values.
Results may differ from the reference program's by a relative error of at most 0.014.
Values may be sent and summed in bfloat16 or wider, within the bound.
A program may use at most 384 MiB of HBM per device.

```python
import math
import jax
import jax.numpy as jnp
from jax import lax

HEADS = 20
HDIM = 128
BLK = 128
NTAB = 16
CACHE_DEV = 64
HD = 2560
STRETCH_WORDS = 1024
CACHE = 8192
NEW_DEV = 8
N_SECTION = 16
N_SEQ = 8


def draw_decay_table(key, part):
    key = jax.random.fold_in(key, 11)
    lowest = math.log(0.1 / STRETCH_WORDS)
    topmost = math.log(1.0 / 30.0)
    rate_values = jnp.exp(jax.random.uniform(key, (NTAB,), jnp.float32, lowest, topmost))
    return jnp.exp(-rate_values)


def draw_gates(key, part):
    key = jax.random.fold_in(key, 12)
    constant_seed_handle, discard_seed_handle, surge_seed_handle = jax.random.split(key, 3)
    extent_sequence = (N_SECTION, STRETCH_WORDS, HEADS)
    constant_sample_ids = jax.random.uniform(constant_seed_handle, extent_sequence, jnp.float32, 0.9995, 1.0)
    discarded_sample_ids = jax.random.uniform(discard_seed_handle, extent_sequence, jnp.float32, 0.5, 0.8)
    surge_sample_ids = jax.random.uniform(surge_seed_handle, extent_sequence, jnp.float32) < 3.0 / STRETCH_WORDS
    return jnp.where(surge_sample_ids, discarded_sample_ids, constant_sample_ids)


def draw_cache_kv(key, part):
    key = jax.random.fold_in(key, 13)
    key_base = jax.random.fold_in(key, 0)
    values = jnp.clip(jax.random.normal(key_base, (CACHE, 2 * HD), jnp.float32), -6.0, 6.0)
    return values.astype(jnp.bfloat16)


def touch_ends(values, rng, low, high):
    extent = values.shape
    spot = [jax.random.randint(jax.random.fold_in(rng, axis), (), 0, extent[axis]) for axis in range(len(extent))]
    values = values.at[tuple(spot)].set(low)
    longest = extent.index(max(extent))
    spot[longest] = (spot[longest] + 1) % extent[longest]
    return values.at[tuple(spot)].set(high)


def block_scale(rng, extent, cuts, least, largest):
    def one(axis_at, shards_of):
        draws = jax.random.uniform(jax.random.fold_in(jax.random.fold_in(rng, 6), axis_at), (shards_of,), jnp.float32, least / len(cuts), largest / len(cuts))
        return jnp.repeat(jnp.exp(draws), extent[axis_at] // shards_of).reshape((-1,) + (1,) * (len(extent) - axis_at - 1))

    level = one(*cuts[0])
    for cut in cuts[1:]:
        level = level * one(*cut)
    return level


def scatter_about(rng, shape, scale, limit, cuts=(), held_as=jnp.bfloat16):
    entries = jax.random.normal(rng, shape, jnp.float32) * scale
    if len(cuts) > 0:
        entries = block_scale(rng, shape, cuts, -0.22, 0.18) * entries
    return jnp.clip(entries, min=-limit, max=limit).astype(held_as)


def setup_inputs(seed: int = 0) -> dict:
    key_of = jax.random.split(jax.random.key(seed), 13)
    return {
        "section_input": scatter_about(key_of[0], (N_SECTION, STRETCH_WORDS, HD), 1.0, 6.0, ((0, 16), (1, 8))),
        "state_in": scatter_about(key_of[1], (N_SECTION, HEADS, HDIM, HDIM), 4.0, 24.0, ((0, 16),), jnp.float32),
        "decay_table": draw_decay_table(jax.random.fold_in(key_of[12], 71), 0),
        "head_rate": touch_ends(jax.random.randint(key_of[3], (N_SECTION, HEADS), 0, NTAB), jax.random.fold_in(key_of[3], 1), 0, NTAB - 1).astype(jnp.int32),
        "gates": draw_gates(jax.random.fold_in(key_of[12], 71), 0),
        "query_gain": jnp.clip(1.0 + 0.15 * jax.random.normal(key_of[5], (N_SECTION, HD), jnp.float32), 0.25, 1.75),
        "key_gain": jnp.clip(1.0 + 0.15 * jax.random.normal(key_of[6], (N_SECTION, HD), jnp.float32), 0.25, 1.75),
        "out_gain": jnp.clip(1.0 + 0.15 * jax.random.normal(key_of[7], (N_SECTION, HD), jnp.float32), 0.25, 1.75),
        "global_gain": jnp.clip(1.0 + 0.15 * jax.random.normal(key_of[8], (2, HD), jnp.float32), 0.25, 1.75),
        "cache_kv": draw_cache_kv(jax.random.fold_in(key_of[12], 71), 0),
        "cache_pos": jax.random.permutation(key_of[10], CACHE).astype(jnp.int32),
        "span_start": touch_ends(jax.random.randint(key_of[11], (N_SECTION,), 0, CACHE - STRETCH_WORDS + 1), jax.random.fold_in(key_of[11], 1), 0, CACHE - STRETCH_WORDS).astype(jnp.int32),
    }


EPSILON = 1e-06
MASKED_SCORE = -1e+30
PRECISE = lax.Precision.HIGHEST

def rms_rows(values):
    return values * lax.rsqrt(lax.optimization_barrier(jnp.mean(values * values, axis=-1, keepdims=True)) + EPSILON)

def block_terms(queries, key_rows, values, logdecay):
    cumulative = jnp.cumsum(logdecay, axis=0)
    ending = cumulative[-1]
    scores = jnp.einsum('thd,shd->hts', queries.astype(jnp.float32), key_rows.astype(jnp.float32))
    causal = (jnp.arange(BLK)[:, None] >= jnp.arange(BLK)[None, :])[None]
    differences = cumulative.T[:, :, None] - cumulative.T[:, None, :]
    weights = jnp.where(causal, scores * jnp.exp(jnp.where(causal, differences, 0.0)), 0.0).astype(jnp.bfloat16)
    weights = lax.optimization_barrier(weights)
    inside = jnp.einsum('hts,shd->thd', weights.astype(jnp.float32), values.astype(jnp.float32))
    fading = jnp.exp(ending[None, :] - cumulative)
    update = jnp.einsum('thd,the->hde', key_rows.astype(jnp.float32) * fading[:, :, None], values.astype(jnp.float32), precision=PRECISE)
    return (inside, jnp.exp(cumulative), jnp.exp(ending), update)

def retain_section(inputs, carried, table_logs, rate_row, gate_rows, query_gain_row, key_gain_row):
    blocks = STRETCH_WORDS // BLK
    normed = rms_rows(inputs.astype(jnp.float32))
    queries = (normed * query_gain_row).astype(jnp.bfloat16)
    key_rows = (normed * key_gain_row).astype(jnp.bfloat16)
    picked = lax.optimization_barrier(jnp.sum(jnp.where(rate_row[:, None] == jnp.arange(NTAB, dtype=jnp.int32)[None, :], table_logs[None, :], 0.0), axis=1))
    logdecay = picked[None, :] + jnp.log(gate_rows)
    shaped = (queries.reshape(blocks, BLK, HEADS, HDIM), key_rows.reshape(blocks, BLK, HEADS, HDIM), inputs.reshape(blocks, BLK, HEADS, HDIM), logdecay.reshape(blocks, BLK, HEADS))

    def advance(state_now, block):
        block_q, block_k, block_v, block_d = block
        inside, growth, fading, update = block_terms(block_q, block_k, block_v, block_d)
        carried_in = jnp.einsum('thd,hde->the', block_q.astype(jnp.float32) * growth[:, :, None], state_now, precision=PRECISE)
        return (fading[:, None, None] * state_now + update, inside + carried_in)
    final_state, retained = lax.scan(advance, carried, shaped)
    retained = rms_rows(retained.reshape(STRETCH_WORDS, HEADS, HDIM))
    return (queries, retained.reshape(STRETCH_WORDS, HD), final_state)

def attend_section(queries, cache_kv, cache_pos, start):
    key_rows = cache_kv[:, :HD].reshape(N_SECTION, N_SEQ, CACHE_DEV, HEADS, HDIM)
    value_rows = cache_kv[:, HD:].reshape(N_SECTION, N_SEQ, CACHE_DEV, HEADS, HDIM)
    places = cache_pos.reshape(N_SECTION, N_SEQ, CACHE_DEV)
    visible = places[None] <= (start + jnp.arange(STRETCH_WORDS, dtype=jnp.int32))[:, None, None, None]

    def one_head(head_at):
        query_head = lax.dynamic_slice_in_dim(queries, head_at * HDIM, HDIM, 1).astype(jnp.float32)
        key_head = lax.dynamic_index_in_dim(key_rows, head_at, 3, keepdims=False).astype(jnp.float32)
        value_head = lax.dynamic_index_in_dim(value_rows, head_at, 3, keepdims=False).astype(jnp.float32)
        scores = jnp.einsum('qd,agcd->qagc', query_head, key_head) * HDIM ** (-0.5)
        scores = jnp.where(visible, scores, MASKED_SCORE)
        highest = lax.optimization_barrier(jnp.max(scores, axis=(1, 3)))
        likely = jnp.exp(scores - highest[:, None, :, None])
        totals = lax.optimization_barrier(jnp.sum(likely, axis=(1, 3)))
        rounded = lax.optimization_barrier(likely.astype(jnp.bfloat16))
        pieces = jnp.einsum('qagc,agcd->qgd', rounded.astype(jnp.float32), value_head)
        overall = lax.optimization_barrier(jnp.max(highest, axis=1))
        factor = jnp.exp(highest - overall[:, None])
        return lax.optimization_barrier(jnp.sum(pieces * factor[:, :, None], axis=1)) / lax.optimization_barrier(jnp.sum(totals * factor, axis=1))[:, None]
    attended = lax.map(one_head, jnp.arange(HEADS, dtype=jnp.int32))
    return jnp.transpose(attended, (1, 0, 2)).reshape(STRETCH_WORDS, HD)

def reference(section_input, state_in, decay_table, head_rate, gates, query_gain, key_gain, out_gain, global_gain, cache_kv, cache_pos, span_start):
    table_logs = jnp.log(decay_table)
    half_sections = N_SECTION // 2
    results = []
    finals = []
    for section_at in range(N_SECTION):
        inputs = section_input[section_at]
        if section_at < half_sections:
            queries, mixed, final_state = retain_section(inputs, state_in[section_at], table_logs, head_rate[section_at], gates[section_at], query_gain[section_at], key_gain[section_at])
            finals.append(final_state)
        else:
            normed = rms_rows(inputs.astype(jnp.float32))
            queries = (normed * query_gain[section_at]).astype(jnp.bfloat16)
            mixed = attend_section(queries, cache_kv, cache_pos, span_start[section_at])
            finals.append(state_in[section_at])
        results.append((inputs.astype(jnp.float32) + mixed * out_gain[section_at]).astype(jnp.bfloat16))
    section_output = jnp.stack([results[(section_at - 1) % N_SECTION] for section_at in range(N_SECTION)])
    state_out = jnp.stack(finals)
    nfresh = rms_rows(results[half_sections - 1].astype(jnp.float32))
    global_new = jnp.concatenate([nfresh * global_gain[0], nfresh * global_gain[1]], axis=1).astype(jnp.bfloat16)
    return (section_output, state_out, global_new.reshape(N_SEQ, N_SECTION, NEW_DEV, 2 * HD))
```

```python
import functools

import jax
import jax.numpy as jnp
from jax import lax
from jax.experimental import pallas as pl
from jax.experimental.pallas import tpu as pltpu
from jax.sharding import PartitionSpec as P

MESH = pl.DeviceIdType.MESH
EPSILON = 1e-06
MASKED_SCORE = -1e30
LOG2E = 1.4426950408889634
HD = 2560
HEADS = 20
HDIM = 128
GROUP = 640
HALF = 64
KEYS = 2048


def place_of():
    section = lax.axis_index("section")
    seq = lax.axis_index("seq")
    return section // 4, ((section // 2) % 2) * 2 + seq % 2, seq // 2, section % 2


def device_at(y, x, z, core):
    return (y * 4 + (x // 2) * 2 + core, z * 2 + x % 2)


def shifted(value, by):
    return lax.rem(value + by + 4, 4)


def greet(peers):
    barrier = pltpu.get_barrier_semaphore()
    for peer in peers:
        pl.semaphore_signal(barrier, inc=1, device_id=peer, device_id_type=MESH)
    pl.semaphore_wait(barrier, len(peers))


def remote(src, dst, send_sem, recv_sem, peer):
    return pltpu.make_async_remote_copy(
        src_ref=src,
        dst_ref=dst,
        send_sem=send_sem,
        recv_sem=recv_sem,
        device_id=peer,
        device_id_type=MESH,
    )


NEAR_Y = [(dy, dx) for dy in (0, 1, 3, 2) for dx in (0, 1, 3, 2)]
NEAR_Z = [(dz, dx) for dz in (0, 1, 3, 2) for dx in (0, 1, 3, 2)]


def exchange_kernel(
    x_ref,
    gain_ref,
    kv_ref,
    meta_ref,
    update_ref,
    fade_ref,
    k_out,
    v_out,
    meta_out,
    q_out,
    at_x,
    at_gain,
    update_out,
    fade_out,
    queries,
    half_send,
    half_recv,
    gain_send,
    gain_recv,
    kv_send,
    kv_recv,
    fwd_send,
    fwd_recv,
    q_send,
    q_recv,
    u_send,
    u_recv,
    local_sem,
):
    y, x, z, core = place_of()
    is_self = y < 2
    sibling = device_at(y, x, z, 1 - core)
    partner = device_at(3 - y, x, z, core)
    peers = [device_at(shifted(y, dy), shifted(x, dx), z, core) for dy, dx in NEAR_Y[1:]]
    peers += [device_at(y, shifted(x, dx), shifted(z, dz), core) for dz, dx in NEAR_Z[4:]]
    peers.append(sibling)
    greet(peers)

    half_copy = remote(x_ref.at[pl.ds(HALF, HALF)], at_x, half_send, half_recv, partner)
    gain_copy = remote(gain_ref, at_gain, gain_send, gain_recv, partner)

    @pl.when(jnp.logical_not(is_self))
    def _():
        half_copy.start()
        gain_copy.start()

    slot = pl.ds(pl.multiple_of((x * 4 + y) * 128 + core * 64, 64), 64)
    meta_slot = (x * 4 + y) * 2 + core

    def kv_pieces(column_place):
        k_cols = pl.ds(pl.multiple_of(column_place * GROUP, 128), GROUP)
        v_cols = pl.ds(pl.multiple_of(HD + column_place * GROUP, 128), GROUP)
        return (
            (meta_ref, meta_out.at[meta_slot]),
            (kv_ref.at[:, k_cols], k_out.at[slot]),
            (kv_ref.at[:, v_cols], v_out.at[slot]),
        )

    kv_copies = []
    for at, (dy, dx) in enumerate(NEAR_Y):
        if at == 0:
            continue
        to_x = shifted(x, dx)
        peer = device_at(shifted(y, dy), to_x, z, core)
        for kind, (src, dst) in enumerate(kv_pieces(to_x)):
            copy = remote(src, dst, kv_send.at[at, kind], kv_recv.at[at, kind], peer)
            copy.start()
            kv_copies.append(copy)
    own_copies = []
    fwd_copies = []
    for kind, (src, dst) in enumerate(kv_pieces(x)):
        copy = pltpu.make_async_copy(src, dst, local_sem.at[kind])
        copy.start()
        own_copies.append(copy)
        copy = remote(src, dst, fwd_send.at[0, kind], fwd_recv.at[0, kind], sibling)
        copy.start()
        fwd_copies.append(copy)

    seq = z * 2 + x % 2
    u_copies = []
    for at in range(8):
        dz, flip = at // 2, at % 2
        to_z, to_x = shifted(z, dz), (x // 2) * 2 + lax.rem(x + flip, 2)
        to_seq = to_z * 2 + to_x % 2
        rows = pl.ds(pl.multiple_of(to_seq * 16, 16), 16)
        pairs = ((update_ref.at[:, rows, :], update_out.at[seq]), (fade_ref, fade_out.at[seq]))
        for kind, (src, dst) in enumerate(pairs):
            if at == 0:
                copy = pltpu.make_async_copy(src, dst, local_sem.at[3 + kind])
            else:
                copy = remote(
                    src, dst, u_send.at[at, kind], u_recv.at[at, kind], device_at(y, to_x, to_z, core)
                )
            u_copies.append(copy)

    @pl.when(is_self)
    def _():
        for copy in u_copies:
            copy.start()
        half_copy.wait_recv()
        gain_copy.wait_recv()

    @pl.when(jnp.logical_not(is_self))
    def _():
        at_x[...] = x_ref[0:HALF, :]
        at_gain[...] = gain_ref[...]

    rows = at_x[...].astype(jnp.float32)
    normed = rows * lax.rsqrt(jnp.mean(rows * rows, axis=1, keepdims=True) + EPSILON)
    queries[...] = (normed * at_gain[0:1, :]).astype(jnp.bfloat16)

    q_copies = []
    q_slot = pl.ds(pl.multiple_of((z * 4 + x) * HALF, HALF), HALF)
    for at, (dz, dx) in enumerate(NEAR_Z):
        to_x, to_z = shifted(x, dx), shifted(z, dz)
        src = queries.at[:, pl.ds(pl.multiple_of(to_x * GROUP, 128), GROUP)]
        dst = q_out.at[q_slot]
        if at == 0:
            copy = pltpu.make_async_copy(src, dst, local_sem.at[5])
        else:
            copy = remote(src, dst, q_send.at[at], q_recv.at[at], device_at(y, to_x, to_z, core))
        copy.start()
        q_copies.append(copy)

    def came_from(at):
        dy, dx = NEAR_Y[at]
        from_x, from_y = shifted(x, -dx), shifted(y, -dy)
        here = pl.ds(pl.multiple_of((from_x * 4 + from_y) * 128 + core * 64, 64), 64)
        meta_here = (from_x * 4 + from_y) * 2 + core
        return (meta_out.at[meta_here], k_out.at[here], v_out.at[here])

    for at in range(1, 16):
        for kind, ref in enumerate(came_from(at)):
            remote(ref, ref, kv_send.at[at, kind], kv_recv.at[at, kind], sibling).wait_recv()
            copy = remote(ref, ref, fwd_send.at[at, kind], fwd_recv.at[at, kind], sibling)
            copy.start()
            fwd_copies.append(copy)

    for copy in own_copies:
        copy.wait()
    for copy in fwd_copies:
        copy.wait()
    for copy in kv_copies:
        copy.wait_send()
    for copy in q_copies:
        copy.wait()

    @pl.when(is_self)
    def _():
        for copy in u_copies:
            copy.wait()

    @pl.when(jnp.logical_not(is_self))
    def _():
        half_copy.wait_send()
        gain_copy.wait_send()


def exchange(x, gains, kv, meta, update, fade):
    any_spec = pl.BlockSpec(memory_space=pl.ANY)
    vmem = pl.BlockSpec(memory_space=pltpu.VMEM)
    dma = pltpu.SemaphoreType.DMA
    return pl.pallas_call(
        exchange_kernel,
        out_shape=(
            jax.ShapeDtypeStruct((KEYS, GROUP), jnp.bfloat16),
            jax.ShapeDtypeStruct((KEYS, GROUP), jnp.bfloat16),
            jax.ShapeDtypeStruct((32, 8, 128), jnp.int32),
            jax.ShapeDtypeStruct((1024, GROUP), jnp.bfloat16),
            jax.ShapeDtypeStruct((HALF, HD), jnp.bfloat16),
            jax.ShapeDtypeStruct((8, HD), jnp.float32),
            jax.ShapeDtypeStruct((8, HEADS, 16, HDIM), jnp.bfloat16),
            jax.ShapeDtypeStruct((8, 8, 128), jnp.float32),
        ),
        in_specs=[vmem, vmem, any_spec, any_spec, any_spec, any_spec],
        out_specs=(any_spec, any_spec, any_spec, any_spec, vmem, vmem, any_spec, any_spec),
        scratch_shapes=[
            pltpu.VMEM((HALF, HD), jnp.bfloat16),
            dma,
            dma,
            dma,
            dma,
            dma((16, 3)),
            dma((16, 3)),
            dma((16, 3)),
            dma((16, 3)),
            dma((16,)),
            dma((16,)),
            dma((8, 2)),
            dma((8, 2)),
            dma((8,)),
        ],
        compiler_params=pltpu.CompilerParams(
            collective_id=0, has_side_effects=True, vmem_limit_bytes=32 * 1024 * 1024
        ),
        name="exchange",
    )(x, gains, kv, meta, update, fade)


QBLOCK = 256


def attend_kernel(starts, pos_ref, q_ref, k_ref, v_ref, o_ref, lse_ref):
    head = pl.program_id(1)
    block = pl.program_id(0)
    index = lax.broadcasted_iota(jnp.int32, (QBLOCK, 1), 0)
    x = index // HALF
    token = block * 256 + (x % 2) * 128 + starts[2] * HALF + index % HALF
    places = jnp.where(x < 2, starts[0], starts[1]) + token
    scores = lax.dot_general(
        q_ref[...], k_ref[...], (((1,), (1,)), ((), ())), preferred_element_type=jnp.float32
    )
    scores = jnp.where(pos_ref[...] <= places, scores, MASKED_SCORE)
    highest = jnp.max(scores, axis=1, keepdims=True)
    factor = HDIM ** (-0.5) * LOG2E
    likely = jnp.exp2((scores - highest) * factor)
    totals = jnp.sum(likely, axis=1, keepdims=True)
    pieces = jnp.dot(likely.astype(jnp.bfloat16), v_ref[...], preferred_element_type=jnp.float32)
    o_ref[...] = (pieces / totals).astype(jnp.bfloat16)
    lse = highest * (HDIM ** (-0.5)) + jnp.log(totals)
    lane = lax.broadcasted_iota(jnp.int32, (QBLOCK, 128), 1)

    @pl.when(head == 0)
    def _():
        lse_ref[...] = jnp.broadcast_to(lse, (QBLOCK, 128))

    @pl.when(head > 0)
    def _():
        lse_ref[...] = jnp.where(lane == head, lse, lse_ref[...])


def attend(starts, pos, q, k, v):
    return pl.pallas_call(
        attend_kernel,
        out_shape=(
            jax.ShapeDtypeStruct((1024, GROUP), jnp.bfloat16),
            jax.ShapeDtypeStruct((1024, 128), jnp.float32),
        ),
        grid=(1024 // QBLOCK, 5),
        in_specs=[
            pl.BlockSpec(memory_space=pltpu.SMEM),
            pl.BlockSpec((1, KEYS), lambda i, h: (0, 0)),
            pl.BlockSpec((QBLOCK, HDIM), lambda i, h: (i, h)),
            pl.BlockSpec((KEYS, HDIM), lambda i, h: (0, h)),
            pl.BlockSpec((KEYS, HDIM), lambda i, h: (0, h)),
        ],
        out_specs=(
            pl.BlockSpec((QBLOCK, HDIM), lambda i, h: (i, h)),
            pl.BlockSpec((QBLOCK, 128), lambda i, h: (i, 0)),
        ),
        compiler_params=pltpu.CompilerParams(vmem_limit_bytes=32 * 1024 * 1024),
        cost_estimate=pl.CostEstimate(
            flops=4 * 1024 * KEYS * GROUP, bytes_accessed=10_000_000, transcendentals=1024 * KEYS * 5
        ),
        name="attend",
    )(starts, pos, q, k, v)


def returning_kernel(
    o_ref, lse_ref, enter_ref, o_out, lse_out, enter_out, o_send, o_recv, e_send, e_recv, local_sem
):
    y, x, z, core = place_of()
    is_self = y < 2
    greet([device_at(y, shifted(x, dx), shifted(z, dz), core) for dz, dx in NEAR_Z[1:]])
    copies = []
    columns = pl.ds(pl.multiple_of(x * GROUP, 128), GROUP)
    for at, (dz, dx) in enumerate(NEAR_Z):
        to_x, to_z = shifted(x, dx), shifted(z, dz)
        rows = pl.ds(pl.multiple_of((to_z * 4 + to_x) * HALF, HALF), HALF)
        pairs = (
            (lse_ref.at[rows], lse_out.at[z, x]),
            (o_ref.at[rows], o_out.at[z, :, columns]),
        )
        for kind, (src, dst) in enumerate(pairs):
            if at == 0:
                copy = pltpu.make_async_copy(src, dst, local_sem.at[kind])
            else:
                copy = remote(
                    src, dst, o_send.at[at, kind], o_recv.at[at, kind], device_at(y, to_x, to_z, core)
                )
            copy.start()
            copies.append(copy)
    seq = z * 2 + x % 2
    e_copies = []
    for at in range(8):
        dz, flip = at // 2, at % 2
        to_z, to_x = shifted(z, dz), (x // 2) * 2 + lax.rem(x + flip, 2)
        src = enter_ref.at[to_z * 2 + to_x % 2]
        dst = enter_out.at[:, pl.ds(pl.multiple_of(seq * 16, 16), 16), :]
        if at == 0:
            copy = pltpu.make_async_copy(src, dst, local_sem.at[2])
        else:
            copy = remote(src, dst, e_send.at[at], e_recv.at[at], device_at(y, to_x, to_z, core))
        e_copies.append(copy)

    @pl.when(is_self)
    def _():
        for copy in e_copies:
            copy.start()

    for copy in copies:
        copy.wait()

    @pl.when(is_self)
    def _():
        for copy in e_copies:
            copy.wait()


def returning(o, lse, enter):
    any_spec = pl.BlockSpec(memory_space=pl.ANY)
    dma = pltpu.SemaphoreType.DMA
    return pl.pallas_call(
        returning_kernel,
        out_shape=(
            jax.ShapeDtypeStruct((4, HALF, HD), jnp.bfloat16),
            jax.ShapeDtypeStruct((4, 4, HALF, 128), jnp.float32),
            jax.ShapeDtypeStruct((HEADS, HDIM, HDIM), jnp.bfloat16),
        ),
        in_specs=[any_spec] * 3,
        out_specs=(any_spec,) * 3,
        scratch_shapes=[dma((16, 2)), dma((16, 2)), dma((8,)), dma((8,)), dma((3,))],
        compiler_params=pltpu.CompilerParams(collective_id=1, has_side_effects=True),
        name="returning",
    )(o, lse, enter)


def onward_kernel(att_ref, mix_ref, out_ref, fresh_ref, s_send, s_recv, f_send, f_recv, local_sem):
    section = lax.axis_index("section")
    seq = lax.axis_index("seq")
    greet([(lax.rem(section + by, 16), seq) for by in range(1, 16)])
    is_self = section < 8
    after = lax.rem(section + 1, 16)
    whole = remote(mix_ref, out_ref, s_send.at[0], s_recv.at[0], (after, seq))
    first = remote(att_ref, out_ref.at[pl.ds(0, HALF)], s_send.at[1], s_recv.at[1], (after, seq))
    helped = jnp.where(section < 4, section + 12, section + 4)
    target = lax.rem(helped + 1, 16)
    second = remote(att_ref, out_ref.at[pl.ds(HALF, HALF)], s_send.at[2], s_recv.at[2], (target, seq))

    def fresh_rows(to):
        return mix_ref.at[pl.ds(pl.multiple_of((to // 2) * 16, 16), 16)]

    own = pltpu.make_async_copy(fresh_rows(section), fresh_ref, local_sem)

    def fresh_copy(by):
        to = lax.rem(section + by, 16)
        return remote(fresh_rows(to), fresh_ref, f_send.at[by], f_recv, (to, seq))

    is_root = section == 7

    @pl.when(is_self)
    def _():
        whole.start()
        second.start()

    @pl.when(jnp.logical_not(is_self))
    def _():
        first.start()

    @pl.when(is_root)
    def _():
        own.start()
        for by in range(1, 16):
            fresh_copy(by).start()

    from_self = jnp.logical_and(section >= 1, section <= 8)

    @pl.when(from_self)
    def _():
        whole.wait_recv()

    @pl.when(jnp.logical_not(from_self))
    def _():
        first.wait_recv()
        second.wait_recv()

    @pl.when(is_self)
    def _():
        whole.wait_send()
        second.wait_send()

    @pl.when(jnp.logical_not(is_self))
    def _():
        first.wait_send()

    @pl.when(is_root)
    def _():
        own.wait()
        for by in range(1, 16):
            fresh_copy(by).wait_send()

    @pl.when(jnp.logical_not(is_root))
    def _():
        fresh_copy(1).wait_recv()


def onward(att, mix):
    any_spec = pl.BlockSpec(memory_space=pl.ANY)
    dma = pltpu.SemaphoreType.DMA
    return pl.pallas_call(
        onward_kernel,
        out_shape=(
            jax.ShapeDtypeStruct((128, HD), jnp.bfloat16),
            jax.ShapeDtypeStruct((16, HD), jnp.bfloat16),
        ),
        in_specs=[any_spec] * 2,
        out_specs=(any_spec,) * 2,
        scratch_shapes=[dma((3,)), dma((3,)), dma((16,)), dma, dma],
        compiler_params=pltpu.CompilerParams(collective_id=2, has_side_effects=True),
        name="onward",
    )(att, mix)


def rms_rows(values):
    return values * lax.rsqrt(jnp.mean(values * values, axis=-1, keepdims=True) + EPSILON)


def block_terms(queries, key_rows, values, logdecay):
    block_len = queries.shape[0]
    cumulative = jnp.cumsum(logdecay, axis=0)
    ending = cumulative[-1]
    scores = jnp.einsum("thd,shd->hts", queries, key_rows, preferred_element_type=jnp.float32)
    causal = (jnp.arange(block_len)[:, None] >= jnp.arange(block_len)[None, :])[None]
    differences = cumulative.T[:, :, None] - cumulative.T[:, None, :]
    weights = jnp.where(causal, scores * jnp.exp(jnp.where(causal, differences, 0.0)), 0.0).astype(
        jnp.bfloat16
    )
    inside = jnp.einsum("hts,shd->thd", weights, values, preferred_element_type=jnp.float32)
    fading = jnp.exp(ending[None, :] - cumulative)
    update = jnp.einsum(
        "thd,the->hde",
        (key_rows.astype(jnp.float32) * fading[:, :, None]).astype(jnp.bfloat16),
        values,
        preferred_element_type=jnp.float32,
    ).astype(jnp.bfloat16)
    return (inside, jnp.exp(cumulative), jnp.exp(ending), update)


def local(
    section_input,
    state_in,
    decay_table,
    head_rate,
    gates,
    query_gain,
    key_gain,
    out_gain,
    global_gain,
    cache_kv,
    cache_pos,
    span_start,
):
    inputs = section_input[0]
    section_at = lax.axis_index("section")
    seq_at = lax.axis_index("seq")
    is_self = section_at < 8
    y, _, z, core = place_of()

    table_logs = jnp.log(decay_table)
    picked = jnp.sum(
        jnp.where(
            head_rate[0][:, None] == jnp.arange(16, dtype=jnp.int32)[None, :],
            table_logs[None, :],
            0.0,
        ),
        axis=1,
    )

    def local_blocks(unused):
        normed = rms_rows(inputs.astype(jnp.float32))
        queries = (normed * query_gain[0]).astype(jnp.bfloat16)
        key_rows = (normed * key_gain[0]).astype(jnp.bfloat16)
        logdecay = picked[None, :] + jnp.log(gates[0])
        shape = (128, HEADS, HDIM)
        terms = block_terms(
            queries.reshape(shape), key_rows.reshape(shape), inputs.reshape(shape), logdecay
        )
        return (queries.reshape(shape),) + terms

    def skip_blocks(unused):
        return (
            jnp.zeros((128, HEADS, HDIM), jnp.bfloat16),
            jnp.zeros((128, HEADS, HDIM), jnp.float32),
            jnp.zeros((128, HEADS), jnp.float32),
            jnp.zeros((HEADS,), jnp.float32),
            jnp.zeros((HEADS, HDIM, HDIM), jnp.bfloat16),
        )

    shaped_q, inside, growth, fade, update = lax.cond(is_self, local_blocks, skip_blocks, 0)

    gains = jnp.concatenate([query_gain, out_gain, jnp.zeros((6, HD), jnp.float32)], axis=0)
    meta = jnp.zeros((8, 128), jnp.int32)
    meta = meta.at[0, :64].set(cache_pos).at[0, 64].set(span_start[0])
    fade_tile = jnp.zeros((8, 128), jnp.float32).at[0, :HEADS].set(fade)
    k, v, metas, q, at_x, at_gain, updates, fades = exchange(
        inputs, gains, cache_kv, meta, update, fade_tile
    )
    metas = metas[:, 0, :]
    pos = metas[:, :64].reshape(1, KEYS)
    y_from = jnp.where(y < 2, 3 - y, y)
    begins = metas[:, 64].reshape(4, 4, 2)
    begins = lax.dynamic_index_in_dim(begins, y_from, 1, False)
    begins = lax.dynamic_index_in_dim(begins, core, 1, False)
    starts = jnp.stack([begins[0], begins[2], jnp.where(y < 2, 1, 0).astype(jnp.int32)])

    o, lse = attend(starts, pos, q, k, v)

    kept = lax.dynamic_slice_in_dim(state_in[0], seq_at * 16, 16, 1)

    def scan(unused):
        entering = []
        now = kept
        for at in range(8):
            entering.append(now.astype(jnp.bfloat16))
            now = fades[at, 0, :HEADS][:, None, None] * now + updates[at].astype(jnp.float32)
        return jnp.stack(entering), now

    def no_scan(unused):
        return jnp.zeros((8, HEADS, 16, HDIM), jnp.bfloat16), kept

    entering, state_local = lax.cond(is_self, scan, no_scan, 0)

    o_parts, lses, entered = returning(o, lse, entering)

    lses = jnp.transpose(lses[..., :5], (0, 2, 1, 3)).reshape(4, HALF, HEADS)
    factor = jnp.exp(lses - jnp.max(lses, axis=0))
    factor = factor / jnp.sum(factor, axis=0)
    shaped = o_parts.reshape(4, HALF, HEADS, HDIM).astype(jnp.float32)
    attended = jnp.sum(shaped * factor[..., None], axis=0).reshape(HALF, HD)
    att = (at_x.astype(jnp.float32) + attended * at_gain[1]).astype(jnp.bfloat16)

    def self_mix(unused):
        carried_in = jnp.einsum(
            "thd,hde->the", shaped_q, entered, preferred_element_type=jnp.float32
        )
        mixed = rms_rows(inside + carried_in * growth[:, :, None]).reshape(128, HD)
        return (inputs.astype(jnp.float32) + mixed * out_gain[0]).astype(jnp.bfloat16)

    def no_mix(unused):
        return jnp.zeros((128, HD), jnp.bfloat16)

    mix = lax.cond(is_self, self_mix, no_mix, 0)
    section_output, fresh = onward(att, mix)
    rows = lax.dynamic_slice_in_dim(fresh, (section_at % 2) * 8, 8, 0)
    nfresh = rms_rows(rows.astype(jnp.float32))
    global_new = jnp.concatenate(
        [nfresh * global_gain[0], nfresh * global_gain[1]], axis=1
    ).astype(jnp.bfloat16)
    return (section_output[None], state_local[None], global_new[None, None])


def solution(mesh):
    return jax.shard_map(
        local,
        mesh=mesh,
        in_specs=(
            P("section", "seq", None),
            P("section", None, None, None),
            P(),
            P("section", None),
            P("section", "seq", None),
            P("section", None),
            P("section", None),
            P("section", None),
            P(),
            P(("section", "seq"), None),
            P(("section", "seq")),
            P("section"),
        ),
        out_specs=(
            P("section", "seq", None),
            P("section", None, "seq", None),
            P("seq", "section", None, None),
        ),
        check_vma=False,
    )
```

```python
import jax
import jax.numpy as jnp
from jax import lax
from jax.experimental import pallas as pl
from jax.experimental.pallas import tpu as pltpu
from jax.sharding import PartitionSpec as P

MESH = pl.DeviceIdType.MESH
EPSILON = 1e-06
MASKED_SCORE = -1e30
LOG2E = 1.4426950408889634
HD = 2560
HEADS = 20
HDIM = 128
GROUP = 640
LOCAL_HEADS = 5
HALF = 64
KEYS = 2048
QBLOCK = 256
KCHUNK = 512
STEP = HDIM ** (-0.5) * LOG2E


def device_at(y, x, z, core):
    return (y * 4 + (x // 2) * 2 + core, z * 2 + x % 2)


def shifted(value, by):
    return lax.rem(value + by + 4, 4)


def remote(src, dst, send_sem, recv_sem, peer):
    return pltpu.make_async_remote_copy(
        src_ref=src,
        dst_ref=dst,
        send_sem=send_sem,
        recv_sem=recv_sem,
        device_id=peer,
        device_id_type=MESH,
    )


def span_kernel(
    x_ref,
    state_ref,
    table_ref,
    rate_ref,
    gates_ref,
    gain_ref,
    key_gain_ref,
    global_ref,
    kv_ref,
    meta_ref,
    out_ref,
    state_out,
    global_out,
    at_x,
    at_gain,
    queries,
    kvbuf,
    metabuf,
    qbuf,
    scores_ref,
    pos_ref,
    o_out,
    lse_out,
    o_in,
    lse_in,
    r_att,
    decays,
    decays_t,
    inside,
    self_q,
    kept,
    update_out,
    fade_out,
    update_in,
    fade_in,
    enter_out,
    enter_in,
    r_self,
    fresh,
    h_send,
    h_recv,
    a_send,
    a_recv,
    a_local,
    b_send,
    b_recv,
    c_send,
    c_recv,
    qa_send,
    qa_recv,
    qa_local,
    qb_send,
    qb_recv,
    o_send,
    o_recv,
    o_local,
    u_send,
    u_recv,
    e_send,
    e_recv,
    s_local,
    r_send,
    r_recv,
    w_send,
    w_recv,
    f_send,
    f_recv,
):
    section = lax.axis_index("section")
    seq = lax.axis_index("seq")
    y, core = section // 4, section % 2
    x, z = ((section // 2) % 2) * 2 + seq % 2, seq // 2
    is_self = section < 8
    is_cross = jnp.logical_not(is_self)
    sibling = device_at(y, x, z, 1 - core)
    partner = device_at(3 - y, x, z, core)

    peers = [(lax.rem(section + by, 16), seq) for by in range(1, 16)]
    for dz in range(4):
        for dx in range(4):
            if (dz, dx) not in ((0, 0), (0, 2)):
                peers.append(device_at(y, shifted(x, dx), shifted(z, dz), core))
    barrier = pltpu.get_barrier_semaphore()
    for peer in peers:
        pl.semaphore_signal(barrier, inc=1, device_id=peer, device_id_type=MESH)
    pl.semaphore_wait(barrier, len(peers))

    waits_at_end = []

    half_copy = remote(x_ref.at[pl.ds(HALF, HALF)], at_x, h_send.at[0], h_recv.at[0], partner)
    gain_copy = remote(gain_ref, at_gain, h_send.at[1], h_recv.at[1], partner)

    @pl.when(is_cross)
    def _():
        half_copy.start()
        gain_copy.start()

    META = LOCAL_HEADS

    def kv_source(item, kind, to_x):
        if item == META:
            return meta_ref
        column = to_x * GROUP + item * HDIM + kind * HD
        return kv_ref.at[:, pl.ds(pl.multiple_of(column, HDIM), HDIM)]

    def kv_landing(item, kind, from_x):
        if item == META:
            return metabuf.at[y * 8 + core * 4 + from_x]
        rows = pl.ds(pl.multiple_of(y * 512 + core * 256 + from_x * 64, 64), 64)
        return kvbuf.at[item, rows, pl.ds(kind * HDIM, HDIM)]

    def kinds(item):
        return (0,) if item == META else (0, 1)

    def kv_spread(item):
        for kind in kinds(item):
            pltpu.make_async_copy(
                kv_source(item, kind, x), kv_landing(item, kind, x), a_local.at[item, kind]
            ).start()
            for at, dx in enumerate((1, 3, 2)):
                to_x = shifted(x, dx)
                copy = remote(
                    kv_source(item, kind, to_x),
                    kv_landing(item, kind, x),
                    a_send.at[item, kind, at],
                    a_recv.at[item, kind, at],
                    device_at(y, to_x, z, core),
                )
                copy.start()
                waits_at_end.append(copy)

    def kv_block(item, from_y, from_core, part):
        start, count = ((0, 4), (0, 2), (2, 2))[part]
        if item == META:
            return metabuf.at[pl.ds(from_y * 8 + from_core * 4 + start, count)]
        rows = pl.ds(
            pl.multiple_of(from_y * 512 + from_core * 256 + start * 64, 64), count * 64
        )
        return kvbuf.at[item, rows]

    up, down = device_at(shifted(y, 1), x, z, core), device_at(shifted(y, 3), x, z, core)
    y_up, y_down, y_far = shifted(y, 1), shifted(y, 3), shifted(y, 2)

    def push(ref, sends, recvs, item, at, peer):
        copy = remote(ref, ref, sends.at[item, at], recvs.at[item, at], peer)
        copy.start()
        waits_at_end.append(copy)

    def arrived(ref, sends, recvs, item, at, peer):
        remote(ref, ref, sends.at[item, at], recvs.at[item, at], peer).wait_recv()

    def kv_own(item):
        for kind in kinds(item):
            pltpu.make_async_copy(
                kv_source(item, kind, x), kv_landing(item, kind, x), a_local.at[item, kind]
            ).wait()
            for at, dx in enumerate((1, 3, 2)):
                landed = kv_landing(item, kind, shifted(x, -dx))
                remote(
                    landed, landed, a_send.at[item, kind, at], a_recv.at[item, kind, at], sibling
                ).wait_recv()
        block = kv_block(item, y, core, 0)
        push(block, b_send, b_recv, item, 0, up)
        push(block, b_send, b_recv, item, 1, down)
        push(block, c_send, c_recv, item, 0, sibling)

    def kv_forward(item):
        block = kv_block(item, y_down, core, 0)
        arrived(block, b_send, b_recv, item, 0, up)
        push(kv_block(item, y_down, core, 1), b_send, b_recv, item, 2, up)
        push(block, c_send, c_recv, item, 1, sibling)
        block = kv_block(item, y_up, core, 0)
        arrived(block, b_send, b_recv, item, 1, down)
        push(kv_block(item, y_up, core, 2), b_send, b_recv, item, 3, down)
        push(block, c_send, c_recv, item, 2, sibling)

    def kv_far(item):
        for part in (1, 2):
            block = kv_block(item, y_far, core, part)
            arrived(block, b_send, b_recv, item, part + 1, up)
            push(block, c_send, c_recv, item, part + 2, sibling)

    def kv_ready(item):
        other = 1 - core
        for at, (from_y, part) in enumerate(
            ((y, 0), (y_down, 0), (y_up, 0), (y_far, 1), (y_far, 2))
        ):
            arrived(kv_block(item, from_y, other, part), c_send, c_recv, item, at, sibling)

    def q_source(item, to_x):
        return queries.at[:, pl.ds(pl.multiple_of(to_x * GROUP + item * HDIM, HDIM), HDIM)]

    def q_landing(item, from_x):
        return qbuf.at[item, pl.ds(pl.multiple_of(z * 256 + from_x * HALF, HALF), HALF)]

    def q_spread(item):
        pltpu.make_async_copy(q_source(item, x), q_landing(item, x), qa_local.at[item]).start()
        for at, dx in enumerate((1, 3, 2)):
            to_x = shifted(x, dx)
            copy = remote(
                q_source(item, to_x),
                q_landing(item, x),
                qa_send.at[item, at],
                qa_recv.at[item, at],
                device_at(y, to_x, z, core),
            )
            copy.start()
            waits_at_end.append(copy)

    z_up, z_down, z_far = shifted(z, 1), shifted(z, 3), shifted(z, 2)
    right, left = device_at(y, x, z_up, core), device_at(y, x, z_down, core)

    def q_block(item, from_z, part):
        start, count = ((0, 256), (0, 128), (128, 128))[part]
        return qbuf.at[item, pl.ds(pl.multiple_of(from_z * 256 + start, 128), count)]

    def q_own(item):
        pltpu.make_async_copy(q_source(item, x), q_landing(item, x), qa_local.at[item]).wait()
        for at, dx in enumerate((1, 3, 2)):
            landed = q_landing(item, shifted(x, -dx))
            arrived(landed, qa_send, qa_recv, item, at, right)
        push(q_block(item, z, 0), qb_send, qb_recv, item, 0, right)
        push(q_block(item, z, 0), qb_send, qb_recv, item, 1, left)

    def q_forward(item):
        arrived(q_block(item, z_down, 0), qb_send, qb_recv, item, 0, right)
        push(q_block(item, z_down, 1), qb_send, qb_recv, item, 2, right)
        arrived(q_block(item, z_up, 0), qb_send, qb_recv, item, 1, left)
        push(q_block(item, z_up, 2), qb_send, qb_recv, item, 3, left)

    def q_ready(item):
        arrived(q_block(item, z_far, 1), qb_send, qb_recv, item, 2, right)
        arrived(q_block(item, z_far, 2), qb_send, qb_recv, item, 3, left)

    state_rows = pltpu.make_async_copy(
        state_ref.at[:, pl.ds(pl.multiple_of(seq * 16, 16), 16), :], kept, s_local.at[0]
    )
    state_rows.start()
    lanes = lax.broadcasted_iota(jnp.int32, (128, 128), 1)
    sublanes = lax.broadcasted_iota(jnp.int32, (128, 128), 0)
    causal = sublanes >= lanes

    def inverse_rms(values):
        return lax.rsqrt(jnp.mean(values * values, axis=1, keepdims=True) + EPSILON)

    def decay_column(head):
        return jnp.sum(jnp.where(lanes == head, decays[...], 0.0), axis=1, keepdims=True)

    def decay_setup():
        picked = jnp.zeros((1, HEADS), jnp.float32)
        for entry in range(16):
            picked = jnp.where(rate_ref[...] == entry, table_ref[entry], picked)
        decays[...] = jnp.zeros((128, 128), jnp.float32)
        decays[:, 0:HEADS] = jnp.log(picked) + jnp.log(gates_ref[...])
        summed = jnp.dot(
            jnp.where(causal, 1.0, 0.0),
            decays[...],
            precision=lax.Precision.HIGHEST,
            preferred_element_type=jnp.float32,
        )
        decays[...] = summed
        turned = jnp.transpose(summed)
        decays_t[...] = turned
        fade_out[...] = jnp.broadcast_to(jnp.exp(turned[:, 127:128])[0:24], (24, 128))

    def retain(first, last):
        scale = inverse_rms(x_ref[...].astype(jnp.float32))

        def one(head, carry):
            columns = pl.ds(pl.multiple_of(head * HDIM, HDIM), HDIM)
            values = x_ref[:, columns]
            normed = values.astype(jnp.float32) * scale
            query = (normed * gain_ref[0:1, columns]).astype(jnp.bfloat16)
            key_rows = (normed * key_gain_ref[:, columns]).astype(jnp.bfloat16)
            self_q[:, columns] = query
            products = lax.dot_general(
                query, key_rows, (((1,), (1,)), ((), ())), preferred_element_type=jnp.float32
            )
            column = decay_column(head)
            row = decays_t[pl.ds(head, 1), :]
            weights = jnp.where(
                causal, products * jnp.exp(jnp.where(causal, column - row, 0.0)), 0.0
            ).astype(jnp.bfloat16)
            inside[:, columns] = jnp.dot(weights, values, preferred_element_type=jnp.float32)
            fading = jnp.exp(row[:, 127:128] - column)
            faded = (key_rows.astype(jnp.float32) * fading).astype(jnp.bfloat16)
            update_out[pl.ds(head, 1)] = lax.dot_general(
                faded, values, (((0,), (0,)), ((), ())), preferred_element_type=jnp.float32
            ).astype(jnp.bfloat16)[None]
            return carry

        lax.fori_loop(first, last, one, 0)

    def seq_peer(at):
        to_z, to_x = shifted(z, at // 2), (x // 2) * 2 + lax.rem(x + at % 2, 2)
        return to_z * 2 + to_x % 2, device_at(y, to_x, to_z, core)

    def update_copies():
        copies = []
        for at in range(8):
            to_seq, peer = seq_peer(at)
            rows = pl.ds(pl.multiple_of(to_seq * 16, 16), 16)
            pairs = (
                (update_out.at[:, rows, :], update_in.at[seq]),
                (fade_out, fade_in.at[seq]),
            )
            for kind, (src, dst) in enumerate(pairs):
                if at == 0:
                    copies.append(pltpu.make_async_copy(src, dst, s_local.at[1 + kind]))
                else:
                    copies.append(
                        remote(src, dst, u_send.at[at, kind], u_recv.at[at, kind], peer)
                    )
        return copies

    def enter_copies():
        copies = []
        for at in range(8):
            to_seq, peer = seq_peer(at)
            dst = enter_in.at[:, pl.ds(pl.multiple_of(seq * 16, 16), 16), :]
            if at == 0:
                copies.append(pltpu.make_async_copy(enter_out.at[to_seq], dst, s_local.at[3]))
            else:
                copies.append(
                    remote(enter_out.at[to_seq], dst, e_send.at[at], e_recv.at[at], peer)
                )
        return copies

    def scan():
        def one(head, carry):
            now = kept[pl.ds(head, 1)][0]
            for at in range(8):
                enter_out[at, pl.ds(head, 1)] = now.astype(jnp.bfloat16)[None]
                fade = fade_in[at, pl.ds(head, 1), :]
                now = fade * now + update_in[at, pl.ds(head, 1)][0].astype(jnp.float32)
            state_out[pl.ds(head, 1)] = now[None]
            return carry

        lax.fori_loop(0, HEADS, one, 0)

    def mix(first, last):
        def one(head, carry):
            columns = pl.ds(pl.multiple_of(head * HDIM, HDIM), HDIM)
            carried = jnp.dot(
                self_q[:, columns], enter_in[pl.ds(head, 1)][0], preferred_element_type=jnp.float32
            )
            retained = inside[:, columns] + jnp.exp(decay_column(head)) * carried
            mixed = retained * inverse_rms(retained)
            r_self[:, columns] = (
                x_ref[:, columns].astype(jnp.float32) + mixed * gain_ref[1:2, columns]
            ).astype(jnp.bfloat16)
            return carry

        lax.fori_loop(first, last, one, 0)

    after = (lax.rem(section + 1, 16), seq)

    def self_result(group):
        columns = pl.ds(group * GROUP, GROUP)
        return remote(
            r_self.at[:, columns], out_ref.at[:, columns], w_send.at[group], w_recv.at[group], after
        )

    def fresh_rows(to):
        return r_self.at[pl.ds(pl.multiple_of((to // 2) * 16, 16), 16)]

    own_fresh = pltpu.make_async_copy(fresh_rows(section), fresh, s_local.at[4])

    def fresh_copy(by):
        to = lax.rem(section + by, 16)
        return remote(fresh_rows(to), fresh, f_send.at[by], f_recv.at[0], (to, seq))

    is_root = section == 7

    half_at = jnp.where(is_self, 1, 0)
    y_from = jnp.where(is_self, 3 - y, y)

    def place_setup():
        lane = lax.broadcasted_iota(jnp.int32, (1, 128), 1)
        for pair in range(16):
            pos_ref[:, pair * 128 : (pair + 1) * 128] = jnp.where(
                lane < 64, metabuf[2 * pair, 0:1, :], metabuf[2 * pair + 1, 0:1, :]
            )

    def attend(item):
        index = lax.broadcasted_iota(jnp.int32, (QBLOCK, 128), 0)
        offset = ((index // 64) % 2) * 128 + half_at * HALF + index % 64
        first_tile = y_from * 8 + core * 4
        begin = jnp.where(
            index < 128, metabuf[first_tile][1:2, :], metabuf[first_tile + 2][1:2, :]
        )
        diagonal = lax.broadcasted_iota(jnp.int32, (QBLOCK, QBLOCK), 0) == (
            lax.broadcasted_iota(jnp.int32, (QBLOCK, QBLOCK), 1)
        )

        def block(at, carry):
            rows = pl.ds(pl.multiple_of(at * QBLOCK, QBLOCK), QBLOCK)
            query = qbuf[item, rows, :]
            places = begin + offset + at * 256
            highest = jnp.full((QBLOCK, 128), MASKED_SCORE, jnp.float32)
            for chunk in range(KEYS // KCHUNK):
                keys = kvbuf[item, chunk * KCHUNK : (chunk + 1) * KCHUNK, 0:HDIM]
                scores = lax.dot_general(
                    query, keys, (((1,), (1,)), ((), ())), preferred_element_type=jnp.float32
                )
                for part in range(KCHUNK // 128):
                    here = slice(chunk * KCHUNK + part * 128, chunk * KCHUNK + (part + 1) * 128)
                    piece = jnp.where(
                        pos_ref[:, here] <= places,
                        scores[:, part * 128 : (part + 1) * 128],
                        MASKED_SCORE,
                    )
                    scores_ref[:, here] = piece
                    highest = jnp.maximum(highest, piece)
            top = jnp.max(highest, axis=1, keepdims=True)
            totals = jnp.zeros((QBLOCK, 128), jnp.float32)
            pieces = jnp.zeros((QBLOCK, HDIM), jnp.float32)
            for chunk in range(KEYS // KCHUNK):
                here = slice(chunk * KCHUNK, (chunk + 1) * KCHUNK)
                likely = jnp.exp2((scores_ref[:, here] - top) * STEP)
                for part in range(KCHUNK // 128):
                    totals += likely[:, part * 128 : (part + 1) * 128]
                pieces += jnp.dot(
                    likely.astype(jnp.bfloat16),
                    kvbuf[item, here, HDIM : 2 * HDIM],
                    preferred_element_type=jnp.float32,
                )
            total = jnp.sum(totals, axis=1, keepdims=True)
            o_out[item, rows, :] = (pieces / total).astype(jnp.bfloat16)
            lse = top * HDIM ** (-0.5) + jnp.log(total)
            flat = jnp.sum(jnp.where(diagonal, lse, 0.0), axis=0, keepdims=True)
            for pair in range(2):
                lse_out[item, at, pair] = jnp.broadcast_to(
                    flat[:, pair * 128 : (pair + 1) * 128], (8, 128)
                )
            return carry

        lax.fori_loop(0, 4, block, 0)

    ORDER = [(dz, dx) for dz in (2, 1, 3, 0) for dx in (2, 1, 3, 0)]

    def piece_copies(item):
        copies = []
        for at, (dz, dx) in enumerate(ORDER):
            to_x, to_z = shifted(x, dx), shifted(z, dz)
            rows = pl.ds(pl.multiple_of(to_z * 256 + to_x * HALF, HALF), HALF)
            pairs = (
                (lse_out.at[item, to_z, to_x // 2], lse_in.at[item, z, x]),
                (o_out.at[item, rows], o_in.at[item, z, x]),
            )
            for kind, (src, dst) in enumerate(pairs):
                if (dz, dx) == (0, 0):
                    copies.append(pltpu.make_async_copy(src, dst, o_local.at[item, kind]))
                else:
                    copies.append(
                        remote(
                            src,
                            dst,
                            o_send.at[item, at, kind],
                            o_recv.at[item, at, kind],
                            device_at(y, to_x, to_z, core),
                        )
                    )
        return copies

    def pieces_back(item):
        for copy in piece_copies(item):
            copy.start()

    helped = jnp.where(section < 4, section + 12, section + 4)
    att_target = (jnp.where(is_self, lax.rem(helped + 1, 16), lax.rem(section + 1, 16)), seq)
    att_rows = pl.ds(pl.multiple_of(half_at * HALF, HALF), HALF)

    def att_result(item, group):
        columns = pl.ds(group * GROUP + item * HDIM, HDIM)
        return remote(
            r_att.at[:, columns],
            out_ref.at[att_rows, columns],
            r_send.at[item, group],
            r_recv.at[half_at, item, group],
            att_target,
        )

    def merge(item):
        for copy in piece_copies(item):
            copy.wait()
        row = lax.broadcasted_iota(jnp.int32, (HALF, 128), 0)
        lane = lax.broadcasted_iota(jnp.int32, (HALF, 128), 1)
        mine = lane == row + (x % 2) * HALF
        for group in range(4):
            sums = [
                jnp.sum(
                    jnp.where(mine, lse_in[item, from_z, group, 0:1, :], 0.0), axis=1, keepdims=True
                )
                for from_z in range(4)
            ]
            overall = jnp.maximum(jnp.maximum(sums[0], sums[1]), jnp.maximum(sums[2], sums[3]))
            shares = [jnp.exp(value - overall) for value in sums]
            whole = shares[0] + shares[1] + shares[2] + shares[3]
            attended = jnp.zeros((HALF, HDIM), jnp.float32)
            for from_z in range(4):
                attended += shares[from_z] * o_in[item, from_z, group].astype(jnp.float32)
            attended = attended / whole
            here = slice(group * GROUP + item * HDIM, group * GROUP + (item + 1) * HDIM)
            r_att[:, here] = (
                at_x[:, here].astype(jnp.float32) + attended * at_gain[1:2, here]
            ).astype(jnp.bfloat16)
            att_result(item, group).start()

    kv_spread(META)
    for item in range(LOCAL_HEADS):
        kv_spread(item)

    @pl.when(is_cross)
    def _():
        at_x[...] = x_ref[0:HALF, :]
        at_gain[...] = gain_ref[...]

    @pl.when(is_self)
    def _():
        decay_setup()
        half_copy.wait_recv()
        gain_copy.wait_recv()

    rows = at_x[...].astype(jnp.float32)
    queries[...] = (rows * inverse_rms(rows) * at_gain[0:1, :]).astype(jnp.bfloat16)
    for item in range(LOCAL_HEADS):
        q_spread(item)
    kv_own(META)
    kv_own(0)
    kv_own(1)

    @pl.when(is_self)
    def _():
        retain(0, 7)

    for item in range(LOCAL_HEADS):
        q_own(item)
    kv_forward(META)
    kv_forward(0)
    kv_own(2)

    @pl.when(is_self)
    def _():
        retain(7, 14)

    for item in range(LOCAL_HEADS):
        q_forward(item)
    kv_far(META)
    kv_far(0)
    kv_forward(1)
    kv_own(3)

    @pl.when(is_self)
    def _():
        retain(14, HEADS)
        for copy in update_copies():
            copy.start()

    kv_ready(META)
    place_setup()
    for item in range(LOCAL_HEADS):
        q_ready(item)
    kv_far(1)
    kv_forward(2)
    kv_own(4)
    kv_ready(0)
    attend(0)
    pieces_back(0)

    kv_far(2)
    kv_forward(3)
    kv_ready(1)
    attend(1)
    pieces_back(1)

    state_rows.wait()

    @pl.when(is_self)
    def _():
        for copy in update_copies():
            copy.wait()
        scan()
        for copy in enter_copies():
            copy.start()

    @pl.when(is_cross)
    def _():
        state_out[...] = kept[...]

    kv_far(3)
    kv_forward(4)
    kv_ready(2)
    merge(0)
    attend(2)
    pieces_back(2)

    kv_far(4)
    kv_ready(3)
    merge(1)
    attend(3)
    pieces_back(3)

    @pl.when(is_self)
    def _():
        for copy in enter_copies():
            copy.wait()
        mix(0, HEADS)
        for group in range(4):
            self_result(group).start()

    @pl.when(is_root)
    def _():
        own_fresh.start()
        for by in range(1, 16):
            fresh_copy(by).start()

    kv_ready(4)
    merge(2)
    attend(4)
    pieces_back(4)
    merge(3)

    @pl.when(is_root)
    def _():
        own_fresh.wait()

    @pl.when(jnp.logical_not(is_root))
    def _():
        fresh_copy(1).wait_recv()

    both = fresh[...].astype(jnp.float32)
    new_rows = jnp.where(core == 0, both[0:8], both[8:16])
    new_rows = new_rows * inverse_rms(new_rows)
    global_out[:, 0:HD] = (new_rows * global_ref[0:1, :]).astype(jnp.bfloat16)
    global_out[:, HD : 2 * HD] = (new_rows * global_ref[1:2, :]).astype(jnp.bfloat16)
    merge(4)

    from_self = jnp.logical_and(section >= 1, section <= 8)

    @pl.when(from_self)
    def _():
        for group in range(4):
            self_result(group).wait_recv()

    @pl.when(jnp.logical_not(from_self))
    def _():
        for half in range(2):
            for item in range(LOCAL_HEADS):
                for group in range(4):
                    columns = pl.ds(group * GROUP + item * HDIM, HDIM)
                    landed = out_ref.at[pl.ds(half * HALF, HALF), columns]
                    remote(
                        landed,
                        landed,
                        r_send.at[item, group],
                        r_recv.at[half, item, group],
                        att_target,
                    ).wait_recv()

    for item in range(LOCAL_HEADS):
        for group in range(4):
            att_result(item, group).wait_send()
    for copy in waits_at_end:
        copy.wait_send()

    @pl.when(is_cross)
    def _():
        half_copy.wait_send()
        gain_copy.wait_send()

    @pl.when(is_self)
    def _():
        for group in range(4):
            self_result(group).wait_send()

    @pl.when(is_root)
    def _():
        for by in range(1, 16):
            fresh_copy(by).wait_send()


def span(*arguments):
    vmem = pl.BlockSpec(memory_space=pltpu.VMEM)
    smem = pl.BlockSpec(memory_space=pltpu.SMEM)
    hbm = pl.BlockSpec(memory_space=pl.ANY)
    dma = pltpu.SemaphoreType.DMA
    items = LOCAL_HEADS + 1

    def bf16(*shape):
        return pltpu.VMEM(shape, jnp.bfloat16)

    def f32(*shape):
        return pltpu.VMEM(shape, jnp.float32)

    return pl.pallas_call(
        span_kernel,
        out_shape=(
            jax.ShapeDtypeStruct((128, HD), jnp.bfloat16),
            jax.ShapeDtypeStruct((HEADS, 16, HDIM), jnp.float32),
            jax.ShapeDtypeStruct((8, 2 * HD), jnp.bfloat16),
        ),
        in_specs=[vmem, hbm, smem, vmem, vmem, vmem, vmem, vmem, hbm, hbm],
        out_specs=(vmem, vmem, vmem),
        scratch_shapes=[
            bf16(HALF, HD),
            f32(8, HD),
            bf16(HALF, HD),
            bf16(LOCAL_HEADS, KEYS, 2 * HDIM),
            pltpu.VMEM((32, 8, 128), jnp.int32),
            bf16(LOCAL_HEADS, 1024, HDIM),
            f32(QBLOCK, KEYS),
            pltpu.VMEM((1, KEYS), jnp.int32),
            bf16(LOCAL_HEADS, 1024, HDIM),
            f32(LOCAL_HEADS, 4, 2, 8, 128),
            bf16(LOCAL_HEADS, 4, 4, HALF, HDIM),
            f32(LOCAL_HEADS, 4, 4, 8, 128),
            bf16(HALF, HD),
            f32(128, 128),
            f32(128, 128),
            f32(128, HD),
            bf16(128, HD),
            f32(HEADS, 16, HDIM),
            bf16(HEADS, HDIM, HDIM),
            f32(24, 128),
            bf16(8, HEADS, 16, HDIM),
            f32(8, 24, 128),
            bf16(8, HEADS, 16, HDIM),
            bf16(HEADS, HDIM, HDIM),
            bf16(128, HD),
            bf16(16, HD),
            dma((2,)),
            dma((2,)),
            dma((items, 2, 3)),
            dma((items, 2, 3)),
            dma((items, 2)),
            dma((items, 4)),
            dma((items, 4)),
            dma((items, 5)),
            dma((items, 5)),
            dma((LOCAL_HEADS, 3)),
            dma((LOCAL_HEADS, 3)),
            dma((LOCAL_HEADS,)),
            dma((LOCAL_HEADS, 4)),
            dma((LOCAL_HEADS, 4)),
            dma((LOCAL_HEADS, 16, 2)),
            dma((LOCAL_HEADS, 16, 2)),
            dma((LOCAL_HEADS, 2)),
            dma((8, 2)),
            dma((8, 2)),
            dma((8,)),
            dma((8,)),
            dma((5,)),
            dma((LOCAL_HEADS, 4)),
            dma((2, LOCAL_HEADS, 4)),
            dma((4,)),
            dma((4,)),
            dma((16,)),
            dma((1,)),
        ],
        compiler_params=pltpu.CompilerParams(
            collective_id=0, has_side_effects=True, vmem_limit_bytes=48 * 1024 * 1024
        ),
        name="span",
    )(*arguments)


def local(
    section_input,
    state_in,
    decay_table,
    head_rate,
    gates,
    query_gain,
    key_gain,
    out_gain,
    global_gain,
    cache_kv,
    cache_pos,
    span_start,
):
    gains = jnp.concatenate([query_gain, out_gain, jnp.zeros((6, HD), jnp.float32)], axis=0)
    rows = jnp.concatenate([cache_pos, cache_pos])[None]
    begin = jnp.broadcast_to(span_start[:, None], (7, 128))
    meta = jnp.concatenate([rows, begin], axis=0)
    section_output, state_out, global_new = span(
        section_input[0],
        state_in[0],
        decay_table,
        head_rate,
        gates[0],
        gains,
        key_gain,
        global_gain,
        cache_kv,
        meta,
    )
    return (section_output[None], state_out[None], global_new[None, None])


def solution(mesh):
    return jax.shard_map(
        local,
        mesh=mesh,
        in_specs=(
            P("section", "seq", None),
            P("section", None, None, None),
            P(),
            P("section", None),
            P("section", "seq", None),
            P("section", None),
            P("section", None),
            P("section", None),
            P(),
            P(("section", "seq"), None),
            P(("section", "seq")),
            P("section"),
        ),
        out_specs=(
            P("section", "seq", None),
            P("section", None, "seq", None),
            P("seq", "section", None, None),
        ),
        check_vma=False,
    )
```

```python
import jax
import jax.numpy as jnp
from jax import lax
from jax.experimental import pallas as pl
from jax.experimental.pallas import tpu as pltpu
from jax.sharding import PartitionSpec as P

MESH = pl.DeviceIdType.MESH
EPSILON = 1e-06
MASKED_SCORE = -1e30
LOG2E = 1.4426950408889634
HD = 2560
HEADS = 20
HDIM = 128
GROUP = 640
LOCAL_HEADS = 5
KEYS = 2048
TOKENS = 128
QBLOCK = 256
KCHUNK = 512
STEP = HDIM ** (-0.5) * LOG2E


def device_at(y, x, z, core):
    return (y * 4 + (x // 2) * 2 + core, z * 2 + x % 2)


def shifted(value, by):
    return lax.rem(value + by + 4, 4)


def remote(src, dst, send_sem, recv_sem, peer):
    return pltpu.make_async_remote_copy(
        src_ref=src,
        dst_ref=dst,
        send_sem=send_sem,
        recv_sem=recv_sem,
        device_id=peer,
        device_id_type=MESH,
    )


def span_kernel(
    x_hbm,
    state_ref,
    table_hbm,
    rate_hbm,
    gates_hbm,
    query_gain_hbm,
    key_gain_hbm,
    out_gain_hbm,
    global_hbm,
    kv_ref,
    positions_hbm,
    start_hbm,
    out_ref,
    state_out,
    global_out,
    x_ref,
    table_ref,
    start_ref,
    rate_ref,
    gates_ref,
    query_gain_ref,
    key_gain_ref,
    out_gain_ref,
    global_ref,
    positions_ref,
    i_local,
    queries,
    meta_ref,
    begin_ref,
    kvbuf,
    metabuf,
    beginbuf,
    qbuf,
    scores_ref,
    pos_ref,
    o_out,
    lse_out,
    o_in,
    lse_in,
    att_out,
    att_in,
    result,
    decays,
    decays_t,
    inside,
    kept,
    update_out,
    fade_out,
    update_in,
    fade_in,
    enter_out,
    enter_in,
    fresh,
    a_send,
    a_recv,
    a_local,
    b_send,
    b_recv,
    c_send,
    c_recv,
    qa_send,
    qa_recv,
    qa_local,
    qb_send,
    qb_recv,
    o_send,
    o_recv,
    t_send,
    t_recv,
    t_local,
    u_send,
    u_recv,
    e_send,
    e_recv,
    s_local,
    r_send,
    r_recv,
    w_send,
    w_recv,
    f_send,
    f_recv,
):
    section = lax.axis_index("section")
    seq = lax.axis_index("seq")
    y, core = section // 4, section % 2
    x, z = ((section // 2) % 2) * 2 + seq % 2, seq // 2
    is_self = section < 8
    is_cross = jnp.logical_not(is_self)
    is_root = section == 7
    sibling = device_at(y, x, z, 1 - core)
    other = device_at(y + 1 - 2 * (y % 2), x, z, core)
    partner = device_at(3 - y, x, z, core)
    after = (lax.rem(section + 1, 16), seq)
    before = (lax.rem(section + 15, 16), seq)

    fetches = [
        pltpu.make_async_copy(src, dst, i_local.at[at])
        for at, (src, dst) in enumerate(
            (
                (x_hbm, x_ref),
                (table_hbm, table_ref),
                (start_hbm, start_ref),
                (query_gain_hbm, query_gain_ref),
                (positions_hbm, positions_ref),
                (rate_hbm, rate_ref),
                (gates_hbm, gates_ref),
                (key_gain_hbm, key_gain_ref),
                (out_gain_hbm, out_gain_ref),
                (global_hbm, global_ref),
            )
        )
    ]
    for copy in fetches:
        copy.start()
    state_rows = pltpu.make_async_copy(
        state_ref.at[:, pl.ds(pl.multiple_of(seq * 16, 16), 16), :], kept, s_local.at[0]
    )
    state_rows.start()

    def seq_peer(at):
        to_z, to_x = shifted(z, at // 2), (x // 2) * 2 + lax.rem(x + at % 2, 2)
        return to_z * 2 + to_x % 2, device_at(y, to_x, to_z, core)

    peers = [sibling, other, partner]
    peers += [device_at(y, shifted(x, dx), z, core) for dx in (1, 2, 3)]
    peers += [seq_peer(at)[1] for at in range(2, 8)]
    barrier = pltpu.get_barrier_semaphore()
    for peer in peers + [before]:
        pl.semaphore_signal(barrier, inc=1, device_id=peer, device_id_type=MESH)

    @pl.when(jnp.logical_not(is_root))
    def _():
        pl.semaphore_signal(barrier, inc=1, device_id=(7, seq), device_id_type=MESH)

    waits_at_end = []

    META = LOCAL_HEADS

    def kinds(item):
        return (0,) if item == META else (0, 1)

    def kv_source(item, kind, to_x):
        if item == META:
            return meta_ref
        column = to_x * GROUP + item * HDIM + kind * HD
        return kv_ref.at[:, pl.ds(pl.multiple_of(column, HDIM), HDIM)]

    def kv_landing(item, kind, from_x):
        if item == META:
            return metabuf.at[z * 8 + core * 4 + from_x]
        rows = pl.ds(pl.multiple_of(z * 512 + core * 256 + from_x * 64, 64), 64)
        return kvbuf.at[item, rows, pl.ds(kind * HDIM, HDIM)]

    def kv_spread(item):
        for kind in kinds(item):
            for at, dx in enumerate((2, 1, 3)):
                to_x = shifted(x, dx)
                copy = remote(
                    kv_source(item, kind, to_x),
                    kv_landing(item, kind, x),
                    a_send.at[item, kind, at],
                    a_recv.at[item, kind, at],
                    device_at(y, to_x, z, core),
                )
                copy.start()
                waits_at_end.append(copy)
            pltpu.make_async_copy(
                kv_source(item, kind, x), kv_landing(item, kind, x), a_local.at[item, kind]
            ).start()

    def kv_block(item, from_z, from_core, part):
        start, count = ((0, 4), (0, 2), (2, 2))[part]
        if item == META:
            return metabuf.at[pl.ds(from_z * 8 + from_core * 4 + start, count)]
        rows = pl.ds(
            pl.multiple_of(from_z * 512 + from_core * 256 + start * 64, 64), count * 64
        )
        return kvbuf.at[item, rows]

    z_up, z_down, z_far = shifted(z, 1), shifted(z, 3), shifted(z, 2)
    up, down = device_at(y, x, z_up, core), device_at(y, x, z_down, core)

    def push(ref, sends, recvs, item, at, peer, came=None):
        copy = remote(ref, ref, sends.at[item, at], recvs.at[item, at if came is None else came], peer)
        copy.start()
        return copy

    def arrived(ref, sends, recvs, item, at, peer):
        remote(ref, ref, sends.at[item, at], recvs.at[item, at], peer).wait_recv()

    def kv_own(item):
        for kind in kinds(item):
            pltpu.make_async_copy(
                kv_source(item, kind, x), kv_landing(item, kind, x), a_local.at[item, kind]
            ).wait()
            for at, dx in enumerate((2, 1, 3)):
                landed = kv_landing(item, kind, shifted(x, -dx))
                remote(
                    landed, landed, a_send.at[item, kind, at], a_recv.at[item, kind, at], sibling
                ).wait_recv()
        block = kv_block(item, z, core, 0)
        waits_at_end.append(push(block, b_send, b_recv, item, 0, up))
        waits_at_end.append(push(block, b_send, b_recv, item, 1, down))
        waits_at_end.append(push(block, c_send, c_recv, item, 0, sibling))

    def kv_forward(item):
        block = kv_block(item, z_down, core, 0)
        arrived(block, b_send, b_recv, item, 0, up)
        waits_at_end.append(push(kv_block(item, z_down, core, 1), b_send, b_recv, item, 2, up))
        waits_at_end.append(push(block, c_send, c_recv, item, 1, sibling))
        block = kv_block(item, z_up, core, 0)
        arrived(block, b_send, b_recv, item, 1, down)
        waits_at_end.append(push(kv_block(item, z_up, core, 2), b_send, b_recv, item, 3, down))
        waits_at_end.append(push(block, c_send, c_recv, item, 2, sibling))

    def kv_far(item):
        for part in (1, 2):
            block = kv_block(item, z_far, core, part)
            arrived(block, b_send, b_recv, item, part + 1, up)
            waits_at_end.append(push(block, c_send, c_recv, item, part + 2, sibling))

    def kv_ready(item):
        for at, (from_z, part) in enumerate(
            ((z, 0), (z_down, 0), (z_up, 0), (z_far, 1), (z_far, 2))
        ):
            arrived(kv_block(item, from_z, 1 - core, part), c_send, c_recv, item, at, sibling)

    own_j = jnp.where(is_self, 1 - y, y - 2)

    def q_source(item, to_x):
        if item == META:
            return begin_ref
        return queries.at[:, pl.ds(pl.multiple_of(to_x * GROUP + item * HDIM, HDIM), HDIM)]

    def q_landing(item, from_x):
        if item == META:
            return beginbuf.at[own_j * 4 + from_x]
        rows = pl.ds(pl.multiple_of(own_j * 512 + from_x * TOKENS, TOKENS), TOKENS)
        return qbuf.at[item, rows]

    def q_own_copy(item):
        return pltpu.make_async_copy(q_source(item, x), q_landing(item, x), qa_local.at[item])

    def q_spread_copies(item):
        return [
            remote(
                q_source(item, shifted(x, dx)),
                q_landing(item, x),
                qa_send.at[item, at],
                qa_recv.at[item, at],
                device_at(y, shifted(x, dx), z, core),
            )
            for at, dx in enumerate((2, 1, 3))
        ]

    def q_spread(item):
        for copy in q_spread_copies(item):
            copy.start()
        q_own_copy(item).start()

    def q_block(item, j):
        if item == META:
            return beginbuf.at[pl.ds(j * 4, 4)]
        return qbuf.at[item, pl.ds(pl.multiple_of(j * 512, 512), 512)]

    def q_push(item, at):
        peer = (other, partner, other)[at]
        return remote(
            q_block(item, own_j),
            q_block(item, own_j),
            qb_send.at[item, at],
            qb_recv.at[item, (0, 0, 1)[at]],
            peer,
        )

    def q_own(item):
        q_own_copy(item).wait()
        for at, dx in enumerate((2, 1, 3)):
            arrived(q_landing(item, shifted(x, -dx)), qa_send, qa_recv, item, at, sibling)
        q_push(item, 1).start()
        q_push(item, 0).start()

    def q_relay(item):
        arrived(q_block(item, own_j), qb_send, qb_recv, item, 0, partner)
        q_push(item, 2).start()

    def q_pass(item):
        @pl.when(is_cross)
        def _():
            q_own(item)

        @pl.when(is_self)
        def _():
            q_relay(item)

    def q_ready(item):
        @pl.when(is_cross)
        def _():
            arrived(q_block(item, 1 - own_j), qb_send, qb_recv, item, 0, other)

        @pl.when(is_self)
        def _():
            arrived(q_block(item, 1 - own_j), qb_send, qb_recv, item, 1, other)

    lanes = lax.broadcasted_iota(jnp.int32, (128, 128), 1)
    sublanes = lax.broadcasted_iota(jnp.int32, (128, 128), 0)
    causal = sublanes >= lanes
    diagonal = sublanes == lanes

    def inverse_rms(values):
        return lax.rsqrt(jnp.mean(values * values, axis=1, keepdims=True) + EPSILON)

    def decay_column(head):
        return jnp.sum(jnp.where(lanes == head, decays[...], 0.0), axis=1, keepdims=True)

    def decay_setup():
        decays[...] = jnp.ones((128, 128), jnp.float32)
        decays_t[...] = jnp.ones((128, 128), jnp.float32)
        for head in range(HEADS):
            decays[head : head + 1, :] = gates_ref[head]
            picked = table_ref[rate_ref[0, head]]
            decays_t[head : head + 1, :] = jnp.full((1, 128), picked, jnp.float32)
        turned = jnp.dot(
            jnp.log(decays_t[...]) + jnp.log(decays[...]),
            jnp.where(sublanes <= lanes, 1.0, 0.0),
            precision=lax.Precision.HIGHEST,
            preferred_element_type=jnp.float32,
        )
        decays_t[...] = turned
        decays[...] = jnp.transpose(turned)
        fade_out[...] = jnp.broadcast_to(jnp.exp(turned[:, 127:128])[0:24], (24, 128))

    def retain(first, last):
        scale = inverse_rms(x_ref[...].astype(jnp.float32))

        def one(head, carry):
            columns = pl.ds(pl.multiple_of(head * HDIM, HDIM), HDIM)
            values = x_ref[:, columns]
            normed = values.astype(jnp.float32) * scale
            query = (normed * query_gain_ref[:, columns]).astype(jnp.bfloat16)
            key_rows = (normed * key_gain_ref[:, columns]).astype(jnp.bfloat16)
            queries[:, columns] = query
            products = lax.dot_general(
                query, key_rows, (((1,), (1,)), ((), ())), preferred_element_type=jnp.float32
            )
            column = decay_column(head)
            row = decays_t[pl.ds(head, 1), :]
            weights = jnp.where(
                causal, products * jnp.exp(jnp.where(causal, column - row, 0.0)), 0.0
            ).astype(jnp.bfloat16)
            inside[:, columns] = jnp.dot(weights, values, preferred_element_type=jnp.float32)
            fading = jnp.exp(row[:, 127:128] - column)
            faded = (key_rows.astype(jnp.float32) * fading).astype(jnp.bfloat16)
            update_out[pl.ds(head, 1)] = lax.dot_general(
                faded, values, (((0,), (0,)), ((), ())), preferred_element_type=jnp.float32
            ).astype(jnp.bfloat16)[None]
            return carry

        lax.fori_loop(first, last, one, 0)

    def update_copies():
        copies = []
        for at in range(8):
            to_seq, peer = seq_peer(at)
            rows = pl.ds(pl.multiple_of(to_seq * 16, 16), 16)
            pairs = (
                (update_out.at[:, rows, :], update_in.at[seq]),
                (fade_out, fade_in.at[seq]),
            )
            for kind, (src, dst) in enumerate(pairs):
                if at == 0:
                    copies.append(pltpu.make_async_copy(src, dst, s_local.at[1 + kind]))
                else:
                    copies.append(
                        remote(src, dst, u_send.at[at, kind], u_recv.at[at, kind], peer)
                    )
        return copies

    def enter_copies():
        copies = []
        for at in range(8):
            to_seq, peer = seq_peer(at)
            dst = enter_in.at[:, pl.ds(pl.multiple_of(seq * 16, 16), 16), :]
            if at == 0:
                copies.append(pltpu.make_async_copy(enter_out.at[to_seq], dst, s_local.at[3]))
            else:
                copies.append(
                    remote(enter_out.at[to_seq], dst, e_send.at[at], e_recv.at[at], peer)
                )
        return copies

    def scan():
        def one(head, carry):
            now = kept[pl.ds(head, 1)][0]
            for at in range(8):
                enter_out[at, pl.ds(head, 1)] = now.astype(jnp.bfloat16)[None]
                fade = fade_in[at, pl.ds(head, 1), :]
                now = fade * now + update_in[at, pl.ds(head, 1)][0].astype(jnp.float32)
            state_out[pl.ds(head, 1)] = now[None]
            return carry

        lax.fori_loop(0, HEADS, one, 0)

    def mix(first, last):
        def one(head, carry):
            columns = pl.ds(pl.multiple_of(head * HDIM, HDIM), HDIM)
            carried = jnp.dot(
                queries[:, columns], enter_in[pl.ds(head, 1)][0], preferred_element_type=jnp.float32
            )
            retained = inside[:, columns] + jnp.exp(decay_column(head)) * carried
            mixed = retained * inverse_rms(retained)
            result[:, columns] = (
                x_ref[:, columns].astype(jnp.float32) + mixed * out_gain_ref[:, columns]
            ).astype(jnp.bfloat16)
            return carry

        lax.fori_loop(first, last, one, 0)

    def self_result(group):
        columns = pl.ds(group * GROUP, GROUP)
        return remote(
            result.at[:, columns], out_ref.at[:, columns], w_send.at[group], w_recv.at[group], after
        )

    def fresh_rows(to):
        return result.at[pl.ds(pl.multiple_of((to // 2) * 16, 16), 16)]

    own_fresh = pltpu.make_async_copy(fresh_rows(section), fresh, s_local.at[4])

    def fresh_copy(by):
        to = lax.rem(section + by, 16)
        return remote(fresh_rows(to), fresh, f_send.at[by], f_recv.at[0], (to, seq))

    first_j = 1 - own_j

    def place_setup():
        lane = lax.broadcasted_iota(jnp.int32, (1, 128), 1)
        for pair in range(16):
            pos_ref[:, pair * 128 : (pair + 1) * 128] = jnp.where(
                lane < 64,
                metabuf[2 * pair, 0:1, :],
                pltpu.roll(metabuf[2 * pair + 1, 0:1, :], 64, 1),
            )

    def attend(item, j):
        index = lax.broadcasted_iota(jnp.int32, (QBLOCK, 128), 0) + z * 256
        wide = lax.broadcasted_iota(jnp.int32, (QBLOCK, QBLOCK), 0) == (
            lax.broadcasted_iota(jnp.int32, (QBLOCK, QBLOCK), 1)
        )

        def block(at, carry):
            rows = pl.ds(pl.multiple_of(j * 512 + at * QBLOCK, QBLOCK), QBLOCK)
            query = qbuf[item, rows, :]
            places = index + beginbuf[j * 4 + at * 2][0:1, :]
            highest = jnp.full((QBLOCK, 128), MASKED_SCORE, jnp.float32)
            for chunk in range(KEYS // KCHUNK):
                keys = kvbuf[item, chunk * KCHUNK : (chunk + 1) * KCHUNK, 0:HDIM]
                scores = lax.dot_general(
                    query, keys, (((1,), (1,)), ((), ())), preferred_element_type=jnp.float32
                )
                for part in range(KCHUNK // 128):
                    here = slice(chunk * KCHUNK + part * 128, chunk * KCHUNK + (part + 1) * 128)
                    piece = jnp.where(
                        pos_ref[:, here] <= places,
                        scores[:, part * 128 : (part + 1) * 128],
                        MASKED_SCORE,
                    )
                    scores_ref[:, here] = piece
                    highest = jnp.maximum(highest, piece)
            top = jnp.max(highest, axis=1, keepdims=True)
            totals = jnp.zeros((QBLOCK, 128), jnp.float32)
            pieces = jnp.zeros((QBLOCK, HDIM), jnp.float32)
            for chunk in range(KEYS // KCHUNK):
                here = slice(chunk * KCHUNK, (chunk + 1) * KCHUNK)
                likely = jnp.exp2((scores_ref[:, here] - top) * STEP)
                for part in range(KCHUNK // 128):
                    totals += likely[:, part * 128 : (part + 1) * 128]
                pieces += jnp.dot(
                    likely.astype(jnp.bfloat16),
                    kvbuf[item, here, HDIM : 2 * HDIM],
                    preferred_element_type=jnp.float32,
                )
            total = jnp.sum(totals, axis=1, keepdims=True)
            o_out[item, rows, :] = (pieces / total).astype(jnp.bfloat16)
            lse = top * HDIM ** (-0.5) + jnp.log(total)
            flat = jnp.sum(jnp.where(wide, lse, 0.0), axis=0, keepdims=True)
            lse_out[item, j, pl.ds(at * 2, 1), :] = flat[:, 0:128]
            lse_out[item, j, pl.ds(at * 2 + 1, 1), :] = flat[:, 128:256]
            return carry

        lax.fori_loop(0, 2, block, 0)

    def pieces_of(item, j):
        return o_out.at[item, pl.ds(pl.multiple_of(j * 512, 512), 512)], lse_out.at[item, j]

    def piece_copies(item, at):
        peer, j = ((other, first_j), (partner, own_j))[at]
        o_src, lse_src = pieces_of(item, j)
        return [
            remote(o_src, o_in.at[item, at], o_send.at[item, at, 0], o_recv.at[item, at, 0], peer),
            remote(
                lse_src, lse_in.at[item, at], o_send.at[item, at, 1], o_recv.at[item, at, 1], peer
            ),
        ]

    def shares_of(tiles):
        overall = tiles[0]
        for tile in tiles[1:]:
            overall = jnp.maximum(overall, tile)
        shares = [jnp.exp(tile - overall) for tile in tiles]
        whole = shares[0]
        for share in shares[1:]:
            whole = whole + share
        return [share / whole for share in shares], overall + jnp.log(whole)

    def weighted(shares, parts, group):
        total = jnp.zeros((TOKENS, HDIM), jnp.float32)
        for share, part in zip(shares, parts):
            column = jnp.sum(
                jnp.where(diagonal, share[group : group + 1, :], 0.0), axis=1, keepdims=True
            )
            total += column * part.astype(jnp.float32)
        return total.astype(jnp.bfloat16)

    def own_rows(group):
        return pl.ds(pl.multiple_of(own_j * 512 + group * TOKENS, TOKENS), TOKENS)

    def merge_self(item):
        for copy in piece_copies(item, 0):
            copy.wait_recv()
        shares, lse = shares_of([lse_out[item, own_j], lse_in[item, 0]])
        for group in range(4):
            here = slice(group * TOKENS, (group + 1) * TOKENS)
            o_out[item, own_rows(group), :] = weighted(
                shares, (o_out[item, own_rows(group), :], o_in[item, 0, here, :]), group
            )
        lse_out[item, own_j] = lse
        for copy in piece_copies(item, 1):
            copy.start()

    def att_copies(item):
        copies = [
            pltpu.make_async_copy(
                att_out.at[item, pl.ds(pl.multiple_of(x * TOKENS, TOKENS), TOKENS)],
                att_in.at[item, x],
                t_local.at[item],
            )
        ]
        for at, dx in enumerate((2, 1, 3)):
            to_x = shifted(x, dx)
            copies.append(
                remote(
                    att_out.at[item, pl.ds(pl.multiple_of(to_x * TOKENS, TOKENS), TOKENS)],
                    att_in.at[item, x],
                    t_send.at[item, at],
                    t_recv.at[item, at],
                    device_at(y, to_x, z, core),
                )
            )
        return copies

    def merge_cross(item):
        for at in range(2):
            for copy in piece_copies(item, at):
                copy.wait_recv()
        shares, _ = shares_of([lse_out[item, own_j], lse_in[item, 0], lse_in[item, 1]])
        for group in range(4):
            here = slice(group * TOKENS, (group + 1) * TOKENS)
            att_out[item, here, :] = weighted(
                shares,
                (
                    o_out[item, own_rows(group), :],
                    o_in[item, 0, here, :],
                    o_in[item, 1, here, :],
                ),
                group,
            )
        for copy in att_copies(item):
            copy.start()

    def att_result(item, group):
        columns = pl.ds(group * GROUP + item * HDIM, HDIM)
        return remote(
            result.at[:, columns],
            out_ref.at[:, columns],
            r_send.at[item, group],
            r_recv.at[item, group],
            after,
        )

    def finish(item):
        for copy in att_copies(item):
            copy.wait()
        for group in range(4):
            here = slice(group * GROUP + item * HDIM, group * GROUP + (item + 1) * HDIM)
            result[:, here] = (
                x_ref[:, here].astype(jnp.float32)
                + att_in[item, group].astype(jnp.float32) * out_gain_ref[:, here]
            ).astype(jnp.bfloat16)
            att_result(item, group).start()

    for copy in fetches:
        copy.wait()
    meta_ref[0:1, 0:64] = positions_ref[...]
    begin_ref[...] = jnp.full((8, 128), start_ref[0, 0], jnp.int32)

    @pl.when(is_cross)
    def _():
        rows = x_ref[...].astype(jnp.float32)
        queries[...] = (rows * inverse_rms(rows) * query_gain_ref[...]).astype(jnp.bfloat16)

    @pl.when(is_self)
    def _():
        decay_setup()

    pl.semaphore_wait(barrier, len(peers) + 1 + jnp.where(is_root, 15, 0))

    for item in (META, 0, 1, 2, 3, 4):
        kv_spread(item)

        @pl.when(is_cross)
        def _():
            q_spread(item)

    kv_own(META)
    kv_own(0)
    kv_own(1)

    @pl.when(is_cross)
    def _():
        q_own(META)
        q_own(0)
        q_own(1)

    @pl.when(is_self)
    def _():
        retain(0, 7)
        q_relay(META)
        q_relay(0)

    kv_forward(META)
    kv_forward(0)
    kv_own(2)

    @pl.when(is_self)
    def _():
        retain(7, 14)
        q_relay(1)

    kv_far(META)
    kv_far(0)
    kv_forward(1)
    kv_own(3)

    @pl.when(is_self)
    def _():
        retain(14, HEADS)
        for copy in update_copies():
            copy.start()

    q_ready(META)
    kv_ready(META)
    place_setup()
    kv_far(1)
    kv_forward(2)
    kv_own(4)

    def service(step):
        if step == 0:
            q_pass(2)
        if step == 1:
            kv_far(2)
            kv_forward(3)
            q_pass(3)
        if step == 2:
            kv_far(3)
            kv_forward(4)
            q_pass(4)
        if step == 3:
            kv_far(4)

    for item in range(LOCAL_HEADS):
        q_ready(item)
        kv_ready(item)
        attend(item, first_j)
        for copy in piece_copies(item, 0):
            copy.start()
        service(item)
        attend(item, own_j)

        @pl.when(is_self)
        def _():
            merge_self(item)

        if item == 1:
            state_rows.wait()

            @pl.when(is_cross)
            def _():
                state_out[...] = kept[...]

            @pl.when(is_self)
            def _():
                for copy in update_copies():
                    copy.wait()
                scan()
                for copy in enter_copies():
                    copy.start()

        if item == 3:

            @pl.when(is_self)
            def _():
                for copy in enter_copies():
                    copy.wait()
                mix(0, HEADS)
                for group in range(4):
                    self_result(group).start()

            @pl.when(is_root)
            def _():
                own_fresh.start()
                for by in range(1, 16):
                    fresh_copy(by).start()

        @pl.when(is_cross)
        def _():
            if item >= 2:
                merge_cross(item - 2)
            if item >= 3:
                finish(item - 3)

    @pl.when(is_cross)
    def _():
        merge_cross(3)
        finish(2)
        merge_cross(4)
        finish(3)
        finish(4)

    @pl.when(is_root)
    def _():
        own_fresh.wait()

    @pl.when(jnp.logical_not(is_root))
    def _():
        fresh_copy(1).wait_recv()

    both = fresh[...].astype(jnp.float32)
    new_rows = jnp.where(core == 0, both[0:8], both[8:16])
    new_rows = new_rows * inverse_rms(new_rows)
    global_out[:, 0:HD] = (new_rows * global_ref[0:1, :]).astype(jnp.bfloat16)
    global_out[:, HD : 2 * HD] = (new_rows * global_ref[1:2, :]).astype(jnp.bfloat16)

    from_self = jnp.logical_and(section >= 1, section <= 8)

    @pl.when(from_self)
    def _():
        for group in range(4):
            self_result(group).wait_recv()

    @pl.when(jnp.logical_not(from_self))
    def _():
        for item in range(LOCAL_HEADS):
            for group in range(4):
                att_result(item, group).wait_recv()

    for copy in waits_at_end:
        copy.wait_send()
    for item in range(LOCAL_HEADS):
        for copy in piece_copies(item, 0):
            copy.wait_send()

    @pl.when(is_cross)
    def _():
        for item in range(LOCAL_HEADS + 1):
            for copy in q_spread_copies(item):
                copy.wait_send()
            q_push(item, 0).wait_send()
            q_push(item, 1).wait_send()
        for item in range(LOCAL_HEADS):
            for group in range(4):
                att_result(item, group).wait_send()

    @pl.when(is_self)
    def _():
        for item in range(LOCAL_HEADS + 1):
            q_push(item, 2).wait_send()
        for item in range(LOCAL_HEADS):
            for copy in piece_copies(item, 1):
                copy.wait_send()
        for group in range(4):
            self_result(group).wait_send()

    @pl.when(is_root)
    def _():
        for by in range(1, 16):
            fresh_copy(by).wait_send()


def span(*arguments):
    vmem = pl.BlockSpec(memory_space=pltpu.VMEM)
    hbm = pl.BlockSpec(memory_space=pl.ANY)
    dma = pltpu.SemaphoreType.DMA
    items = LOCAL_HEADS + 1

    def bf16(*shape):
        return pltpu.VMEM(shape, jnp.bfloat16)

    def f32(*shape):
        return pltpu.VMEM(shape, jnp.float32)

    def i32(*shape):
        return pltpu.VMEM(shape, jnp.int32)

    return pl.pallas_call(
        span_kernel,
        out_shape=(
            jax.ShapeDtypeStruct((TOKENS, HD), jnp.bfloat16),
            jax.ShapeDtypeStruct((HEADS, 16, HDIM), jnp.float32),
            jax.ShapeDtypeStruct((8, 2 * HD), jnp.bfloat16),
        ),
        in_specs=[hbm] * 12,
        out_specs=(vmem, vmem, vmem),
        scratch_shapes=[
            bf16(TOKENS, HD),
            pltpu.SMEM((16,), jnp.float32),
            pltpu.SMEM((1, 1), jnp.int32),
            pltpu.SMEM((1, HEADS), jnp.int32),
            f32(HEADS, 1, TOKENS),
            f32(1, HD),
            f32(1, HD),
            f32(1, HD),
            f32(2, HD),
            i32(1, 64),
            dma((10,)),
            bf16(TOKENS, HD),
            i32(8, 128),
            i32(8, 128),
            bf16(LOCAL_HEADS, KEYS, 2 * HDIM),
            i32(32, 8, 128),
            i32(8, 8, 128),
            bf16(LOCAL_HEADS, 1024, HDIM),
            f32(QBLOCK, KEYS),
            i32(1, KEYS),
            bf16(LOCAL_HEADS, 1024, HDIM),
            f32(LOCAL_HEADS, 2, 8, 128),
            bf16(LOCAL_HEADS, 2, 512, HDIM),
            f32(LOCAL_HEADS, 2, 8, 128),
            bf16(LOCAL_HEADS, 512, HDIM),
            bf16(LOCAL_HEADS, 4, TOKENS, HDIM),
            bf16(TOKENS, HD),
            f32(128, 128),
            f32(128, 128),
            f32(TOKENS, HD),
            f32(HEADS, 16, HDIM),
            bf16(HEADS, HDIM, HDIM),
            f32(24, 128),
            bf16(8, HEADS, 16, HDIM),
            f32(8, 24, 128),
            bf16(8, HEADS, 16, HDIM),
            bf16(HEADS, HDIM, HDIM),
            bf16(16, HD),
            dma((items, 2, 3)),
            dma((items, 2, 3)),
            dma((items, 2)),
            dma((items, 4)),
            dma((items, 4)),
            dma((items, 5)),
            dma((items, 5)),
            dma((items, 3)),
            dma((items, 3)),
            dma((items,)),
            dma((items, 3)),
            dma((items, 2)),
            dma((LOCAL_HEADS, 2, 2)),
            dma((LOCAL_HEADS, 2, 2)),
            dma((LOCAL_HEADS, 3)),
            dma((LOCAL_HEADS, 3)),
            dma((LOCAL_HEADS,)),
            dma((8, 2)),
            dma((8, 2)),
            dma((8,)),
            dma((8,)),
            dma((5,)),
            dma((LOCAL_HEADS, 4)),
            dma((LOCAL_HEADS, 4)),
            dma((4,)),
            dma((4,)),
            dma((16,)),
            dma((1,)),
        ],
        compiler_params=pltpu.CompilerParams(
            collective_id=0, has_side_effects=True, vmem_limit_bytes=58 * 1024 * 1024
        ),
        name="span",
    )(*arguments)


def local(
    section_input,
    state_in,
    decay_table,
    head_rate,
    gates,
    query_gain,
    key_gain,
    out_gain,
    global_gain,
    cache_kv,
    cache_pos,
    span_start,
):
    section_output, state_out, global_new = span(
        section_input[0],
        state_in[0],
        decay_table,
        head_rate,
        jnp.transpose(gates, (2, 0, 1)),
        query_gain,
        key_gain,
        out_gain,
        global_gain,
        cache_kv,
        cache_pos[None],
        span_start[None],
    )
    return (section_output[None], state_out[None], global_new[None, None])


def solution(mesh):
    return jax.shard_map(
        local,
        mesh=mesh,
        in_specs=(
            P("section", "seq", None),
            P("section", None, None, None),
            P(),
            P("section", None),
            P("section", "seq", None),
            P("section", None),
            P("section", None),
            P("section", None),
            P(),
            P(("section", "seq"), None),
            P(("section", "seq")),
            P("section"),
        ),
        out_specs=(
            P("section", "seq", None),
            P("section", None, "seq", None),
            P("seq", "section", None, None),
        ),
        check_vma=False,
    )
```

```python
import jax
import jax.numpy as jnp
from jax import lax
from jax.experimental import pallas as pl
from jax.experimental.pallas import tpu as pltpu
from jax.sharding import PartitionSpec as P

MESH = pl.DeviceIdType.MESH
EPSILON = 1e-06
MASKED_SCORE = -1e30
LOG2E = 1.4426950408889634
HD = 2560
HEADS = 20
HDIM = 128
GROUP = 640
LOCAL_HEADS = 5
KEYS = 2048
TOKENS = 128
QBLOCK = 256
KCHUNK = 512
STEP = HDIM ** (-0.5) * LOG2E


def device_at(y, x, z, core):
    return (y * 4 + (x // 2) * 2 + core, z * 2 + x % 2)


def shifted(value, by):
    return lax.rem(value + by + 4, 4)


def remote(src, dst, send_sem, recv_sem, peer):
    return pltpu.make_async_remote_copy(
        src_ref=src,
        dst_ref=dst,
        send_sem=send_sem,
        recv_sem=recv_sem,
        device_id=peer,
        device_id_type=MESH,
    )


def span_kernel(
    x_hbm,
    state_ref,
    table_hbm,
    rate_hbm,
    gates_hbm,
    query_gain_hbm,
    key_gain_hbm,
    out_gain_hbm,
    global_hbm,
    kv_ref,
    positions_hbm,
    start_hbm,
    out_ref,
    state_out,
    global_out,
    x_ref,
    table_ref,
    start_ref,
    rate_ref,
    gates_ref,
    query_gain_ref,
    key_gain_ref,
    out_gain_ref,
    global_ref,
    positions_ref,
    i_local,
    queries,
    meta_ref,
    begin_ref,
    kvbuf,
    metabuf,
    beginbuf,
    qbuf,
    scores_even,
    scores_odd,
    top_even,
    top_odd,
    pos_ref,
    o_out,
    lse_out,
    o_in,
    lse_in,
    att_out,
    att_in,
    result,
    decays,
    decays_t,
    inside,
    kept,
    update_out,
    fade_out,
    update_in,
    fade_in,
    enter_out,
    enter_in,
    fresh,
    a_send,
    a_recv,
    a_local,
    b_send,
    b_recv,
    c_send,
    c_recv,
    qa_send,
    qa_recv,
    qa_local,
    qb_send,
    qb_recv,
    o_send,
    o_recv,
    t_send,
    t_recv,
    t_local,
    u_send,
    u_recv,
    e_send,
    e_recv,
    s_local,
    r_send,
    r_recv,
    w_send,
    w_recv,
    f_send,
    f_recv,
):
    section = lax.axis_index("section")
    seq = lax.axis_index("seq")
    y, core = section // 4, section % 2
    x, z = ((section // 2) % 2) * 2 + seq % 2, seq // 2
    is_self = section < 8
    is_cross = jnp.logical_not(is_self)
    is_root = section == 7
    sibling = device_at(y, x, z, 1 - core)
    other = device_at(y + 1 - 2 * (y % 2), x, z, core)
    partner = device_at(3 - y, x, z, core)
    after = (lax.rem(section + 1, 16), seq)
    before = (lax.rem(section + 15, 16), seq)

    fetches = [
        pltpu.make_async_copy(src, dst, i_local.at[at])
        for at, (src, dst) in enumerate(
            (
                (x_hbm, x_ref),
                (table_hbm, table_ref),
                (start_hbm, start_ref),
                (query_gain_hbm, query_gain_ref),
                (positions_hbm, positions_ref),
                (rate_hbm, rate_ref),
                (gates_hbm, gates_ref),
                (key_gain_hbm, key_gain_ref),
                (out_gain_hbm, out_gain_ref),
                (global_hbm, global_ref),
            )
        )
    ]
    for copy in fetches:
        copy.start()
    state_rows = pltpu.make_async_copy(
        state_ref.at[:, pl.ds(pl.multiple_of(seq * 16, 16), 16), :], kept, s_local.at[0]
    )
    state_rows.start()

    def seq_peer(at):
        to_z, to_x = shifted(z, at // 2), (x // 2) * 2 + lax.rem(x + at % 2, 2)
        return to_z * 2 + to_x % 2, device_at(y, to_x, to_z, core)

    peers = [sibling, other, partner]
    peers += [device_at(y, shifted(x, dx), z, core) for dx in (1, 3)]
    peers += [seq_peer(at)[1] for at in range(2, 8)]
    barrier = pltpu.get_barrier_semaphore()
    for peer in peers + [before]:
        pl.semaphore_signal(barrier, inc=1, device_id=peer, device_id_type=MESH)

    @pl.when(jnp.logical_not(is_root))
    def _():
        pl.semaphore_signal(barrier, inc=1, device_id=(7, seq), device_id_type=MESH)

    META = LOCAL_HEADS

    def is_meta(item):
        return isinstance(item, int) and item == META

    def kinds(item):
        return (0,) if is_meta(item) else (0, 1)

    def kv_source(item, kind, to_z):
        if is_meta(item):
            return meta_ref
        column = to_z * GROUP + item * HDIM + kind * HD
        return kv_ref.at[:, pl.ds(pl.multiple_of(column, HDIM), HDIM)]

    def kv_landing(item, kind, from_z):
        if is_meta(item):
            return metabuf.at[x * 8 + core * 4 + from_z]
        rows = pl.ds(pl.multiple_of(x * 512 + core * 256 + from_z * 64, 64), 64)
        return kvbuf.at[item, rows, pl.ds(kind * HDIM, HDIM)]

    def kv_spread_copies(item):
        return [
            remote(
                kv_source(item, kind, shifted(z, dz)),
                kv_landing(item, kind, z),
                a_send.at[item, kind, at],
                a_recv.at[item, kind, at],
                device_at(y, x, shifted(z, dz), core),
            )
            for kind in kinds(item)
            for at, dz in enumerate((2, 1, 3))
        ]

    def kv_spread(item):
        for copy in kv_spread_copies(item):
            copy.start()
        for kind in kinds(item):
            pltpu.make_async_copy(
                kv_source(item, kind, z), kv_landing(item, kind, z), a_local.at[item, kind]
            ).start()

    def kv_block(item, from_x, from_core, part):
        start, count = ((0, 4), (0, 2), (2, 2))[part]
        if is_meta(item):
            return metabuf.at[pl.ds(from_x * 8 + from_core * 4 + start, count)]
        rows = pl.ds(
            pl.multiple_of(from_x * 512 + from_core * 256 + start * 64, 64), count * 64
        )
        return kvbuf.at[item, rows]

    x_up, x_down, x_far = shifted(x, 1), shifted(x, 3), shifted(x, 2)
    up, down = device_at(y, x_up, z, core), device_at(y, x_down, z, core)

    def arrived(ref, sends, recvs, item, at, peer):
        remote(ref, ref, sends.at[item, at], recvs.at[item, at], peer).wait_recv()

    def kv_own(item):
        for kind in kinds(item):
            pltpu.make_async_copy(
                kv_source(item, kind, z), kv_landing(item, kind, z), a_local.at[item, kind]
            ).wait()
            for at, dz in enumerate((2, 1, 3)):
                landed = kv_landing(item, kind, shifted(z, -dz))
                remote(
                    landed, landed, a_send.at[item, kind, at], a_recv.at[item, kind, at], sibling
                ).wait_recv()
        for copy in kv_pushes(item)[0:3]:
            copy.start()

    def kv_pushes(item):
        here, below = kv_block(item, x, core, 0), kv_block(item, x_down, core, 0)
        above = kv_block(item, x_up, core, 0)

        def along(ref, at, peer):
            return remote(ref, ref, b_send.at[item, at], b_recv.at[item, at], peer)

        def across(ref, at):
            return remote(ref, ref, c_send.at[item, at], c_recv.at[item, at], sibling)

        return [
            along(here, 0, up),
            along(here, 1, down),
            across(here, 0),
            along(kv_block(item, x_down, core, 1), 2, up),
            across(below, 1),
            along(kv_block(item, x_up, core, 2), 3, down),
            across(above, 2),
            across(kv_block(item, x_far, core, 1), 3),
            across(kv_block(item, x_far, core, 2), 4),
        ]

    def kv_forward(item):
        pushes = kv_pushes(item)
        arrived(kv_block(item, x_down, core, 0), b_send, b_recv, item, 0, up)
        pushes[3].start()
        pushes[4].start()
        arrived(kv_block(item, x_up, core, 0), b_send, b_recv, item, 1, down)
        pushes[5].start()
        pushes[6].start()

    def kv_far(item):
        pushes = kv_pushes(item)
        for part in (1, 2):
            arrived(kv_block(item, x_far, core, part), b_send, b_recv, item, part + 1, up)
            pushes[part + 6].start()

    def kv_ready(item):
        for at, (from_x, part) in enumerate(
            ((x, 0), (x_down, 0), (x_up, 0), (x_far, 1), (x_far, 2))
        ):
            arrived(kv_block(item, from_x, 1 - core, part), c_send, c_recv, item, at, sibling)

    own_j = jnp.where(is_self, 1 - y, y - 2)

    def q_source(item, to_z):
        if is_meta(item):
            return begin_ref
        return queries.at[:, pl.ds(pl.multiple_of(to_z * GROUP + item * HDIM, HDIM), HDIM)]

    def q_landing(item, from_z):
        if is_meta(item):
            return beginbuf.at[own_j * 4 + from_z]
        rows = pl.ds(pl.multiple_of(own_j * 512 + from_z * TOKENS, TOKENS), TOKENS)
        return qbuf.at[item, rows]

    def q_own_copy(item):
        return pltpu.make_async_copy(q_source(item, z), q_landing(item, z), qa_local.at[item])

    def q_spread_copies(item):
        return [
            remote(
                q_source(item, shifted(z, dz)),
                q_landing(item, z),
                qa_send.at[item, at],
                qa_recv.at[item, at],
                device_at(y, x, shifted(z, dz), core),
            )
            for at, dz in enumerate((2, 1, 3))
        ]

    def q_spread(item):
        for copy in q_spread_copies(item):
            copy.start()
        q_own_copy(item).start()

    def q_block(item, j):
        if is_meta(item):
            return beginbuf.at[pl.ds(j * 4, 4)]
        return qbuf.at[item, pl.ds(pl.multiple_of(j * 512, 512), 512)]

    def q_push(item, at):
        peer = (other, partner, other)[at]
        return remote(
            q_block(item, own_j),
            q_block(item, own_j),
            qb_send.at[item, at],
            qb_recv.at[item, (0, 0, 1)[at]],
            peer,
        )

    def q_own(item):
        q_own_copy(item).wait()
        for at, dz in enumerate((2, 1, 3)):
            arrived(q_landing(item, shifted(z, -dz)), qa_send, qa_recv, item, at, sibling)
        q_push(item, 1).start()
        q_push(item, 0).start()

    def q_relay(item):
        arrived(q_block(item, own_j), qb_send, qb_recv, item, 0, partner)
        q_push(item, 2).start()

    def q_ready(item):
        @pl.when(is_cross)
        def _():
            arrived(q_block(item, 1 - own_j), qb_send, qb_recv, item, 0, other)

        @pl.when(is_self)
        def _():
            arrived(q_block(item, 1 - own_j), qb_send, qb_recv, item, 1, other)

    lanes = lax.broadcasted_iota(jnp.int32, (128, 128), 1)
    sublanes = lax.broadcasted_iota(jnp.int32, (128, 128), 0)
    causal = sublanes >= lanes
    diagonal = sublanes == lanes

    def inverse_rms(values):
        return lax.rsqrt(jnp.mean(values * values, axis=1, keepdims=True) + EPSILON)

    def decay_column(head):
        return jnp.sum(jnp.where(lanes == head, decays[...], 0.0), axis=1, keepdims=True)

    def decay_setup():
        decays[...] = jnp.ones((128, 128), jnp.float32)
        decays_t[...] = jnp.ones((128, 128), jnp.float32)
        for head in range(HEADS):
            decays[head : head + 1, :] = gates_ref[head]
            picked = table_ref[rate_ref[0, head]]
            decays_t[head : head + 1, :] = jnp.full((1, 128), picked, jnp.float32)
        turned = jnp.dot(
            jnp.log(decays_t[...]) + jnp.log(decays[...]),
            jnp.where(sublanes <= lanes, 1.0, 0.0),
            precision=lax.Precision.HIGHEST,
            preferred_element_type=jnp.float32,
        )
        decays_t[...] = turned
        decays[...] = jnp.transpose(turned)
        fade_out[...] = jnp.broadcast_to(jnp.exp(turned[:, 127:128])[0:24], (24, 128))

    def retain(first, last):
        scale = inverse_rms(x_ref[...].astype(jnp.float32))

        def one(head, carry):
            columns = pl.ds(pl.multiple_of(head * HDIM, HDIM), HDIM)
            values = x_ref[:, columns]
            normed = values.astype(jnp.float32) * scale
            query = (normed * query_gain_ref[:, columns]).astype(jnp.bfloat16)
            key_rows = (normed * key_gain_ref[:, columns]).astype(jnp.bfloat16)
            queries[:, columns] = query
            products = lax.dot_general(
                query, key_rows, (((1,), (1,)), ((), ())), preferred_element_type=jnp.float32
            )
            column = decay_column(head)
            row = decays_t[pl.ds(head, 1), :]
            weights = jnp.where(
                causal, products * jnp.exp(jnp.where(causal, column - row, 0.0)), 0.0
            ).astype(jnp.bfloat16)
            inside[:, columns] = jnp.dot(weights, values, preferred_element_type=jnp.float32)
            fading = jnp.exp(row[:, 127:128] - column)
            faded = (key_rows.astype(jnp.float32) * fading).astype(jnp.bfloat16)
            update_out[pl.ds(head, 1)] = lax.dot_general(
                faded, values, (((0,), (0,)), ((), ())), preferred_element_type=jnp.float32
            ).astype(jnp.bfloat16)[None]
            return carry

        lax.fori_loop(first, last, one, 0, unroll=4 if (last - first) % 4 == 0 else 5)

    def update_copies():
        copies = []
        for at in range(8):
            to_seq, peer = seq_peer(at)
            rows = pl.ds(pl.multiple_of(to_seq * 16, 16), 16)
            pairs = (
                (update_out.at[:, rows, :], update_in.at[seq]),
                (fade_out, fade_in.at[seq]),
            )
            for kind, (src, dst) in enumerate(pairs):
                if at == 0:
                    copies.append(pltpu.make_async_copy(src, dst, s_local.at[1 + kind]))
                else:
                    copies.append(
                        remote(src, dst, u_send.at[at, kind], u_recv.at[at, kind], peer)
                    )
        return copies

    def enter_copies():
        copies = []
        for at in range(8):
            to_seq, peer = seq_peer(at)
            dst = enter_in.at[:, pl.ds(pl.multiple_of(seq * 16, 16), 16), :]
            if at == 0:
                copies.append(pltpu.make_async_copy(enter_out.at[to_seq], dst, s_local.at[3]))
            else:
                copies.append(
                    remote(enter_out.at[to_seq], dst, e_send.at[at], e_recv.at[at], peer)
                )
        return copies

    def scan():
        def one(head, carry):
            now = kept[pl.ds(head, 1)][0]
            for at in range(8):
                enter_out[at, pl.ds(head, 1)] = now.astype(jnp.bfloat16)[None]
                fade = fade_in[at, pl.ds(head, 1), :]
                now = fade * now + update_in[at, pl.ds(head, 1)][0].astype(jnp.float32)
            state_out[pl.ds(head, 1)] = now[None]
            return carry

        lax.fori_loop(0, HEADS, one, 0)

    def mix(first, last):
        def one(head, carry):
            columns = pl.ds(pl.multiple_of(head * HDIM, HDIM), HDIM)
            carried = jnp.dot(
                queries[:, columns], enter_in[pl.ds(head, 1)][0], preferred_element_type=jnp.float32
            )
            retained = inside[:, columns] + jnp.exp(decay_column(head)) * carried
            mixed = retained * inverse_rms(retained)
            result[:, columns] = (
                x_ref[:, columns].astype(jnp.float32) + mixed * out_gain_ref[:, columns]
            ).astype(jnp.bfloat16)
            return carry

        lax.fori_loop(first, last, one, 0, unroll=4 if (last - first) % 4 == 0 else 5)

    def self_result(group):
        columns = pl.ds(group * GROUP, GROUP)
        return remote(
            result.at[:, columns], out_ref.at[:, columns], w_send.at[group], w_recv.at[group], after
        )

    def fresh_rows(to):
        return result.at[pl.ds(pl.multiple_of((to // 2) * 16, 16), 16)]

    own_fresh = pltpu.make_async_copy(fresh_rows(section), fresh, s_local.at[4])

    def fresh_copy(by):
        to = lax.rem(section + by, 16)
        return remote(fresh_rows(to), fresh, f_send.at[by], f_recv.at[0], (to, seq))

    first_j = 1 - own_j

    def place_setup():
        lane = lax.broadcasted_iota(jnp.int32, (1, 128), 1)
        for pair in range(16):
            pos_ref[:, pair * 128 : (pair + 1) * 128] = jnp.where(
                lane < 64,
                metabuf[2 * pair, 0:1, :],
                pltpu.roll(metabuf[2 * pair + 1, 0:1, :], 64, 1),
            )

    def tree(combine, values):
        while len(values) > 1:
            values = [
                combine(values[at], values[at + 1]) if at + 1 < len(values) else values[at]
                for at in range(0, len(values), 2)
            ]
        return values[0]

    def block_of(step):
        item, block = step // 4, step % 4
        return item, jnp.where(block < 2, first_j, own_j), block % 2

    def block_rows(j, at):
        return pl.ds(pl.multiple_of(j * 512 + at * QBLOCK, QBLOCK), QBLOCK)

    def stage(current, previous, even):
        fill, fill_top = (scores_even, top_even) if even else (scores_odd, top_odd)
        drain, drain_top = (scores_odd, top_odd) if even else (scores_even, top_even)
        if current is not None:
            item, j, at = block_of(current)
            row = lax.broadcasted_iota(jnp.int32, (QBLOCK, 128), 0)
            index = (at * 2 + row // TOKENS) * 256 + (x % 2) * TOKENS + row % TOKENS
            query = qbuf[item, block_rows(j, at), :]
            places = index + beginbuf[j * 4][0:1, :]
            highest = jnp.full((QBLOCK, 128), MASKED_SCORE, jnp.float32)
        if previous is not None:
            item_p, j_p, at_p = block_of(previous)
            top = drain_top[...][:, 0:1]
            totals = jnp.zeros((QBLOCK, 128), jnp.float32)
            pieces = jnp.zeros((QBLOCK, HDIM), jnp.float32)
        for chunk in range(KEYS // KCHUNK):
            here = slice(chunk * KCHUNK, (chunk + 1) * KCHUNK)
            parts = [
                slice(chunk * KCHUNK + part * 128, chunk * KCHUNK + (part + 1) * 128)
                for part in range(KCHUNK // 128)
            ]
            if current is not None:
                scores = lax.dot_general(
                    query,
                    kvbuf[item, here, 0:HDIM],
                    (((1,), (1,)), ((), ())),
                    preferred_element_type=jnp.float32,
                )
            if previous is not None:
                likely = [jnp.exp2((drain[:, part] - top) * STEP) for part in parts]
                totals += tree(jnp.add, likely)
                pieces += jnp.dot(
                    jnp.concatenate([value.astype(jnp.bfloat16) for value in likely], axis=1),
                    kvbuf[item_p, here, HDIM : 2 * HDIM],
                    preferred_element_type=jnp.float32,
                )
            if current is not None:
                masked = []
                for at_part, part in enumerate(parts):
                    piece = jnp.where(
                        pos_ref[:, part] <= places,
                        scores[:, at_part * 128 : (at_part + 1) * 128],
                        MASKED_SCORE,
                    )
                    fill[:, part] = piece
                    masked.append(piece)
                highest = jnp.maximum(highest, tree(jnp.maximum, masked))
        if current is not None:
            fill_top[...] = jnp.broadcast_to(
                jnp.max(highest, axis=1, keepdims=True), (QBLOCK, 128)
            )
        if previous is not None:
            total = jnp.sum(totals, axis=1, keepdims=True)
            o_out[item_p, block_rows(j_p, at_p), :] = (pieces / total).astype(jnp.bfloat16)
            lse = top * HDIM ** (-0.5) + jnp.log(total)
            wide = lax.broadcasted_iota(jnp.int32, (QBLOCK, QBLOCK), 0) == (
                lax.broadcasted_iota(jnp.int32, (QBLOCK, QBLOCK), 1)
            )
            flat = jnp.sum(jnp.where(wide, lse, 0.0), axis=0, keepdims=True)
            lse_out[item_p, j_p, pl.ds(at_p * 2, 1), :] = flat[:, 0:128]
            lse_out[item_p, j_p, pl.ds(at_p * 2 + 1, 1), :] = flat[:, 128:256]

    def pieces_of(item, j):
        return o_out.at[item, pl.ds(pl.multiple_of(j * 512, 512), 512)], lse_out.at[item, j]

    def piece_copies(item, at):
        peer, j = ((other, first_j), (partner, own_j))[at]
        o_src, lse_src = pieces_of(item, j)
        return [
            remote(o_src, o_in.at[item, at], o_send.at[item, at, 0], o_recv.at[item, at, 0], peer),
            remote(
                lse_src, lse_in.at[item, at], o_send.at[item, at, 1], o_recv.at[item, at, 1], peer
            ),
        ]

    def shares_of(tiles):
        overall = tiles[0]
        for tile in tiles[1:]:
            overall = jnp.maximum(overall, tile)
        shares = [jnp.exp(tile - overall) for tile in tiles]
        whole = shares[0]
        for share in shares[1:]:
            whole = whole + share
        return [share / whole for share in shares], overall + jnp.log(whole)

    def weighted(shares, parts, group):
        total = jnp.zeros((TOKENS, HDIM), jnp.float32)
        for share, part in zip(shares, parts):
            column = jnp.sum(
                jnp.where(diagonal, share[group : group + 1, :], 0.0), axis=1, keepdims=True
            )
            total += column * part.astype(jnp.float32)
        return total.astype(jnp.bfloat16)

    def own_rows(group):
        return pl.ds(pl.multiple_of(own_j * 512 + group * TOKENS, TOKENS), TOKENS)

    def merge_self(item):
        for copy in piece_copies(item, 0):
            copy.wait_recv()
        shares, lse = shares_of([lse_out[item, own_j], lse_in[item, 0]])
        for group in range(4):
            here = slice(group * TOKENS, (group + 1) * TOKENS)
            o_out[item, own_rows(group), :] = weighted(
                shares, (o_out[item, own_rows(group), :], o_in[item, 0, here, :]), group
            )
        lse_out[item, own_j] = lse
        for copy in piece_copies(item, 1):
            copy.start()

    def att_copies(item):
        copies = [
            pltpu.make_async_copy(
                att_out.at[item, pl.ds(pl.multiple_of(z * TOKENS, TOKENS), TOKENS)],
                att_in.at[item, z],
                t_local.at[item],
            )
        ]
        for at, dz in enumerate((2, 1, 3)):
            to_z = shifted(z, dz)
            copies.append(
                remote(
                    att_out.at[item, pl.ds(pl.multiple_of(to_z * TOKENS, TOKENS), TOKENS)],
                    att_in.at[item, z],
                    t_send.at[item, at],
                    t_recv.at[item, at],
                    device_at(y, x, to_z, core),
                )
            )
        return copies

    def merge_cross(item):
        for at in range(2):
            for copy in piece_copies(item, at):
                copy.wait_recv()
        shares, _ = shares_of([lse_out[item, own_j], lse_in[item, 0], lse_in[item, 1]])
        for group in range(4):
            here = slice(group * TOKENS, (group + 1) * TOKENS)
            att_out[item, here, :] = weighted(
                shares,
                (
                    o_out[item, own_rows(group), :],
                    o_in[item, 0, here, :],
                    o_in[item, 1, here, :],
                ),
                group,
            )
        for copy in att_copies(item):
            copy.start()

    def head_columns(item, group):
        return pl.ds(pl.multiple_of(group * GROUP + item * HDIM, HDIM), HDIM)

    def att_result(item, group):
        columns = head_columns(item, group)
        return remote(
            result.at[:, columns],
            out_ref.at[:, columns],
            r_send.at[item, group],
            r_recv.at[item, group],
            after,
        )

    def finish(item):
        for copy in att_copies(item):
            copy.wait()
        for group in range(4):
            here = head_columns(item, group)
            result[:, here] = (
                x_ref[:, here].astype(jnp.float32)
                + att_in[item, group].astype(jnp.float32) * out_gain_ref[:, here]
            ).astype(jnp.bfloat16)
            att_result(item, group).start()

    pl.semaphore_wait(barrier, len(peers) + 1 + jnp.where(is_root, 15, 0))
    kv_spread(0)
    for copy in fetches:
        copy.wait()
    meta_ref[0:1, 0:64] = positions_ref[...]
    begin_ref[...] = jnp.full((8, 128), start_ref[0, 0], jnp.int32)
    kv_spread(META)

    def on_self(*steps):
        @pl.when(is_self)
        def _():
            for step in steps:
                step()

    def on_cross(*steps):
        @pl.when(is_cross)
        def _():
            for step in steps:
                step()

    def send_updates():
        for copy in update_copies():
            copy.start()

    def enter():
        for copy in update_copies():
            copy.wait()
        scan()
        for copy in enter_copies():
            copy.start()

    def keep_state():
        state_rows.wait()
        on_cross(lambda: state_out.__setitem__(Ellipsis, kept[...]))
        on_self(enter)

    def self_mix():
        for copy in enter_copies():
            copy.wait()
        for group in range(4):
            mix(group * LOCAL_HEADS, (group + 1) * LOCAL_HEADS)
            self_result(group).start()

    def send_fresh():
        @pl.when(is_root)
        def _():
            own_fresh.start()
            for by in range(1, 16):
                fresh_copy(by).start()

    def own(item):
        kv_own(item)
        on_cross(lambda: q_own(item))

    def make_queries():
        rows = x_ref[...].astype(jnp.float32)
        queries[...] = (rows * inverse_rms(rows) * query_gain_ref[...]).astype(jnp.bfloat16)
        q_spread(META)
        q_spread(0)

    def spread(item):
        kv_spread(item)
        on_cross(lambda: q_spread(item))

    on_cross(make_queries)
    spread(1)
    on_self(decay_setup, lambda: retain(0, 8))
    own(META)
    own(0)
    spread(2)
    on_self(lambda: retain(8, 16))
    own(1)
    spread(3)
    kv_forward(META)
    kv_forward(0)
    on_self(lambda: retain(16, HEADS))
    own(2)
    spread(4)
    on_self(lambda: q_relay(META), lambda: q_relay(0))
    kv_forward(1)
    kv_far(META)
    kv_far(0)
    own(3)
    on_self(lambda: q_relay(1))
    kv_forward(2)
    kv_far(1)
    q_ready(META)
    kv_ready(META)
    place_setup()

    hooks = {
        15: (keep_state,),
        0: (lambda: own(4), lambda: on_self(lambda: q_relay(2))),
        1: (lambda: kv_forward(3),),
        2: (lambda: kv_far(2),),
        3: (lambda: on_self(lambda: q_relay(3)),),
        4: (lambda: kv_forward(4),),
        5: (lambda: kv_far(3),),
        7: (lambda: on_self(lambda: q_relay(4)),),
        8: (lambda: kv_far(4), lambda: on_self(send_updates)),
        12: (lambda: on_cross(lambda: merge_cross(0)),),
        16: (lambda: on_cross(lambda: finish(0), lambda: merge_cross(1)),),
    }

    def after_block(step):
        item, block = step // 4, step % 4

        @pl.when(block == 1)
        def _():
            for copy in piece_copies(item, 0):
                copy.start()

        for due, steps in hooks.items():

            @pl.when(step == due)
            def _():
                for one in steps:
                    one()

        @pl.when(jnp.logical_and(is_self, jnp.logical_and(block == 1, item >= 1)))
        def _():
            merge_self(item - 1)

    q_ready(0)
    kv_ready(0)
    stage(0, None, True)

    def two_blocks(pair, carry):
        step = 2 * pair
        stage(step + 1, step, False)
        after_block(step)

        @pl.when(pair % 2 == 1)
        def _():
            q_ready((step + 2) // 4)
            kv_ready((step + 2) // 4)

        stage(step + 2, step + 1, True)
        after_block(step + 1)
        return carry

    last = 4 * LOCAL_HEADS - 1
    lax.fori_loop(0, (last - 1) // 2, two_blocks, 0)
    stage(last, last - 1, False)
    after_block(jnp.int32(last - 1))
    stage(None, last, True)
    on_self(lambda: merge_self(4))
    on_self(self_mix)
    send_fresh()
    on_cross(
        lambda: finish(1),
        lambda: merge_cross(2),
        lambda: merge_cross(3),
        lambda: finish(2),
        lambda: finish(3),
        lambda: merge_cross(4),
        lambda: finish(4),
    )

    @pl.when(is_root)
    def _():
        own_fresh.wait()

    @pl.when(jnp.logical_not(is_root))
    def _():
        fresh_copy(1).wait_recv()

    both = fresh[...].astype(jnp.float32)
    new_rows = jnp.where(core == 0, both[0:8], both[8:16])
    new_rows = new_rows * inverse_rms(new_rows)
    global_out[:, 0:HD] = (new_rows * global_ref[0:1, :]).astype(jnp.bfloat16)
    global_out[:, HD : 2 * HD] = (new_rows * global_ref[1:2, :]).astype(jnp.bfloat16)

    from_self = jnp.logical_and(section >= 1, section <= 8)

    @pl.when(from_self)
    def _():
        for group in range(4):
            self_result(group).wait_recv()

    @pl.when(jnp.logical_not(from_self))
    def _():
        for item in range(LOCAL_HEADS):
            for group in range(4):
                att_result(item, group).wait_recv()

    for item in range(LOCAL_HEADS + 1):
        for copy in kv_spread_copies(item) + kv_pushes(item):
            copy.wait_send()
    for item in range(LOCAL_HEADS):
        for copy in piece_copies(item, 0):
            copy.wait_send()

    @pl.when(is_cross)
    def _():
        for item in range(LOCAL_HEADS + 1):
            for copy in q_spread_copies(item):
                copy.wait_send()
            q_push(item, 0).wait_send()
            q_push(item, 1).wait_send()
        for item in range(LOCAL_HEADS):
            for group in range(4):
                att_result(item, group).wait_send()

    @pl.when(is_self)
    def _():
        for item in range(LOCAL_HEADS + 1):
            q_push(item, 2).wait_send()
        for item in range(LOCAL_HEADS):
            for copy in piece_copies(item, 1):
                copy.wait_send()
        for group in range(4):
            self_result(group).wait_send()

    @pl.when(is_root)
    def _():
        for by in range(1, 16):
            fresh_copy(by).wait_send()


def span(*arguments):
    vmem = pl.BlockSpec(memory_space=pltpu.VMEM)
    hbm = pl.BlockSpec(memory_space=pl.ANY)
    dma = pltpu.SemaphoreType.DMA
    items = LOCAL_HEADS + 1

    def bf16(*shape):
        return pltpu.VMEM(shape, jnp.bfloat16)

    def f32(*shape):
        return pltpu.VMEM(shape, jnp.float32)

    def i32(*shape):
        return pltpu.VMEM(shape, jnp.int32)

    return pl.pallas_call(
        span_kernel,
        out_shape=(
            jax.ShapeDtypeStruct((TOKENS, HD), jnp.bfloat16),
            jax.ShapeDtypeStruct((HEADS, 16, HDIM), jnp.float32),
            jax.ShapeDtypeStruct((8, 2 * HD), jnp.bfloat16),
        ),
        in_specs=[hbm] * 12,
        out_specs=(vmem, vmem, vmem),
        scratch_shapes=[
            bf16(TOKENS, HD),
            pltpu.SMEM((16,), jnp.float32),
            pltpu.SMEM((1, 1), jnp.int32),
            pltpu.SMEM((1, HEADS), jnp.int32),
            f32(HEADS, 1, TOKENS),
            f32(1, HD),
            f32(1, HD),
            f32(1, HD),
            f32(2, HD),
            i32(1, 64),
            dma((10,)),
            bf16(TOKENS, HD),
            i32(8, 128),
            i32(8, 128),
            bf16(LOCAL_HEADS, KEYS, 2 * HDIM),
            i32(32, 8, 128),
            i32(8, 8, 128),
            bf16(LOCAL_HEADS, 1024, HDIM),
            f32(QBLOCK, KEYS),
            f32(QBLOCK, KEYS),
            f32(QBLOCK, 128),
            f32(QBLOCK, 128),
            i32(1, KEYS),
            bf16(LOCAL_HEADS, 1024, HDIM),
            f32(LOCAL_HEADS, 2, 8, 128),
            bf16(LOCAL_HEADS, 2, 512, HDIM),
            f32(LOCAL_HEADS, 2, 8, 128),
            bf16(LOCAL_HEADS, 512, HDIM),
            bf16(LOCAL_HEADS, 4, TOKENS, HDIM),
            bf16(TOKENS, HD),
            f32(128, 128),
            f32(128, 128),
            f32(TOKENS, HD),
            f32(HEADS, 16, HDIM),
            bf16(HEADS, HDIM, HDIM),
            f32(24, 128),
            bf16(8, HEADS, 16, HDIM),
            f32(8, 24, 128),
            bf16(8, HEADS, 16, HDIM),
            bf16(HEADS, HDIM, HDIM),
            bf16(16, HD),
            dma((items, 2, 3)),
            dma((items, 2, 3)),
            dma((items, 2)),
            dma((items, 4)),
            dma((items, 4)),
            dma((items, 5)),
            dma((items, 5)),
            dma((items, 3)),
            dma((items, 3)),
            dma((items,)),
            dma((items, 3)),
            dma((items, 2)),
            dma((LOCAL_HEADS, 2, 2)),
            dma((LOCAL_HEADS, 2, 2)),
            dma((LOCAL_HEADS, 3)),
            dma((LOCAL_HEADS, 3)),
            dma((LOCAL_HEADS,)),
            dma((8, 2)),
            dma((8, 2)),
            dma((8,)),
            dma((8,)),
            dma((5,)),
            dma((LOCAL_HEADS, 4)),
            dma((LOCAL_HEADS, 4)),
            dma((4,)),
            dma((4,)),
            dma((16,)),
            dma((1,)),
        ],
        compiler_params=pltpu.CompilerParams(
            collective_id=0, has_side_effects=True, vmem_limit_bytes=58 * 1024 * 1024
        ),
        name="span",
    )(*arguments)


def local(
    section_input,
    state_in,
    decay_table,
    head_rate,
    gates,
    query_gain,
    key_gain,
    out_gain,
    global_gain,
    cache_kv,
    cache_pos,
    span_start,
):
    section_output, state_out, global_new = span(
        section_input[0],
        state_in[0],
        decay_table,
        head_rate,
        jnp.transpose(gates, (2, 0, 1)),
        query_gain,
        key_gain,
        out_gain,
        global_gain,
        cache_kv,
        cache_pos[None],
        span_start[None],
    )
    return (section_output[None], state_out[None], global_new[None, None])


def solution(mesh):
    return jax.shard_map(
        local,
        mesh=mesh,
        in_specs=(
            P("section", "seq", None),
            P("section", None, None, None),
            P(),
            P("section", None),
            P("section", "seq", None),
            P("section", None),
            P("section", None),
            P("section", None),
            P(),
            P(("section", "seq"), None),
            P(("section", "seq")),
            P("section"),
        ),
        out_specs=(
            P("section", "seq", None),
            P("section", None, "seq", None),
            P("seq", "section", None, None),
        ),
        check_vma=False,
    )
```

```python
import jax
import jax.numpy as jnp
from jax import lax
from jax.experimental import pallas as pl
from jax.experimental.pallas import tpu as pltpu
from jax.sharding import PartitionSpec as P

MESH = pl.DeviceIdType.MESH
EPSILON = 1e-06
MASKED_SCORE = -1e30
LOG2E = 1.4426950408889634
HD = 2560
HEADS = 20
HDIM = 128
GROUP = 640
LOCAL_HEADS = 5
KEYS = 2048
TOKENS = 128
QBLOCK = 256
KCHUNK = 512
STEP = HDIM ** (-0.5) * LOG2E


def device_at(y, x, z, core):
    return (y * 4 + (x // 2) * 2 + core, z * 2 + x % 2)


def shifted(value, by):
    return lax.rem(value + by + 4, 4)


def remote(src, dst, send_sem, recv_sem, peer):
    return pltpu.make_async_remote_copy(
        src_ref=src,
        dst_ref=dst,
        send_sem=send_sem,
        recv_sem=recv_sem,
        device_id=peer,
        device_id_type=MESH,
    )


def span_kernel(
    x_hbm,
    state_ref,
    table_hbm,
    rate_hbm,
    gates_hbm,
    query_gain_hbm,
    key_gain_hbm,
    out_gain_hbm,
    global_hbm,
    kv_ref,
    positions_hbm,
    start_hbm,
    out_ref,
    state_out,
    global_out,
    x_ref,
    table_ref,
    start_ref,
    rate_ref,
    gates_ref,
    query_gain_ref,
    key_gain_ref,
    out_gain_ref,
    global_ref,
    positions_ref,
    i_local,
    queries,
    meta_ref,
    begin_ref,
    kvbuf,
    metabuf,
    beginbuf,
    qbuf,
    scores_even,
    scores_odd,
    top_even,
    top_odd,
    pos_ref,
    o_out,
    lse_out,
    o_in,
    lse_in,
    att_out,
    att_in,
    result,
    decays,
    decays_t,
    inside,
    kept,
    update_out,
    fade_out,
    update_in,
    fade_in,
    enter_out,
    enter_in,
    fresh,
    a_send,
    a_recv,
    a_local,
    b_send,
    b_recv,
    c_send,
    c_recv,
    qa_send,
    qa_recv,
    qa_local,
    qb_send,
    qb_recv,
    o_send,
    o_recv,
    t_send,
    t_recv,
    t_local,
    u_send,
    u_recv,
    e_send,
    e_recv,
    s_local,
    r_send,
    r_recv,
    w_send,
    w_recv,
    f_send,
    f_recv,
):
    section = lax.axis_index("section")
    seq = lax.axis_index("seq")
    y, core = section // 4, section % 2
    x, z = ((section // 2) % 2) * 2 + seq % 2, seq // 2
    is_self = section < 8
    is_cross = jnp.logical_not(is_self)
    is_root = section == 7
    sibling = device_at(y, x, z, 1 - core)
    other = device_at(y + 1 - 2 * (y % 2), x, z, core)
    partner = device_at(3 - y, x, z, core)
    after = (lax.rem(section + 1, 16), seq)
    before = (lax.rem(section + 15, 16), seq)

    fetches = [
        pltpu.make_async_copy(src, dst, i_local.at[at])
        for at, (src, dst) in enumerate(
            (
                (x_hbm, x_ref),
                (table_hbm, table_ref),
                (start_hbm, start_ref),
                (query_gain_hbm, query_gain_ref),
                (positions_hbm, positions_ref),
                (rate_hbm, rate_ref),
                (gates_hbm, gates_ref),
                (key_gain_hbm, key_gain_ref),
                (out_gain_hbm, out_gain_ref),
                (global_hbm, global_ref),
            )
        )
    ]
    for copy in fetches:
        copy.start()
    state_rows = pltpu.make_async_copy(
        state_ref.at[:, pl.ds(pl.multiple_of(seq * 16, 16), 16), :], kept, s_local.at[0]
    )
    state_rows.start()

    def seq_peer(at):
        to_z, to_x = shifted(z, at // 2), (x // 2) * 2 + lax.rem(x + at % 2, 2)
        return to_z * 2 + to_x % 2, device_at(y, to_x, to_z, core)

    peers = [sibling, other, partner]
    peers += [device_at(y, shifted(x, dx), z, core) for dx in (1, 3)]
    peers += [seq_peer(at)[1] for at in range(2, 8)]
    barrier = pltpu.get_barrier_semaphore()
    for peer in peers + [before]:
        pl.semaphore_signal(barrier, inc=1, device_id=peer, device_id_type=MESH)

    @pl.when(jnp.logical_not(is_root))
    def _():
        pl.semaphore_signal(barrier, inc=1, device_id=(7, seq), device_id_type=MESH)

    META = LOCAL_HEADS

    def is_meta(item):
        return isinstance(item, int) and item == META

    def kinds(item):
        return (0,) if is_meta(item) else (0, 1)

    def kv_source(item, kind, to_z):
        if is_meta(item):
            return meta_ref
        column = to_z * GROUP + item * HDIM + kind * HD
        return kv_ref.at[:, pl.ds(pl.multiple_of(column, HDIM), HDIM)]

    def kv_landing(item, kind, from_z):
        if is_meta(item):
            return metabuf.at[x * 8 + core * 4 + from_z]
        rows = pl.ds(pl.multiple_of(x * 512 + core * 256 + from_z * 64, 64), 64)
        return kvbuf.at[item, rows, pl.ds(kind * HDIM, HDIM)]

    def kv_spread_copies(item):
        return [
            remote(
                kv_source(item, kind, shifted(z, dz)),
                kv_landing(item, kind, z),
                a_send.at[item, kind, at],
                a_recv.at[item, kind, at],
                device_at(y, x, shifted(z, dz), core),
            )
            for kind in kinds(item)
            for at, dz in enumerate((2, 1, 3))
        ]

    def kv_spread(item):
        for copy in kv_spread_copies(item):
            copy.start()
        for kind in kinds(item):
            pltpu.make_async_copy(
                kv_source(item, kind, z), kv_landing(item, kind, z), a_local.at[item, kind]
            ).start()

    def kv_block(item, from_x, from_core, part):
        start, count = ((0, 4), (0, 2), (2, 2))[part]
        if is_meta(item):
            return metabuf.at[pl.ds(from_x * 8 + from_core * 4 + start, count)]
        rows = pl.ds(
            pl.multiple_of(from_x * 512 + from_core * 256 + start * 64, 64), count * 64
        )
        return kvbuf.at[item, rows]

    x_up, x_down, x_far = shifted(x, 1), shifted(x, 3), shifted(x, 2)
    up, down = device_at(y, x_up, z, core), device_at(y, x_down, z, core)

    def arrived(ref, sends, recvs, item, at, peer):
        remote(ref, ref, sends.at[item, at], recvs.at[item, at], peer).wait_recv()

    def kv_own(item):
        for kind in kinds(item):
            pltpu.make_async_copy(
                kv_source(item, kind, z), kv_landing(item, kind, z), a_local.at[item, kind]
            ).wait()
            for at, dz in enumerate((2, 1, 3)):
                landed = kv_landing(item, kind, shifted(z, -dz))
                remote(
                    landed, landed, a_send.at[item, kind, at], a_recv.at[item, kind, at], sibling
                ).wait_recv()
        for copy in kv_pushes(item)[0:3]:
            copy.start()

    def kv_pushes(item):
        here, below = kv_block(item, x, core, 0), kv_block(item, x_down, core, 0)
        above = kv_block(item, x_up, core, 0)

        def along(ref, at, peer):
            return remote(ref, ref, b_send.at[item, at], b_recv.at[item, at], peer)

        def across(ref, at):
            return remote(ref, ref, c_send.at[item, at], c_recv.at[item, at], sibling)

        return [
            along(here, 0, up),
            along(here, 1, down),
            across(here, 0),
            along(kv_block(item, x_down, core, 1), 2, up),
            across(below, 1),
            along(kv_block(item, x_up, core, 2), 3, down),
            across(above, 2),
            across(kv_block(item, x_far, core, 1), 3),
            across(kv_block(item, x_far, core, 2), 4),
        ]

    def kv_forward(item):
        pushes = kv_pushes(item)
        arrived(kv_block(item, x_down, core, 0), b_send, b_recv, item, 0, up)
        pushes[3].start()
        pushes[4].start()
        arrived(kv_block(item, x_up, core, 0), b_send, b_recv, item, 1, down)
        pushes[5].start()
        pushes[6].start()

    def kv_far(item):
        pushes = kv_pushes(item)
        for part in (1, 2):
            arrived(kv_block(item, x_far, core, part), b_send, b_recv, item, part + 1, up)
            pushes[part + 6].start()

    def kv_ready(item):
        for at, (from_x, part) in enumerate(
            ((x, 0), (x_down, 0), (x_up, 0), (x_far, 1), (x_far, 2))
        ):
            arrived(kv_block(item, from_x, 1 - core, part), c_send, c_recv, item, at, sibling)

    own_j = jnp.where(is_self, 1 - y, y - 2)

    def q_source(item, to_z):
        if is_meta(item):
            return begin_ref
        return queries.at[:, pl.ds(pl.multiple_of(to_z * GROUP + item * HDIM, HDIM), HDIM)]

    def q_landing(item, from_z):
        if is_meta(item):
            return beginbuf.at[own_j * 4 + from_z]
        rows = pl.ds(pl.multiple_of(own_j * 512 + from_z * TOKENS, TOKENS), TOKENS)
        return qbuf.at[item, rows]

    def q_own_copy(item):
        return pltpu.make_async_copy(q_source(item, z), q_landing(item, z), qa_local.at[item])

    def q_spread_copies(item):
        return [
            remote(
                q_source(item, shifted(z, dz)),
                q_landing(item, z),
                qa_send.at[item, at],
                qa_recv.at[item, at],
                device_at(y, x, shifted(z, dz), core),
            )
            for at, dz in enumerate((2, 1, 3))
        ]

    def q_spread(item):
        for copy in q_spread_copies(item):
            copy.start()
        q_own_copy(item).start()

    def q_block(item, j):
        if is_meta(item):
            return beginbuf.at[pl.ds(j * 4, 4)]
        return qbuf.at[item, pl.ds(pl.multiple_of(j * 512, 512), 512)]

    def q_push(item, at):
        peer = (other, partner, other)[at]
        return remote(
            q_block(item, own_j),
            q_block(item, own_j),
            qb_send.at[item, at],
            qb_recv.at[item, (0, 0, 1)[at]],
            peer,
        )

    def q_own(item):
        q_own_copy(item).wait()
        for at, dz in enumerate((2, 1, 3)):
            arrived(q_landing(item, shifted(z, -dz)), qa_send, qa_recv, item, at, sibling)
        q_push(item, 1).start()
        q_push(item, 0).start()

    def q_relay(item):
        arrived(q_block(item, own_j), qb_send, qb_recv, item, 0, partner)
        q_push(item, 2).start()

    def q_ready(item):
        @pl.when(is_cross)
        def _():
            arrived(q_block(item, 1 - own_j), qb_send, qb_recv, item, 0, other)

        @pl.when(is_self)
        def _():
            arrived(q_block(item, 1 - own_j), qb_send, qb_recv, item, 1, other)

    lanes = lax.broadcasted_iota(jnp.int32, (128, 128), 1)
    sublanes = lax.broadcasted_iota(jnp.int32, (128, 128), 0)
    causal = sublanes >= lanes
    diagonal = sublanes == lanes

    def inverse_rms(values):
        return lax.rsqrt(jnp.mean(values * values, axis=1, keepdims=True) + EPSILON)

    def decay_column(head):
        return jnp.sum(jnp.where(lanes == head, decays[...], 0.0), axis=1, keepdims=True)

    def decay_setup():
        decays[...] = jnp.ones((128, 128), jnp.float32)
        decays_t[...] = jnp.ones((128, 128), jnp.float32)
        for head in range(HEADS):
            decays[head : head + 1, :] = gates_ref[head]
            picked = table_ref[rate_ref[0, head]]
            decays_t[head : head + 1, :] = jnp.full((1, 128), picked, jnp.float32)
        turned = jnp.dot(
            jnp.log(decays_t[...]) + jnp.log(decays[...]),
            jnp.where(sublanes <= lanes, 1.0, 0.0),
            precision=lax.Precision.HIGHEST,
            preferred_element_type=jnp.float32,
        )
        decays_t[...] = turned
        decays[...] = jnp.transpose(turned)
        fade_out[...] = jnp.broadcast_to(jnp.exp(turned[:, 127:128])[0:24], (24, 128))

    def retain(first, last):
        scale = inverse_rms(x_ref[...].astype(jnp.float32))

        def one(head, carry):
            columns = pl.ds(pl.multiple_of(head * HDIM, HDIM), HDIM)
            values = x_ref[:, columns]
            normed = values.astype(jnp.float32) * scale
            query = (normed * query_gain_ref[:, columns]).astype(jnp.bfloat16)
            key_rows = (normed * key_gain_ref[:, columns]).astype(jnp.bfloat16)
            queries[:, columns] = query
            products = lax.dot_general(
                query, key_rows, (((1,), (1,)), ((), ())), preferred_element_type=jnp.float32
            )
            column = decay_column(head)
            row = decays_t[pl.ds(head, 1), :]
            weights = jnp.where(
                causal, products * jnp.exp(jnp.where(causal, column - row, 0.0)), 0.0
            ).astype(jnp.bfloat16)
            inside[:, columns] = jnp.dot(weights, values, preferred_element_type=jnp.float32)
            fading = jnp.exp(row[:, 127:128] - column)
            faded = (key_rows.astype(jnp.float32) * fading).astype(jnp.bfloat16)
            update_out[pl.ds(head, 1)] = lax.dot_general(
                faded, values, (((0,), (0,)), ((), ())), preferred_element_type=jnp.float32
            ).astype(jnp.bfloat16)[None]
            return carry

        lax.fori_loop(first, last, one, 0, unroll=4 if (last - first) % 4 == 0 else 5)

    def update_copies():
        copies = []
        for at in range(8):
            to_seq, peer = seq_peer(at)
            rows = pl.ds(pl.multiple_of(to_seq * 16, 16), 16)
            pairs = (
                (update_out.at[:, rows, :], update_in.at[seq]),
                (fade_out, fade_in.at[seq]),
            )
            for kind, (src, dst) in enumerate(pairs):
                if at == 0:
                    copies.append(pltpu.make_async_copy(src, dst, s_local.at[1 + kind]))
                else:
                    copies.append(
                        remote(src, dst, u_send.at[at, kind], u_recv.at[at, kind], peer)
                    )
        return copies

    def enter_copies():
        copies = []
        for at in range(8):
            to_seq, peer = seq_peer(at)
            dst = enter_in.at[:, pl.ds(pl.multiple_of(seq * 16, 16), 16), :]
            if at == 0:
                copies.append(pltpu.make_async_copy(enter_out.at[to_seq], dst, s_local.at[3]))
            else:
                copies.append(
                    remote(enter_out.at[to_seq], dst, e_send.at[at], e_recv.at[at], peer)
                )
        return copies

    def scan():
        def one(head, carry):
            now = kept[pl.ds(head, 1)][0]
            for at in range(8):
                enter_out[at, pl.ds(head, 1)] = now.astype(jnp.bfloat16)[None]
                fade = fade_in[at, pl.ds(head, 1), :]
                now = fade * now + update_in[at, pl.ds(head, 1)][0].astype(jnp.float32)
            state_out[pl.ds(head, 1)] = now[None]
            return carry

        lax.fori_loop(0, HEADS, one, 0)

    def mix(first, last):
        def one(head, carry):
            columns = pl.ds(pl.multiple_of(head * HDIM, HDIM), HDIM)
            carried = jnp.dot(
                queries[:, columns], enter_in[pl.ds(head, 1)][0], preferred_element_type=jnp.float32
            )
            retained = inside[:, columns] + jnp.exp(decay_column(head)) * carried
            mixed = retained * inverse_rms(retained)
            result[:, columns] = (
                x_ref[:, columns].astype(jnp.float32) + mixed * out_gain_ref[:, columns]
            ).astype(jnp.bfloat16)
            return carry

        lax.fori_loop(first, last, one, 0, unroll=4 if (last - first) % 4 == 0 else 5)

    def self_result(group):
        columns = pl.ds(group * GROUP, GROUP)
        return remote(
            result.at[:, columns], out_ref.at[:, columns], w_send.at[group], w_recv.at[group], after
        )

    def fresh_rows(to):
        return result.at[pl.ds(pl.multiple_of((to // 2) * 16, 16), 16)]

    own_fresh = pltpu.make_async_copy(fresh_rows(section), fresh, s_local.at[4])

    def fresh_copy(by):
        to = lax.rem(section + 2 * by, 16)
        return remote(fresh_rows(to), fresh, f_send.at[by], f_recv.at[0], (to, seq))

    fresh_across = remote(fresh, fresh, f_send.at[0], f_recv.at[1], sibling)

    first_j = 1 - own_j

    def place_setup():
        lane = lax.broadcasted_iota(jnp.int32, (1, 128), 1)
        for pair in range(16):
            pos_ref[:, pair * 128 : (pair + 1) * 128] = jnp.where(
                lane < 64,
                metabuf[2 * pair, 0:1, :],
                pltpu.roll(metabuf[2 * pair + 1, 0:1, :], 64, 1),
            )

    def tree(combine, values):
        while len(values) > 1:
            values = [
                combine(values[at], values[at + 1]) if at + 1 < len(values) else values[at]
                for at in range(0, len(values), 2)
            ]
        return values[0]

    def block_of(step):
        item, block = step // 4, step % 4
        return item, jnp.where(block < 2, first_j, own_j), block % 2

    def block_rows(j, at):
        return pl.ds(pl.multiple_of(j * 512 + at * QBLOCK, QBLOCK), QBLOCK)

    def stage(current, previous, even):
        fill, fill_top = (scores_even, top_even) if even else (scores_odd, top_odd)
        drain, drain_top = (scores_odd, top_odd) if even else (scores_even, top_even)
        if current is not None:
            item, j, at = block_of(current)
            row = lax.broadcasted_iota(jnp.int32, (QBLOCK, 128), 0)
            index = (at * 2 + row // TOKENS) * 256 + (x % 2) * TOKENS + row % TOKENS
            query = qbuf[item, block_rows(j, at), :]
            places = index + beginbuf[j * 4][0:1, :]
            highest = jnp.full((QBLOCK, 128), MASKED_SCORE, jnp.float32)
        if previous is not None:
            item_p, j_p, at_p = block_of(previous)
            top = drain_top[...][:, 0:1]
            totals = jnp.zeros((QBLOCK, 128), jnp.float32)
            pieces = jnp.zeros((QBLOCK, HDIM), jnp.float32)
        for chunk in range(KEYS // KCHUNK):
            here = slice(chunk * KCHUNK, (chunk + 1) * KCHUNK)
            parts = [
                slice(chunk * KCHUNK + part * 128, chunk * KCHUNK + (part + 1) * 128)
                for part in range(KCHUNK // 128)
            ]
            if current is not None:
                scores = lax.dot_general(
                    query,
                    kvbuf[item, here, 0:HDIM],
                    (((1,), (1,)), ((), ())),
                    preferred_element_type=jnp.float32,
                )
            if previous is not None:
                likely = [jnp.exp2((drain[:, part] - top) * STEP) for part in parts]
                totals += tree(jnp.add, likely)
                pieces += jnp.dot(
                    jnp.concatenate([value.astype(jnp.bfloat16) for value in likely], axis=1),
                    kvbuf[item_p, here, HDIM : 2 * HDIM],
                    preferred_element_type=jnp.float32,
                )
            if current is not None:
                masked = []
                for at_part, part in enumerate(parts):
                    piece = jnp.where(
                        pos_ref[:, part] <= places,
                        scores[:, at_part * 128 : (at_part + 1) * 128],
                        MASKED_SCORE,
                    )
                    fill[:, part] = piece
                    masked.append(piece)
                highest = jnp.maximum(highest, tree(jnp.maximum, masked))
        if current is not None:
            fill_top[...] = jnp.broadcast_to(
                jnp.max(highest, axis=1, keepdims=True), (QBLOCK, 128)
            )
        if previous is not None:
            total = jnp.sum(totals, axis=1, keepdims=True)
            o_out[item_p, block_rows(j_p, at_p), :] = (pieces / total).astype(jnp.bfloat16)
            lse = top * HDIM ** (-0.5) + jnp.log(total)
            wide = lax.broadcasted_iota(jnp.int32, (QBLOCK, QBLOCK), 0) == (
                lax.broadcasted_iota(jnp.int32, (QBLOCK, QBLOCK), 1)
            )
            flat = jnp.sum(jnp.where(wide, lse, 0.0), axis=0, keepdims=True)
            lse_out[item_p, j_p, pl.ds(at_p * 2, 1), :] = flat[:, 0:128]
            lse_out[item_p, j_p, pl.ds(at_p * 2 + 1, 1), :] = flat[:, 128:256]

    def pieces_of(item, j):
        return o_out.at[item, pl.ds(pl.multiple_of(j * 512, 512), 512)], lse_out.at[item, j]

    def piece_copies(item, at):
        peer, j = ((other, first_j), (partner, own_j))[at]
        o_src, lse_src = pieces_of(item, j)
        return [
            remote(o_src, o_in.at[item, at], o_send.at[item, at, 0], o_recv.at[item, at, 0], peer),
            remote(
                lse_src, lse_in.at[item, at], o_send.at[item, at, 1], o_recv.at[item, at, 1], peer
            ),
        ]

    def shares_of(tiles):
        overall = tiles[0]
        for tile in tiles[1:]:
            overall = jnp.maximum(overall, tile)
        shares = [jnp.exp(tile - overall) for tile in tiles]
        whole = shares[0]
        for share in shares[1:]:
            whole = whole + share
        return [share / whole for share in shares], overall + jnp.log(whole)

    def weighted(shares, parts, group):
        total = jnp.zeros((TOKENS, HDIM), jnp.float32)
        for share, part in zip(shares, parts):
            column = jnp.sum(
                jnp.where(diagonal, share[group : group + 1, :], 0.0), axis=1, keepdims=True
            )
            total += column * part.astype(jnp.float32)
        return total.astype(jnp.bfloat16)

    def own_rows(group):
        return pl.ds(pl.multiple_of(own_j * 512 + group * TOKENS, TOKENS), TOKENS)

    def merge_self(item):
        for copy in piece_copies(item, 0):
            copy.wait_recv()
        shares, lse = shares_of([lse_out[item, own_j], lse_in[item, 0]])
        for group in range(4):
            here = slice(group * TOKENS, (group + 1) * TOKENS)
            o_out[item, own_rows(group), :] = weighted(
                shares, (o_out[item, own_rows(group), :], o_in[item, 0, here, :]), group
            )
        lse_out[item, own_j] = lse
        for copy in piece_copies(item, 1):
            copy.start()

    def att_copies(item):
        copies = [
            pltpu.make_async_copy(
                att_out.at[item, pl.ds(pl.multiple_of(z * TOKENS, TOKENS), TOKENS)],
                att_in.at[item, z],
                t_local.at[item],
            )
        ]
        for at, dz in enumerate((2, 1, 3)):
            to_z = shifted(z, dz)
            copies.append(
                remote(
                    att_out.at[item, pl.ds(pl.multiple_of(to_z * TOKENS, TOKENS), TOKENS)],
                    att_in.at[item, z],
                    t_send.at[item, at],
                    t_recv.at[item, at],
                    device_at(y, x, to_z, core),
                )
            )
        return copies

    def merge_cross(item):
        for at in range(2):
            for copy in piece_copies(item, at):
                copy.wait_recv()
        shares, _ = shares_of([lse_out[item, own_j], lse_in[item, 0], lse_in[item, 1]])
        for group in range(4):
            here = slice(group * TOKENS, (group + 1) * TOKENS)
            att_out[item, here, :] = weighted(
                shares,
                (
                    o_out[item, own_rows(group), :],
                    o_in[item, 0, here, :],
                    o_in[item, 1, here, :],
                ),
                group,
            )
        for copy in att_copies(item):
            copy.start()

    def head_columns(item, group):
        return pl.ds(pl.multiple_of(group * GROUP + item * HDIM, HDIM), HDIM)

    def att_result(item, group):
        columns = head_columns(item, group)
        return remote(
            result.at[:, columns],
            out_ref.at[:, columns],
            r_send.at[item, group],
            r_recv.at[item, group],
            after,
        )

    def finish(item):
        for copy in att_copies(item):
            copy.wait()
        for group in range(4):
            here = head_columns(item, group)
            result[:, here] = (
                x_ref[:, here].astype(jnp.float32)
                + att_in[item, group].astype(jnp.float32) * out_gain_ref[:, here]
            ).astype(jnp.bfloat16)
            att_result(item, group).start()

    pl.semaphore_wait(barrier, len(peers) + 1 + jnp.where(is_root, 15, 0))
    kv_spread(0)
    for copy in fetches:
        copy.wait()
    meta_ref[0:1, 0:64] = positions_ref[...]
    begin_ref[...] = jnp.full((8, 128), start_ref[0, 0], jnp.int32)
    kv_spread(META)

    def on_self(*steps):
        @pl.when(is_self)
        def _():
            for step in steps:
                step()

    def on_cross(*steps):
        @pl.when(is_cross)
        def _():
            for step in steps:
                step()

    def send_updates():
        for copy in update_copies():
            copy.start()

    def enter():
        for copy in update_copies():
            copy.wait()
        scan()
        for copy in enter_copies():
            copy.start()

    def keep_state():
        state_rows.wait()
        on_cross(lambda: state_out.__setitem__(Ellipsis, kept[...]))
        on_self(enter)

    def self_mix():
        for copy in enter_copies():
            copy.wait()
        for group in range(4):
            mix(group * LOCAL_HEADS, (group + 1) * LOCAL_HEADS)
            self_result(group).start()

    def send_fresh():
        @pl.when(is_root)
        def _():
            own_fresh.start()
            for by in range(1, 8):
                fresh_copy(by).start()

    def own(item):
        kv_own(item)
        on_cross(lambda: q_own(item))

    def make_queries():
        rows = x_ref[...].astype(jnp.float32)
        queries[...] = (rows * inverse_rms(rows) * query_gain_ref[...]).astype(jnp.bfloat16)
        q_spread(META)
        q_spread(0)

    def spread(item):
        kv_spread(item)
        on_cross(lambda: q_spread(item))

    on_cross(make_queries)
    spread(1)
    on_self(decay_setup, lambda: retain(0, 8))
    own(META)
    own(0)
    spread(2)
    on_self(lambda: retain(8, 16))
    own(1)
    spread(3)
    kv_forward(META)
    kv_forward(0)
    on_self(lambda: retain(16, HEADS))
    own(2)
    spread(4)
    on_self(lambda: q_relay(META), lambda: q_relay(0))
    kv_forward(1)
    kv_far(META)
    kv_far(0)
    own(3)
    on_self(lambda: q_relay(1))
    kv_forward(2)
    kv_far(1)
    q_ready(META)
    kv_ready(META)
    place_setup()

    hooks = {
        0: (lambda: own(4), lambda: on_self(lambda: q_relay(2))),
        1: (lambda: kv_forward(3),),
        2: (lambda: kv_far(2),),
        3: (lambda: on_self(lambda: q_relay(3)),),
        4: (lambda: kv_forward(4),),
        5: (lambda: kv_far(3),),
        6: (lambda: on_self(lambda: q_relay(4)),),
        7: (lambda: kv_far(4), lambda: on_self(send_updates)),
        12: (lambda: on_cross(lambda: merge_cross(0)),),
        14: (keep_state,),
        16: (lambda: on_cross(lambda: finish(0), lambda: merge_cross(1)),),
    }

    def after_block(step):
        item, block = step // 4, step % 4

        @pl.when(block == 1)
        def _():
            for copy in piece_copies(item, 0):
                copy.start()

        for due, steps in hooks.items():

            @pl.when(step == due)
            def _():
                for one in steps:
                    one()

        @pl.when(jnp.logical_and(is_self, jnp.logical_and(block == 1, item >= 1)))
        def _():
            merge_self(item - 1)

    q_ready(0)
    kv_ready(0)
    stage(0, None, True)

    def two_blocks(pair, carry):
        step = 2 * pair
        stage(step + 1, step, False)
        after_block(step)

        @pl.when(pair % 2 == 1)
        def _():
            q_ready((step + 2) // 4)
            kv_ready((step + 2) // 4)

        stage(step + 2, step + 1, True)
        after_block(step + 1)
        return carry

    last = 4 * LOCAL_HEADS - 1
    lax.fori_loop(0, (last - 1) // 2, two_blocks, 0)
    stage(last, last - 1, False)
    after_block(jnp.int32(last - 1))
    stage(None, last, True)
    on_self(lambda: merge_self(4))
    on_self(self_mix)
    send_fresh()
    on_cross(
        lambda: finish(1),
        lambda: merge_cross(2),
        lambda: merge_cross(3),
        lambda: finish(2),
        lambda: finish(3),
        lambda: merge_cross(4),
        lambda: finish(4),
    )

    @pl.when(is_root)
    def _():
        own_fresh.wait()

    @pl.when(jnp.logical_and(core == 1, jnp.logical_not(is_root)))
    def _():
        fresh_copy(1).wait_recv()

    @pl.when(core == 1)
    def _():
        fresh_across.start()

    @pl.when(core == 0)
    def _():
        fresh_across.wait_recv()

    both = fresh[...].astype(jnp.float32)
    new_rows = jnp.where(core == 0, both[0:8], both[8:16])
    new_rows = new_rows * inverse_rms(new_rows)
    global_out[:, 0:HD] = (new_rows * global_ref[0:1, :]).astype(jnp.bfloat16)
    global_out[:, HD : 2 * HD] = (new_rows * global_ref[1:2, :]).astype(jnp.bfloat16)

    from_self = jnp.logical_and(section >= 1, section <= 8)

    @pl.when(from_self)
    def _():
        for group in range(4):
            self_result(group).wait_recv()

    @pl.when(jnp.logical_not(from_self))
    def _():
        for item in range(LOCAL_HEADS):
            for group in range(4):
                att_result(item, group).wait_recv()

    for item in range(LOCAL_HEADS + 1):
        for copy in kv_spread_copies(item) + kv_pushes(item):
            copy.wait_send()
    for item in range(LOCAL_HEADS):
        for copy in piece_copies(item, 0):
            copy.wait_send()

    @pl.when(is_cross)
    def _():
        for item in range(LOCAL_HEADS + 1):
            for copy in q_spread_copies(item):
                copy.wait_send()
            q_push(item, 0).wait_send()
            q_push(item, 1).wait_send()
        for item in range(LOCAL_HEADS):
            for group in range(4):
                att_result(item, group).wait_send()

    @pl.when(is_self)
    def _():
        for item in range(LOCAL_HEADS + 1):
            q_push(item, 2).wait_send()
        for item in range(LOCAL_HEADS):
            for copy in piece_copies(item, 1):
                copy.wait_send()
        for group in range(4):
            self_result(group).wait_send()

    @pl.when(core == 1)
    def _():
        fresh_across.wait_send()

    @pl.when(is_root)
    def _():
        for by in range(1, 8):
            fresh_copy(by).wait_send()


def span(*arguments):
    vmem = pl.BlockSpec(memory_space=pltpu.VMEM)
    hbm = pl.BlockSpec(memory_space=pl.ANY)
    dma = pltpu.SemaphoreType.DMA
    items = LOCAL_HEADS + 1

    def bf16(*shape):
        return pltpu.VMEM(shape, jnp.bfloat16)

    def f32(*shape):
        return pltpu.VMEM(shape, jnp.float32)

    def i32(*shape):
        return pltpu.VMEM(shape, jnp.int32)

    return pl.pallas_call(
        span_kernel,
        out_shape=(
            jax.ShapeDtypeStruct((TOKENS, HD), jnp.bfloat16),
            jax.ShapeDtypeStruct((HEADS, 16, HDIM), jnp.float32),
            jax.ShapeDtypeStruct((8, 2 * HD), jnp.bfloat16),
        ),
        in_specs=[hbm] * 12,
        out_specs=(vmem, vmem, vmem),
        scratch_shapes=[
            bf16(TOKENS, HD),
            pltpu.SMEM((16,), jnp.float32),
            pltpu.SMEM((1, 1), jnp.int32),
            pltpu.SMEM((1, HEADS), jnp.int32),
            f32(HEADS, 1, TOKENS),
            f32(1, HD),
            f32(1, HD),
            f32(1, HD),
            f32(2, HD),
            i32(1, 64),
            dma((10,)),
            bf16(TOKENS, HD),
            i32(8, 128),
            i32(8, 128),
            bf16(LOCAL_HEADS, KEYS, 2 * HDIM),
            i32(32, 8, 128),
            i32(8, 8, 128),
            bf16(LOCAL_HEADS, 1024, HDIM),
            f32(QBLOCK, KEYS),
            f32(QBLOCK, KEYS),
            f32(QBLOCK, 128),
            f32(QBLOCK, 128),
            i32(1, KEYS),
            bf16(LOCAL_HEADS, 1024, HDIM),
            f32(LOCAL_HEADS, 2, 8, 128),
            bf16(LOCAL_HEADS, 2, 512, HDIM),
            f32(LOCAL_HEADS, 2, 8, 128),
            bf16(LOCAL_HEADS, 512, HDIM),
            bf16(LOCAL_HEADS, 4, TOKENS, HDIM),
            bf16(TOKENS, HD),
            f32(128, 128),
            f32(128, 128),
            f32(TOKENS, HD),
            f32(HEADS, 16, HDIM),
            bf16(HEADS, HDIM, HDIM),
            f32(24, 128),
            bf16(8, HEADS, 16, HDIM),
            f32(8, 24, 128),
            bf16(8, HEADS, 16, HDIM),
            bf16(HEADS, HDIM, HDIM),
            bf16(16, HD),
            dma((items, 2, 3)),
            dma((items, 2, 3)),
            dma((items, 2)),
            dma((items, 4)),
            dma((items, 4)),
            dma((items, 5)),
            dma((items, 5)),
            dma((items, 3)),
            dma((items, 3)),
            dma((items,)),
            dma((items, 3)),
            dma((items, 2)),
            dma((LOCAL_HEADS, 2, 2)),
            dma((LOCAL_HEADS, 2, 2)),
            dma((LOCAL_HEADS, 3)),
            dma((LOCAL_HEADS, 3)),
            dma((LOCAL_HEADS,)),
            dma((8, 2)),
            dma((8, 2)),
            dma((8,)),
            dma((8,)),
            dma((5,)),
            dma((LOCAL_HEADS, 4)),
            dma((LOCAL_HEADS, 4)),
            dma((4,)),
            dma((4,)),
            dma((8,)),
            dma((2,)),
        ],
        compiler_params=pltpu.CompilerParams(
            collective_id=0, has_side_effects=True, vmem_limit_bytes=58 * 1024 * 1024
        ),
        name="span",
    )(*arguments)


def local(
    section_input,
    state_in,
    decay_table,
    head_rate,
    gates,
    query_gain,
    key_gain,
    out_gain,
    global_gain,
    cache_kv,
    cache_pos,
    span_start,
):
    section_output, state_out, global_new = span(
        section_input[0],
        state_in[0],
        decay_table,
        head_rate,
        jnp.transpose(gates, (2, 0, 1)),
        query_gain,
        key_gain,
        out_gain,
        global_gain,
        cache_kv,
        cache_pos[None],
        span_start[None],
    )
    return (section_output[None], state_out[None], global_new[None, None])


def solution(mesh):
    return jax.shard_map(
        local,
        mesh=mesh,
        in_specs=(
            P("section", "seq", None),
            P("section", None, None, None),
            P(),
            P("section", None),
            P("section", "seq", None),
            P("section", None),
            P("section", None),
            P("section", None),
            P(),
            P(("section", "seq"), None),
            P(("section", "seq")),
            P("section"),
        ),
        out_specs=(
            P("section", "seq", None),
            P("section", None, "seq", None),
            P("seq", "section", None, None),
        ),
        check_vma=False,
    )
```

```python
import jax
import jax.numpy as jnp
from jax import lax
from jax.experimental import pallas as pl
from jax.experimental.pallas import tpu as pltpu
from jax.sharding import PartitionSpec as P

MESH = pl.DeviceIdType.MESH
EPSILON = 1e-06
MASKED_SCORE = -1e30
LOG2E = 1.4426950408889634
HD = 2560
HEADS = 20
HDIM = 128
GROUP = 640
LOCAL_HEADS = 5
KEYS = 2048
TOKENS = 128
QBLOCK = 256
KCHUNK = 512
STEP = HDIM ** (-0.5) * LOG2E


def device_at(y, x, z, core):
    return (y * 4 + (x // 2) * 2 + core, z * 2 + x % 2)


def shifted(value, by):
    return lax.rem(value + by + 4, 4)


def remote(src, dst, send_sem, recv_sem, peer):
    return pltpu.make_async_remote_copy(
        src_ref=src,
        dst_ref=dst,
        send_sem=send_sem,
        recv_sem=recv_sem,
        device_id=peer,
        device_id_type=MESH,
    )


def span_kernel(
    x_hbm,
    state_ref,
    table_hbm,
    rate_hbm,
    gates_hbm,
    query_gain_hbm,
    key_gain_hbm,
    out_gain_hbm,
    global_hbm,
    kv_ref,
    positions_hbm,
    start_hbm,
    out_ref,
    state_out,
    global_out,
    x_ref,
    table_ref,
    start_ref,
    rate_ref,
    gates_ref,
    query_gain_ref,
    key_gain_ref,
    out_gain_ref,
    global_ref,
    positions_ref,
    i_local,
    queries,
    meta_ref,
    begin_ref,
    kvbuf,
    metabuf,
    beginbuf,
    qbuf,
    scores_even,
    scores_odd,
    top_even,
    top_odd,
    pos_ref,
    o_out,
    lse_out,
    o_in,
    lse_in,
    att_out,
    att_in,
    result,
    decays,
    decays_t,
    inside,
    kept,
    update_out,
    fade_out,
    update_in,
    fade_in,
    enter_out,
    enter_in,
    fresh,
    a_send,
    a_recv,
    a_local,
    b_send,
    b_recv,
    c_send,
    c_recv,
    qa_send,
    qa_recv,
    qa_local,
    qb_send,
    qb_recv,
    o_send,
    o_recv,
    t_send,
    t_recv,
    t_local,
    u_send,
    u_recv,
    e_send,
    e_recv,
    s_local,
    r_send,
    r_recv,
    w_send,
    w_recv,
    f_send,
    f_recv,
):
    section = lax.axis_index("section")
    seq = lax.axis_index("seq")
    y, core = section // 4, section % 2
    x, z = ((section // 2) % 2) * 2 + seq % 2, seq // 2
    is_self = section < 8
    is_cross = jnp.logical_not(is_self)
    is_root = section == 7
    sibling = device_at(y, x, z, 1 - core)
    other = device_at(y + 1 - 2 * (y % 2), x, z, core)
    partner = device_at(3 - y, x, z, core)
    after = (lax.rem(section + 1, 16), seq)
    before = (lax.rem(section + 15, 16), seq)

    fetches = [
        pltpu.make_async_copy(src, dst, i_local.at[at])
        for at, (src, dst) in enumerate(
            (
                (x_hbm, x_ref),
                (table_hbm, table_ref),
                (start_hbm, start_ref),
                (query_gain_hbm, query_gain_ref),
                (positions_hbm, positions_ref),
                (rate_hbm, rate_ref),
                (gates_hbm, gates_ref),
                (key_gain_hbm, key_gain_ref),
                (out_gain_hbm, out_gain_ref),
                (global_hbm, global_ref),
            )
        )
    ]
    for copy in fetches:
        copy.start()
    state_rows = pltpu.make_async_copy(
        state_ref.at[:, pl.ds(pl.multiple_of(seq * 16, 16), 16), :], kept, s_local.at[0]
    )
    state_rows.start()

    def seq_peer(at):
        to_z, to_x = shifted(z, at // 2), (x // 2) * 2 + lax.rem(x + at % 2, 2)
        return to_z * 2 + to_x % 2, device_at(y, to_x, to_z, core)

    peers = [sibling, other, partner]
    peers += [device_at(y, shifted(x, dx), z, core) for dx in (1, 3)]
    peers += [seq_peer(at)[1] for at in range(2, 8)]
    barrier = pltpu.get_barrier_semaphore()
    for peer in peers + [before]:
        pl.semaphore_signal(barrier, inc=1, device_id=peer, device_id_type=MESH)

    @pl.when(jnp.logical_not(is_root))
    def _():
        pl.semaphore_signal(barrier, inc=1, device_id=(7, seq), device_id_type=MESH)

    META = LOCAL_HEADS

    def is_meta(item):
        return isinstance(item, int) and item == META

    def kinds(item):
        return (0,) if is_meta(item) else (0, 1)

    def kv_source(item, kind, to_z):
        if is_meta(item):
            return meta_ref
        column = to_z * GROUP + item * HDIM + kind * HD
        return kv_ref.at[:, pl.ds(pl.multiple_of(column, HDIM), HDIM)]

    def kv_landing(item, kind, from_z):
        if is_meta(item):
            return metabuf.at[x * 8 + core * 4 + from_z]
        rows = pl.ds(pl.multiple_of(x * 512 + core * 256 + from_z * 64, 64), 64)
        return kvbuf.at[item, rows, pl.ds(kind * HDIM, HDIM)]

    def kv_spread_copies(item):
        return [
            remote(
                kv_source(item, kind, shifted(z, dz)),
                kv_landing(item, kind, z),
                a_send.at[item, kind, at],
                a_recv.at[item, kind, at],
                device_at(y, x, shifted(z, dz), core),
            )
            for kind in kinds(item)
            for at, dz in enumerate((2, 1, 3))
        ]

    def kv_spread(item):
        for copy in kv_spread_copies(item):
            copy.start()
        for kind in kinds(item):
            pltpu.make_async_copy(
                kv_source(item, kind, z), kv_landing(item, kind, z), a_local.at[item, kind]
            ).start()

    def kv_block(item, from_x, from_core, part):
        start, count = ((0, 4), (0, 2), (2, 2))[part]
        if is_meta(item):
            return metabuf.at[pl.ds(from_x * 8 + from_core * 4 + start, count)]
        rows = pl.ds(
            pl.multiple_of(from_x * 512 + from_core * 256 + start * 64, 64), count * 64
        )
        return kvbuf.at[item, rows]

    x_up, x_down, x_far = shifted(x, 1), shifted(x, 3), shifted(x, 2)
    up, down = device_at(y, x_up, z, core), device_at(y, x_down, z, core)

    def arrived(ref, sends, recvs, item, at, peer):
        remote(ref, ref, sends.at[item, at], recvs.at[item, at], peer).wait_recv()

    def kv_own(item):
        for kind in kinds(item):
            pltpu.make_async_copy(
                kv_source(item, kind, z), kv_landing(item, kind, z), a_local.at[item, kind]
            ).wait()
            for at, dz in enumerate((2, 1, 3)):
                landed = kv_landing(item, kind, shifted(z, -dz))
                remote(
                    landed, landed, a_send.at[item, kind, at], a_recv.at[item, kind, at], sibling
                ).wait_recv()
        for copy in kv_pushes(item)[0:3]:
            copy.start()

    def kv_pushes(item):
        here, below = kv_block(item, x, core, 0), kv_block(item, x_down, core, 0)
        above = kv_block(item, x_up, core, 0)

        def along(ref, at, peer):
            return remote(ref, ref, b_send.at[item, at], b_recv.at[item, at], peer)

        def across(ref, at):
            return remote(ref, ref, c_send.at[item, at], c_recv.at[item, at], sibling)

        return [
            along(here, 0, up),
            along(here, 1, down),
            across(here, 0),
            along(kv_block(item, x_down, core, 1), 2, up),
            across(below, 1),
            along(kv_block(item, x_up, core, 2), 3, down),
            across(above, 2),
            across(kv_block(item, x_far, core, 1), 3),
            across(kv_block(item, x_far, core, 2), 4),
        ]

    def kv_forward(item):
        pushes = kv_pushes(item)
        arrived(kv_block(item, x_down, core, 0), b_send, b_recv, item, 0, up)
        pushes[3].start()
        pushes[4].start()
        arrived(kv_block(item, x_up, core, 0), b_send, b_recv, item, 1, down)
        pushes[5].start()
        pushes[6].start()

    def kv_far(item):
        pushes = kv_pushes(item)
        for part in (1, 2):
            arrived(kv_block(item, x_far, core, part), b_send, b_recv, item, part + 1, up)
            pushes[part + 6].start()

    def kv_ready(item):
        for at, (from_x, part) in enumerate(
            ((x, 0), (x_down, 0), (x_up, 0), (x_far, 1), (x_far, 2))
        ):
            arrived(kv_block(item, from_x, 1 - core, part), c_send, c_recv, item, at, sibling)

    own_j = jnp.where(is_self, 1 - y, y - 2)

    def q_source(item, to_z):
        if is_meta(item):
            return begin_ref
        return queries.at[:, pl.ds(pl.multiple_of(to_z * GROUP + item * HDIM, HDIM), HDIM)]

    def q_landing(item, from_z):
        if is_meta(item):
            return beginbuf.at[own_j * 4 + from_z]
        rows = pl.ds(pl.multiple_of(own_j * 512 + from_z * TOKENS, TOKENS), TOKENS)
        return qbuf.at[item, rows]

    def q_own_copy(item):
        return pltpu.make_async_copy(q_source(item, z), q_landing(item, z), qa_local.at[item])

    def q_spread_copies(item):
        return [
            remote(
                q_source(item, shifted(z, dz)),
                q_landing(item, z),
                qa_send.at[item, at],
                qa_recv.at[item, at],
                device_at(y, x, shifted(z, dz), core),
            )
            for at, dz in enumerate((2, 1, 3))
        ]

    def q_spread(item):
        for copy in q_spread_copies(item):
            copy.start()
        q_own_copy(item).start()

    def q_block(item, j):
        if is_meta(item):
            return beginbuf.at[pl.ds(j * 4, 4)]
        return qbuf.at[item, pl.ds(pl.multiple_of(j * 512, 512), 512)]

    def q_push(item, at):
        peer = (other, partner, other)[at]
        return remote(
            q_block(item, own_j),
            q_block(item, own_j),
            qb_send.at[item, at],
            qb_recv.at[item, (0, 0, 1)[at]],
            peer,
        )

    def q_own(item):
        q_own_copy(item).wait()
        for at, dz in enumerate((2, 1, 3)):
            arrived(q_landing(item, shifted(z, -dz)), qa_send, qa_recv, item, at, sibling)
        q_push(item, 1).start()
        q_push(item, 0).start()

    def q_relay(item):
        arrived(q_block(item, own_j), qb_send, qb_recv, item, 0, partner)
        q_push(item, 2).start()

    def q_ready(item):
        @pl.when(is_cross)
        def _():
            arrived(q_block(item, 1 - own_j), qb_send, qb_recv, item, 0, other)

        @pl.when(is_self)
        def _():
            arrived(q_block(item, 1 - own_j), qb_send, qb_recv, item, 1, other)

    lanes = lax.broadcasted_iota(jnp.int32, (128, 128), 1)
    sublanes = lax.broadcasted_iota(jnp.int32, (128, 128), 0)
    causal = sublanes >= lanes
    diagonal = sublanes == lanes

    def inverse_rms(values):
        return lax.rsqrt(jnp.mean(values * values, axis=1, keepdims=True) + EPSILON)

    def decay_column(head):
        return jnp.sum(jnp.where(lanes == head, decays[...], 0.0), axis=1, keepdims=True)

    def decay_setup():
        decays[...] = jnp.ones((128, 128), jnp.float32)
        decays_t[...] = jnp.ones((128, 128), jnp.float32)
        for head in range(HEADS):
            decays[head : head + 1, :] = gates_ref[head]
            picked = table_ref[rate_ref[0, head]]
            decays_t[head : head + 1, :] = jnp.full((1, 128), picked, jnp.float32)
        turned = jnp.dot(
            jnp.log(decays_t[...]) + jnp.log(decays[...]),
            jnp.where(sublanes <= lanes, 1.0, 0.0),
            precision=lax.Precision.HIGHEST,
            preferred_element_type=jnp.float32,
        )
        decays_t[...] = turned
        decays[...] = jnp.transpose(turned)
        fade_out[...] = jnp.broadcast_to(jnp.exp(turned[:, 127:128])[0:24], (24, 128))

    def retain(first, last):
        scale = inverse_rms(x_ref[...].astype(jnp.float32))

        def one(head, carry):
            columns = pl.ds(pl.multiple_of(head * HDIM, HDIM), HDIM)
            values = x_ref[:, columns]
            normed = values.astype(jnp.float32) * scale
            query = (normed * query_gain_ref[:, columns]).astype(jnp.bfloat16)
            key_rows = (normed * key_gain_ref[:, columns]).astype(jnp.bfloat16)
            queries[:, columns] = query
            products = lax.dot_general(
                query, key_rows, (((1,), (1,)), ((), ())), preferred_element_type=jnp.float32
            )
            column = decay_column(head)
            row = decays_t[pl.ds(head, 1), :]
            weights = jnp.where(
                causal, products * jnp.exp(jnp.where(causal, column - row, 0.0)), 0.0
            ).astype(jnp.bfloat16)
            inside[:, columns] = jnp.dot(weights, values, preferred_element_type=jnp.float32)
            fading = jnp.exp(row[:, 127:128] - column)
            faded = (key_rows.astype(jnp.float32) * fading).astype(jnp.bfloat16)
            update_out[pl.ds(head, 1)] = lax.dot_general(
                faded, values, (((0,), (0,)), ((), ())), preferred_element_type=jnp.float32
            ).astype(jnp.bfloat16)[None]
            return carry

        lax.fori_loop(first, last, one, 0, unroll=4 if (last - first) % 4 == 0 else 5)

    def update_copies():
        copies = []
        for at in range(8):
            to_seq, peer = seq_peer(at)
            rows = pl.ds(pl.multiple_of(to_seq * 16, 16), 16)
            pairs = (
                (update_out.at[:, rows, :], update_in.at[seq]),
                (fade_out, fade_in.at[seq]),
            )
            for kind, (src, dst) in enumerate(pairs):
                if at == 0:
                    copies.append(pltpu.make_async_copy(src, dst, s_local.at[1 + kind]))
                else:
                    copies.append(
                        remote(src, dst, u_send.at[at, kind], u_recv.at[at, kind], peer)
                    )
        return copies

    def enter_copies():
        copies = []
        for at in range(8):
            to_seq, peer = seq_peer(at)
            dst = enter_in.at[:, pl.ds(pl.multiple_of(seq * 16, 16), 16), :]
            if at == 0:
                copies.append(pltpu.make_async_copy(enter_out.at[to_seq], dst, s_local.at[3]))
            else:
                copies.append(
                    remote(enter_out.at[to_seq], dst, e_send.at[at], e_recv.at[at], peer)
                )
        return copies

    def scan():
        def one(head, carry):
            now = kept[pl.ds(head, 1)][0]
            for at in range(8):
                enter_out[at, pl.ds(head, 1)] = now.astype(jnp.bfloat16)[None]
                fade = fade_in[at, pl.ds(head, 1), :]
                now = fade * now + update_in[at, pl.ds(head, 1)][0].astype(jnp.float32)
            state_out[pl.ds(head, 1)] = now[None]
            return carry

        lax.fori_loop(0, HEADS, one, 0, unroll=4)

    def mix(first, last):
        def one(head, carry):
            columns = pl.ds(pl.multiple_of(head * HDIM, HDIM), HDIM)
            carried = jnp.dot(
                queries[:, columns], enter_in[pl.ds(head, 1)][0], preferred_element_type=jnp.float32
            )
            retained = inside[:, columns] + jnp.exp(decay_column(head)) * carried
            mixed = retained * inverse_rms(retained)
            result[:, columns] = (
                x_ref[:, columns].astype(jnp.float32) + mixed * out_gain_ref[:, columns]
            ).astype(jnp.bfloat16)
            return carry

        lax.fori_loop(first, last, one, 0, unroll=4 if (last - first) % 4 == 0 else 5)

    def self_result(group):
        columns = pl.ds(group * GROUP, GROUP)
        return remote(
            result.at[:, columns], out_ref.at[:, columns], w_send.at[group], w_recv.at[group], after
        )

    def fresh_rows(to):
        return result.at[pl.ds(pl.multiple_of((to // 2) * 16, 16), 16)]

    own_fresh = pltpu.make_async_copy(fresh_rows(section), fresh, s_local.at[4])

    def fresh_copy(by):
        to = lax.rem(section + 2 * by, 16)
        return remote(fresh_rows(to), fresh, f_send.at[by], f_recv.at[0], (to, seq))

    fresh_across = remote(fresh, fresh, f_send.at[0], f_recv.at[1], sibling)

    first_j = 1 - own_j

    def place_setup():
        lane = lax.broadcasted_iota(jnp.int32, (1, 128), 1)
        for pair in range(16):
            pos_ref[:, pair * 128 : (pair + 1) * 128] = jnp.where(
                lane < 64,
                metabuf[2 * pair, 0:1, :],
                pltpu.roll(metabuf[2 * pair + 1, 0:1, :], 64, 1),
            )

    def tree(combine, values):
        while len(values) > 1:
            values = [
                combine(values[at], values[at + 1]) if at + 1 < len(values) else values[at]
                for at in range(0, len(values), 2)
            ]
        return values[0]

    def block_of(step):
        item, block = step // 4, step % 4
        return item, jnp.where(block < 2, first_j, own_j), block % 2

    def block_rows(j, at):
        return pl.ds(pl.multiple_of(j * 512 + at * QBLOCK, QBLOCK), QBLOCK)

    def stage(current, previous, even):
        fill, fill_top = (scores_even, top_even) if even else (scores_odd, top_odd)
        drain, drain_top = (scores_odd, top_odd) if even else (scores_even, top_even)
        if current is not None:
            item, j, at = block_of(current)
            row = lax.broadcasted_iota(jnp.int32, (QBLOCK, 128), 0)
            index = (at * 2 + row // TOKENS) * 256 + (x % 2) * TOKENS + row % TOKENS
            query = qbuf[item, block_rows(j, at), :]
            places = index + beginbuf[j * 4][0:1, :]
            highest = jnp.full((QBLOCK, 128), MASKED_SCORE, jnp.float32)
        if previous is not None:
            item_p, j_p, at_p = block_of(previous)
            top = drain_top[...][:, 0:1]
            totals = jnp.zeros((QBLOCK, 128), jnp.float32)
            pieces = jnp.zeros((QBLOCK, HDIM), jnp.float32)
        for chunk in range(KEYS // KCHUNK):
            here = slice(chunk * KCHUNK, (chunk + 1) * KCHUNK)
            parts = [
                slice(chunk * KCHUNK + part * 128, chunk * KCHUNK + (part + 1) * 128)
                for part in range(KCHUNK // 128)
            ]
            if current is not None:
                scores = lax.dot_general(
                    query,
                    kvbuf[item, here, 0:HDIM],
                    (((1,), (1,)), ((), ())),
                    preferred_element_type=jnp.float32,
                )
            if previous is not None:
                likely = [jnp.exp2((drain[:, part] - top) * STEP) for part in parts]
                totals += tree(jnp.add, likely)
                pieces += jnp.dot(
                    jnp.concatenate([value.astype(jnp.bfloat16) for value in likely], axis=1),
                    kvbuf[item_p, here, HDIM : 2 * HDIM],
                    preferred_element_type=jnp.float32,
                )
            if current is not None:
                masked = []
                for at_part, part in enumerate(parts):
                    piece = jnp.where(
                        pos_ref[:, part] <= places,
                        scores[:, at_part * 128 : (at_part + 1) * 128],
                        MASKED_SCORE,
                    )
                    fill[:, part] = piece
                    masked.append(piece)
                highest = jnp.maximum(highest, tree(jnp.maximum, masked))
        if current is not None:
            fill_top[...] = jnp.broadcast_to(
                jnp.max(highest, axis=1, keepdims=True), (QBLOCK, 128)
            )
        if previous is not None:
            total = jnp.sum(totals, axis=1, keepdims=True)
            o_out[item_p, block_rows(j_p, at_p), :] = (pieces / total).astype(jnp.bfloat16)
            lse = top * HDIM ** (-0.5) + jnp.log(total)
            wide = lax.broadcasted_iota(jnp.int32, (QBLOCK, QBLOCK), 0) == (
                lax.broadcasted_iota(jnp.int32, (QBLOCK, QBLOCK), 1)
            )
            flat = jnp.sum(jnp.where(wide, lse, 0.0), axis=0, keepdims=True)
            lse_out[item_p, j_p, pl.ds(at_p * 2, 1), :] = flat[:, 0:128]
            lse_out[item_p, j_p, pl.ds(at_p * 2 + 1, 1), :] = flat[:, 128:256]

    def pieces_of(item, j):
        return o_out.at[item, pl.ds(pl.multiple_of(j * 512, 512), 512)], lse_out.at[item, j]

    def piece_copies(item, at):
        peer, j = ((other, first_j), (partner, own_j))[at]
        o_src, lse_src = pieces_of(item, j)
        return [
            remote(o_src, o_in.at[item, at], o_send.at[item, at, 0], o_recv.at[item, at, 0], peer),
            remote(
                lse_src, lse_in.at[item, at], o_send.at[item, at, 1], o_recv.at[item, at, 1], peer
            ),
        ]

    def shares_of(tiles):
        overall = tiles[0]
        for tile in tiles[1:]:
            overall = jnp.maximum(overall, tile)
        shares = [jnp.exp(tile - overall) for tile in tiles]
        whole = shares[0]
        for share in shares[1:]:
            whole = whole + share
        return [share / whole for share in shares], overall + jnp.log(whole)

    def weighted(shares, parts, group):
        total = jnp.zeros((TOKENS, HDIM), jnp.float32)
        for share, part in zip(shares, parts):
            column = jnp.sum(
                jnp.where(diagonal, share[group : group + 1, :], 0.0), axis=1, keepdims=True
            )
            total += column * part.astype(jnp.float32)
        return total.astype(jnp.bfloat16)

    def own_rows(group):
        return pl.ds(pl.multiple_of(own_j * 512 + group * TOKENS, TOKENS), TOKENS)

    def merge_self(item):
        for copy in piece_copies(item, 0):
            copy.wait_recv()
        shares, lse = shares_of([lse_out[item, own_j], lse_in[item, 0]])
        for group in range(4):
            here = slice(group * TOKENS, (group + 1) * TOKENS)
            o_out[item, own_rows(group), :] = weighted(
                shares, (o_out[item, own_rows(group), :], o_in[item, 0, here, :]), group
            )
        lse_out[item, own_j] = lse
        for copy in piece_copies(item, 1):
            copy.start()

    def att_copies(item):
        copies = [
            pltpu.make_async_copy(
                att_out.at[item, pl.ds(pl.multiple_of(z * TOKENS, TOKENS), TOKENS)],
                att_in.at[item, z],
                t_local.at[item],
            )
        ]
        for at, dz in enumerate((2, 1, 3)):
            to_z = shifted(z, dz)
            copies.append(
                remote(
                    att_out.at[item, pl.ds(pl.multiple_of(to_z * TOKENS, TOKENS), TOKENS)],
                    att_in.at[item, z],
                    t_send.at[item, at],
                    t_recv.at[item, at],
                    device_at(y, x, to_z, core),
                )
            )
        return copies

    def merge_cross(item):
        for at in range(2):
            for copy in piece_copies(item, at):
                copy.wait_recv()
        shares, _ = shares_of([lse_out[item, own_j], lse_in[item, 0], lse_in[item, 1]])
        for group in range(4):
            here = slice(group * TOKENS, (group + 1) * TOKENS)
            att_out[item, here, :] = weighted(
                shares,
                (
                    o_out[item, own_rows(group), :],
                    o_in[item, 0, here, :],
                    o_in[item, 1, here, :],
                ),
                group,
            )
        for copy in att_copies(item):
            copy.start()

    def head_columns(item, group):
        return pl.ds(pl.multiple_of(group * GROUP + item * HDIM, HDIM), HDIM)

    def att_result(item, group):
        columns = head_columns(item, group)
        return remote(
            result.at[:, columns],
            out_ref.at[:, columns],
            r_send.at[item, group],
            r_recv.at[item, group],
            after,
        )

    def finish(item):
        for copy in att_copies(item):
            copy.wait()
        for group in range(4):
            here = head_columns(item, group)
            result[:, here] = (
                x_ref[:, here].astype(jnp.float32)
                + att_in[item, group].astype(jnp.float32) * out_gain_ref[:, here]
            ).astype(jnp.bfloat16)
            att_result(item, group).start()

    pl.semaphore_wait(barrier, len(peers) + 1 + jnp.where(is_root, 15, 0))
    kv_spread(0)
    for copy in fetches:
        copy.wait()
    meta_ref[0:1, 0:64] = positions_ref[...]
    begin_ref[...] = jnp.full((8, 128), start_ref[0, 0], jnp.int32)
    kv_spread(META)

    def on_self(*steps):
        @pl.when(is_self)
        def _():
            for step in steps:
                step()

    def on_cross(*steps):
        @pl.when(is_cross)
        def _():
            for step in steps:
                step()

    def send_updates():
        for copy in update_copies():
            copy.start()

    def enter():
        for copy in update_copies():
            copy.wait()
        scan()
        for copy in enter_copies():
            copy.start()

    def keep_state():
        state_rows.wait()
        on_cross(lambda: state_out.__setitem__(Ellipsis, kept[...]))
        on_self(enter)

    def self_mix():
        for copy in enter_copies():
            copy.wait()
        for group in range(4):
            mix(group * LOCAL_HEADS, (group + 1) * LOCAL_HEADS)
            self_result(group).start()

    def send_fresh():
        @pl.when(is_root)
        def _():
            own_fresh.start()
            for by in range(1, 8):
                fresh_copy(by).start()

    def own(item):
        kv_own(item)
        on_cross(lambda: q_own(item))

    def make_queries():
        rows = x_ref[...].astype(jnp.float32)
        queries[...] = (rows * inverse_rms(rows) * query_gain_ref[...]).astype(jnp.bfloat16)
        q_spread(META)
        q_spread(0)

    def spread(item):
        kv_spread(item)
        on_cross(lambda: q_spread(item))

    on_cross(make_queries)
    spread(1)
    on_self(decay_setup, lambda: retain(0, 8))
    own(META)
    own(0)
    spread(2)
    on_self(lambda: retain(8, 16))
    own(1)
    spread(3)
    kv_forward(META)
    kv_forward(0)
    on_self(lambda: retain(16, HEADS))
    own(2)
    spread(4)
    on_self(lambda: q_relay(META), lambda: q_relay(0))
    kv_forward(1)
    kv_far(META)
    kv_far(0)
    own(3)
    on_self(lambda: q_relay(1))
    kv_forward(2)
    kv_far(1)
    q_ready(META)
    kv_ready(META)
    place_setup()

    hooks = {
        0: (lambda: own(4), lambda: on_self(lambda: q_relay(2))),
        1: (lambda: kv_forward(3),),
        2: (lambda: kv_far(2),),
        3: (lambda: on_self(lambda: q_relay(3)),),
        4: (lambda: kv_forward(4),),
        5: (lambda: kv_far(3),),
        6: (lambda: on_self(lambda: q_relay(4)),),
        7: (lambda: kv_far(4), lambda: on_self(send_updates)),
        12: (lambda: on_cross(lambda: merge_cross(0)),),
        14: (keep_state,),
        16: (lambda: on_cross(lambda: finish(0), lambda: merge_cross(1)),),
    }

    def after_block(step):
        item, block = step // 4, step % 4

        @pl.when(block == 1)
        def _():
            for copy in piece_copies(item, 0):
                copy.start()

        for due, steps in hooks.items():

            @pl.when(step == due)
            def _():
                for one in steps:
                    one()

        @pl.when(jnp.logical_and(is_self, jnp.logical_and(block == 1, item >= 1)))
        def _():
            merge_self(item - 1)

    q_ready(0)
    kv_ready(0)
    stage(0, None, True)

    def two_blocks(pair, carry):
        step = 2 * pair
        stage(step + 1, step, False)
        after_block(step)

        @pl.when(pair % 2 == 1)
        def _():
            q_ready((step + 2) // 4)
            kv_ready((step + 2) // 4)

        stage(step + 2, step + 1, True)
        after_block(step + 1)
        return carry

    last = 4 * LOCAL_HEADS - 1
    lax.fori_loop(0, (last - 1) // 2, two_blocks, 0)
    stage(last, last - 1, False)
    after_block(jnp.int32(last - 1))
    stage(None, last, True)
    on_self(lambda: merge_self(4))
    on_self(self_mix)
    send_fresh()
    on_cross(
        lambda: finish(1),
        lambda: merge_cross(2),
        lambda: merge_cross(3),
        lambda: finish(2),
        lambda: finish(3),
        lambda: merge_cross(4),
        lambda: finish(4),
    )

    @pl.when(is_root)
    def _():
        own_fresh.wait()

    @pl.when(jnp.logical_and(core == 1, jnp.logical_not(is_root)))
    def _():
        fresh_copy(1).wait_recv()

    @pl.when(core == 1)
    def _():
        fresh_across.start()

    @pl.when(core == 0)
    def _():
        fresh_across.wait_recv()

    both = fresh[...].astype(jnp.float32)
    new_rows = jnp.where(core == 0, both[0:8], both[8:16])
    new_rows = new_rows * inverse_rms(new_rows)
    global_out[:, 0:HD] = (new_rows * global_ref[0:1, :]).astype(jnp.bfloat16)
    global_out[:, HD : 2 * HD] = (new_rows * global_ref[1:2, :]).astype(jnp.bfloat16)

    from_self = jnp.logical_and(section >= 1, section <= 8)

    @pl.when(from_self)
    def _():
        for group in range(4):
            self_result(group).wait_recv()

    @pl.when(jnp.logical_not(from_self))
    def _():
        for item in range(LOCAL_HEADS):
            for group in range(4):
                att_result(item, group).wait_recv()

    for item in range(LOCAL_HEADS + 1):
        for copy in kv_spread_copies(item) + kv_pushes(item):
            copy.wait_send()
    for item in range(LOCAL_HEADS):
        for copy in piece_copies(item, 0):
            copy.wait_send()

    @pl.when(is_cross)
    def _():
        for item in range(LOCAL_HEADS + 1):
            for copy in q_spread_copies(item):
                copy.wait_send()
            q_push(item, 0).wait_send()
            q_push(item, 1).wait_send()
        for item in range(LOCAL_HEADS):
            for group in range(4):
                att_result(item, group).wait_send()

    @pl.when(is_self)
    def _():
        for item in range(LOCAL_HEADS + 1):
            q_push(item, 2).wait_send()
        for item in range(LOCAL_HEADS):
            for copy in piece_copies(item, 1):
                copy.wait_send()
        for group in range(4):
            self_result(group).wait_send()

    @pl.when(core == 1)
    def _():
        fresh_across.wait_send()

    @pl.when(is_root)
    def _():
        for by in range(1, 8):
            fresh_copy(by).wait_send()


def span(*arguments):
    vmem = pl.BlockSpec(memory_space=pltpu.VMEM)
    hbm = pl.BlockSpec(memory_space=pl.ANY)
    dma = pltpu.SemaphoreType.DMA
    items = LOCAL_HEADS + 1

    def bf16(*shape):
        return pltpu.VMEM(shape, jnp.bfloat16)

    def f32(*shape):
        return pltpu.VMEM(shape, jnp.float32)

    def i32(*shape):
        return pltpu.VMEM(shape, jnp.int32)

    return pl.pallas_call(
        span_kernel,
        out_shape=(
            jax.ShapeDtypeStruct((TOKENS, HD), jnp.bfloat16),
            jax.ShapeDtypeStruct((HEADS, 16, HDIM), jnp.float32),
            jax.ShapeDtypeStruct((8, 2 * HD), jnp.bfloat16),
        ),
        in_specs=[hbm] * 12,
        out_specs=(vmem, vmem, vmem),
        scratch_shapes=[
            bf16(TOKENS, HD),
            pltpu.SMEM((16,), jnp.float32),
            pltpu.SMEM((1, 1), jnp.int32),
            pltpu.SMEM((1, HEADS), jnp.int32),
            f32(HEADS, 1, TOKENS),
            f32(1, HD),
            f32(1, HD),
            f32(1, HD),
            f32(2, HD),
            i32(1, 64),
            dma((10,)),
            bf16(TOKENS, HD),
            i32(8, 128),
            i32(8, 128),
            bf16(LOCAL_HEADS, KEYS, 2 * HDIM),
            i32(32, 8, 128),
            i32(8, 8, 128),
            bf16(LOCAL_HEADS, 1024, HDIM),
            f32(QBLOCK, KEYS),
            f32(QBLOCK, KEYS),
            f32(QBLOCK, 128),
            f32(QBLOCK, 128),
            i32(1, KEYS),
            bf16(LOCAL_HEADS, 1024, HDIM),
            f32(LOCAL_HEADS, 2, 8, 128),
            bf16(LOCAL_HEADS, 2, 512, HDIM),
            f32(LOCAL_HEADS, 2, 8, 128),
            bf16(LOCAL_HEADS, 512, HDIM),
            bf16(LOCAL_HEADS, 4, TOKENS, HDIM),
            bf16(TOKENS, HD),
            f32(128, 128),
            f32(128, 128),
            f32(TOKENS, HD),
            f32(HEADS, 16, HDIM),
            bf16(HEADS, HDIM, HDIM),
            f32(24, 128),
            bf16(8, HEADS, 16, HDIM),
            f32(8, 24, 128),
            bf16(8, HEADS, 16, HDIM),
            bf16(HEADS, HDIM, HDIM),
            bf16(16, HD),
            dma((items, 2, 3)),
            dma((items, 2, 3)),
            dma((items, 2)),
            dma((items, 4)),
            dma((items, 4)),
            dma((items, 5)),
            dma((items, 5)),
            dma((items, 3)),
            dma((items, 3)),
            dma((items,)),
            dma((items, 3)),
            dma((items, 2)),
            dma((LOCAL_HEADS, 2, 2)),
            dma((LOCAL_HEADS, 2, 2)),
            dma((LOCAL_HEADS, 3)),
            dma((LOCAL_HEADS, 3)),
            dma((LOCAL_HEADS,)),
            dma((8, 2)),
            dma((8, 2)),
            dma((8,)),
            dma((8,)),
            dma((5,)),
            dma((LOCAL_HEADS, 4)),
            dma((LOCAL_HEADS, 4)),
            dma((4,)),
            dma((4,)),
            dma((8,)),
            dma((2,)),
        ],
        compiler_params=pltpu.CompilerParams(
            collective_id=0, has_side_effects=True, vmem_limit_bytes=58 * 1024 * 1024
        ),
        name="span",
    )(*arguments)


def local(
    section_input,
    state_in,
    decay_table,
    head_rate,
    gates,
    query_gain,
    key_gain,
    out_gain,
    global_gain,
    cache_kv,
    cache_pos,
    span_start,
):
    section_output, state_out, global_new = span(
        section_input[0],
        state_in[0],
        decay_table,
        head_rate,
        jnp.transpose(gates, (2, 0, 1)),
        query_gain,
        key_gain,
        out_gain,
        global_gain,
        cache_kv,
        cache_pos[None],
        span_start[None],
    )
    return (section_output[None], state_out[None], global_new[None, None])


def solution(mesh):
    return jax.shard_map(
        local,
        mesh=mesh,
        in_specs=(
            P("section", "seq", None),
            P("section", None, None, None),
            P(),
            P("section", None),
            P("section", "seq", None),
            P("section", None),
            P("section", None),
            P("section", None),
            P(),
            P(("section", "seq"), None),
            P(("section", "seq")),
            P("section"),
        ),
        out_specs=(
            P("section", "seq", None),
            P("section", None, "seq", None),
            P("seq", "section", None, None),
        ),
        check_vma=False,
    )
```
